128 devices in a mesh: dp: 4 (over x), expert: 32 (over y, z, core).
Axes of the slice: x: 4, y: 4, z: 4, core: 2. Of those that a mesh axis runs over, the one named last changes fastest.
Arguments:
- hidden_in: bfloat16 [2, 8192, 1024], P(None, ('dp', 'expert')), may hold values from -6 to 6
- segment_ids: int32 [2, 8192], P(None, ('dp', 'expert')), may hold values from 0 to 64, as said below
- token_counts: int32 [2, 128], P(None, ('dp', 'expert')), may hold values from 32 to 64, as said below
- expert_ids: int32 [2, 8192, 8], P(None, ('dp', 'expert')), may hold values from 0 to 31, all different within a row; in each aligned block of 64 rows (0 to 63, 64 to 127, ..., all dimensions but the last counted through in order) at most 24 rows name the same one
- norm_one: bfloat16 [1024], P('dp'), may hold values from 0.5 to 1.5
- qkv_weight: bfloat16 [1024, 2048], P('dp'), may hold values from -0.1875 to 0.1875
- out_weight: bfloat16 [1024, 1024], P('dp'), may hold values from -0.75 to 0.75
- norm_two: bfloat16 [1024], P('dp'), may hold values from 0.5 to 1.5
- router_weight: bfloat16 [1024, 32], P('dp'), may hold values from -0.09375 to 0.09375
- gate_weight: bfloat16 [32, 1024, 512], P('expert'), may hold values from -0.1875 to 0.1875
- up_weight: bfloat16 [32, 1024, 512], P('expert'), may hold values from -0.1875 to 0.1875
- down_weight: bfloat16 [32, 512, 1024], P('expert'), may hold values from -1 to 1
- cotangent: bfloat16 [2, 8192, 1024], P(None, ('dp', 'expert')), may hold values from -6 to 6
Outputs:
- output: bfloat16 [2, 8192, 1024], P(None, ('dp', 'expert'))
- input_grad: float32 [2, 8192, 1024], P(None, ('dp', 'expert'))
- norm_one_grad: float32 [1024], P('dp')
- qkv_grad: float32 [1024, 2048], P('dp')
- out_proj_grad: float32 [1024, 1024], P('dp')
- norm_two_grad: float32 [1024], P('dp')
- router_grad: float32 [1024, 32], P('dp')
- gate_proj_grad: float32 [32, 1024, 512], P('expert')
- up_proj_grad: float32 [32, 1024, 512], P('expert')
- down_proj_grad: float32 [32, 512, 1024], P('expert')
The draws below stay inside these ranges and needn't reach their ends.
Inputs may be any that keep to these rules, and one draw needn't show every extreme that they name: `expert_ids`: in each device's micro-batch (aligned blocks of 64 rows) no expert is named by more than 24 rows; a row names 8 different experts. `token_counts`: some device's micro-batch is full and some holds 32 live slots. `segment_ids`: within each device's micro-batch the ids never fall; slots from the token count on hold 64, live slots less.
All inputs are finite; a program needn't handle non-finite values.
Results may differ from the reference program's by a relative error of at most 0.023.
Values may be sent and summed in bfloat16 or wider, within the bound.
No kernel may reach another device: no remote copies, remote signals or barrier semaphores. Data moves between devices by JAX's collectives and lax.ppermute only.
A program may use at most 128 MiB of HBM per device.

```python
import math
import jax
import jax.numpy as jnp
import numpy as np
from jax import lax

D = 1024
QUERY_HEADS = 16
KEY_VALUE_HEADS = 8
HEAD_SIZE = 64
FFE = 512
TOPK = 8
MICRO = 2
TOK_MB = 64
EXPERTS = 32
TOKENS = 8192
CAP = 24
QKV = 2048
DEVICES = 128


def count_table(key):
    entries = MICRO * DEVICES
    picked_counts = jax.random.randint(jax.random.fold_in(key, 11), (entries,), TOK_MB // 2, TOK_MB + 1)
    fullest = jax.random.randint(jax.random.fold_in(key, 12), (), 0, entries)
    offset = jax.random.randint(jax.random.fold_in(key, 13), (), 1, entries)
    emptiest = (fullest + offset) % entries
    picked_counts = picked_counts.at[fullest].set(TOK_MB).at[emptiest].set(TOK_MB // 2)
    return picked_counts.reshape(MICRO, DEVICES).astype(jnp.int32)


def draw_token_counts(key, part):
    return count_table(key)


def draw_segment_ids(key, part):
    counts_table = count_table(key)
    starting = jax.random.randint(jax.random.fold_in(key, 14), (MICRO, DEVICES, TOK_MB), 0, 16) == 0
    places = jnp.arange(TOK_MB, dtype=jnp.int32)
    starting = starting & (places > 0)[None, None, :]
    labels = jnp.cumsum(starting.astype(jnp.int32), axis=-1)
    active = places[None, None, :] < counts_table[:, :, None]
    labels = jnp.where(active, labels, TOK_MB)
    return labels.reshape(MICRO, TOKENS).astype(jnp.int32)


def block_scale(key, shape, pieces, smallest, largest):
    factor_of, own = 1.0, jax.random.fold_in(key, 6)
    for axis_at, blocks in pieces:
        heights = jnp.exp(jax.random.uniform(jax.random.fold_in(own, axis_at), (blocks,), jnp.float32, smallest / len(pieces), largest / len(pieces)))
        factor_of = factor_of * jnp.repeat(heights, shape[axis_at] // blocks).reshape([-1 if axis == axis_at else 1 for axis in range(len(shape))])
    return factor_of


def shared_out(key, own, number, rows, count, top, most, slope):
    order = jax.random.permutation(key, count)
    packed, usual = shares(count, rows * top, most, slope, True), shares(count, rows * top, most, slope, False)
    places = jnp.arange(count)

    def named(sizes, rotation):
        used = int((sizes > 0).sum())
        fixed = max(1, used // 4)
        moved = fixed + (places - fixed + rotation * (used - fixed)) % max(1, count - fixed)
        return jnp.zeros((count,), jnp.int32).at[order[jnp.where(places < fixed, places, moved)]].set(jnp.asarray(sizes, jnp.int32))

    sizes = jnp.where(number % 4 == 0, named(packed, number // 4), named(usual, number - number // 4 - 1))
    mixed = jax.random.permutation(jax.random.fold_in(own, 3), count)
    donor, sink = mixed[0:count // 2 * 2:2], mixed[1:count // 2 * 2:2]
    room = jnp.minimum(sizes[donor] - 1, most - sizes[sink]) // 2
    room = jnp.where((donor == order[0]) | (sink == order[0]) | (sizes[sink] == 0), 0, jnp.maximum(room, 0))
    moved = jax.random.randint(jax.random.fold_in(own, 4), (count // 2,), 0, 1 << 20) % (room + 1)
    sizes = sizes.at[donor].add(-moved).at[sink].add(moved)
    items = jnp.searchsorted(jnp.cumsum(sizes), jnp.arange(rows * top), side="right").astype(jnp.int32)
    listing = items.reshape(top, rows).T
    listing = listing[jax.random.permutation(jax.random.fold_in(own, 1), rows)]
    rotation = jax.random.randint(jax.random.fold_in(own, 2), (rows, 1), 0, top)
    return jnp.take_along_axis(listing, (jnp.arange(top)[None, :] + rotation) % top, axis=1)


def shares(count, total, bound, slope, full):
    loads = [(1 << 20) // math.isqrt(rank ** slope) + 1 for rank in range(1, count + 1)]
    largest = bound if full else min(bound, max(-(-total // count), total * loads[0] // sum(loads)))
    least = 1 if total - largest >= count - 1 else 0
    given, rest = [largest] + [least] * (count - 1), total - largest - least * (count - 1)
    while rest > 0:
        candidates = [i for i in range(1, count) if given[i] < largest] or [i for i in range(1, count) if given[i] < bound]
        pool, budget = sum([loads[i] for i in candidates]), rest
        for i in candidates:
            extra = min(bound - given[i], max(1, budget * loads[i] // pool), rest)
            given[i] = given[i] + extra
            rest = rest - extra
    return np.array(given)


def scatter_about(key, shape, deviation, most, pieces=(), held_as=jnp.bfloat16):
    values = jax.random.normal(key, shape, jnp.float32) * deviation
    if len(pieces) > 0:
        values = block_scale(key, shape, pieces, -0.22, 0.18) * values
    return jnp.clip(values, min=-most, max=most).astype(held_as)


def setup_inputs(seed: int = 0) -> dict:
    key_list = jax.random.split(jax.random.key(seed), 14)
    hidden_in = scatter_about(key_list[0], (MICRO, TOKENS, D), 1.0, 6.0, ((1, 128),))
    segment_ids = draw_segment_ids(jax.random.fold_in(key_list[13], 71), 0)
    token_counts = draw_token_counts(jax.random.fold_in(key_list[13], 71), 0)
    expert_ids_keys = jax.random.split(jax.random.fold_in(key_list[3], 1), MICRO * TOKENS // TOK_MB)
    expert_ids_turns = jax.random.permutation(jax.random.fold_in(key_list[3], 3), MICRO * TOKENS // TOK_MB)
    expert_ids = jax.vmap(lambda own, number: shared_out(jax.random.fold_in(key_list[3], 2), own, number, TOK_MB, EXPERTS, TOPK, CAP, 1))(expert_ids_keys, expert_ids_turns).reshape((MICRO, TOKENS, TOPK))
    norm_one = jnp.clip(1.0 + 0.1 * jax.random.normal(key_list[4], (D,), jnp.float32), 0.5, 1.5).astype(jnp.bfloat16)
    qkv_weight = scatter_about(key_list[5], (D, QKV), D ** -0.5, 0.1875, ((0, 4),))
    out_weight = scatter_about(key_list[6], (QUERY_HEADS * HEAD_SIZE, D), (QUERY_HEADS * HEAD_SIZE // 16) ** -0.5, 0.75, ((0, 4),))
    norm_two = jnp.clip(1.0 + 0.1 * jax.random.normal(key_list[7], (D,), jnp.float32), 0.5, 1.5).astype(jnp.bfloat16)
    router_weight = scatter_about(key_list[8], (D, EXPERTS), (4 * D) ** -0.5, 0.09375, ((0, 4),))
    gate_weight = scatter_about(key_list[9], (EXPERTS, D, FFE), D ** -0.5, 0.1875, ((0, 32),))
    up_weight = scatter_about(key_list[10], (EXPERTS, D, FFE), D ** -0.5, 0.1875, ((0, 32),))
    down_weight = scatter_about(key_list[11], (EXPERTS, FFE, D), (FFE // 16) ** -0.5, 1.0, ((0, 32),))
    cotangent = scatter_about(key_list[12], (MICRO, TOKENS, D), 1.0, 6.0, ((1, 128),))
    return dict(hidden_in=hidden_in, segment_ids=segment_ids, token_counts=token_counts, expert_ids=expert_ids, norm_one=norm_one, qkv_weight=qkv_weight, out_weight=out_weight, norm_two=norm_two, router_weight=router_weight, gate_weight=gate_weight, up_weight=up_weight, down_weight=down_weight, cotangent=cotangent)


@jax.custom_vjp
def lowered_input(v):
    return lax.optimization_barrier(v.astype(jnp.bfloat16)).astype(jnp.float32)

@jax.custom_vjp
def low_back(v):
    return v

def low_keep(v):
    return (lowered_input(v), None)

def low_pass(kept, grad):
    return (grad,)

def back_keep(v):
    return (v, None)

def back_low(kept, grad):
    return (lowered_input(grad),)
lowered_input.defvjp(low_keep, low_pass)
low_back.defvjp(back_keep, back_low)
epsilon = 1e-06
highest = lax.Precision.HIGHEST

def rms_scale(values, gain):
    return values * lax.rsqrt(lax.optimization_barrier(jnp.mean(values * values, axis=-1, keepdims=True)) + epsilon) * gain

def rope_tables(segment_key):
    sequence_length = segment_key.shape[0]
    places = jnp.arange(sequence_length, dtype=jnp.int32)
    changes = jnp.concatenate([jnp.ones((1,), dtype=bool), segment_key[1:] != segment_key[:-1]])
    leading = lax.cummax(jnp.where(changes, places, 0), axis=0)
    position = (places - leading).astype(jnp.float32)
    frequency = 10000.0 ** (-2.0 * jnp.arange(HEAD_SIZE // 2, dtype=jnp.float32) / HEAD_SIZE)
    angles = position[:, None] * frequency[None, :]
    return (jnp.cos(angles)[:, None, :], jnp.sin(angles)[:, None, :])

def apply_rotation(values, cosine_table, sine_table):
    half_width = values.shape[-1] // 2
    leading_half = values[..., :half_width]
    trailing_half = values[..., half_width:]
    return jnp.concatenate([leading_half * cosine_table - trailing_half * sine_table, trailing_half * cosine_table + leading_half * sine_table], axis=-1)

def layer_block(params, block_x, block_seg, block_valid, block_routes):
    norm_gain, qkv_full, out_full, norm_gain_two, router_full, gate_full, up_full, down_full = params
    sequence_length = block_x.shape[0]
    query_groups = QUERY_HEADS // KEY_VALUE_HEADS
    scale = HEAD_SIZE ** (-0.5)
    cosine_table, sine_table = rope_tables(block_seg)
    normed = rms_scale(block_x, norm_gain)
    projected_rows = low_back(jnp.dot(lowered_input(normed), qkv_full, precision=highest, preferred_element_type=jnp.float32))
    query_rows = projected_rows[:, :QUERY_HEADS * HEAD_SIZE].reshape(sequence_length, QUERY_HEADS, HEAD_SIZE)
    key_head_rows = projected_rows[:, QUERY_HEADS * HEAD_SIZE:(QUERY_HEADS + KEY_VALUE_HEADS) * HEAD_SIZE].reshape(sequence_length, KEY_VALUE_HEADS, HEAD_SIZE)
    value_head_rows = projected_rows[:, (QUERY_HEADS + KEY_VALUE_HEADS) * HEAD_SIZE:].reshape(sequence_length, KEY_VALUE_HEADS, HEAD_SIZE)
    lowered_query = lowered_input(apply_rotation(query_rows, cosine_table, sine_table)).reshape(sequence_length, KEY_VALUE_HEADS, query_groups, HEAD_SIZE)
    key_low = lowered_input(apply_rotation(key_head_rows, cosine_table, sine_table))
    value_low = lowered_input(value_head_rows)
    scores = low_back(jnp.einsum('qkgd,pkd->kgqp', lowered_query, key_low, precision=highest) * scale)
    places = jnp.arange(sequence_length)
    allowed = (block_seg[:, None] == block_seg[None, :]) & (places[:, None] >= places[None, :])
    scores = jnp.where(allowed, scores, -1e+30)
    peak = lax.optimization_barrier(jnp.max(scores, axis=-1, keepdims=True))
    expo = jnp.exp(scores - peak)
    probs = expo / lax.optimization_barrier(jnp.sum(expo, axis=-1, keepdims=True))
    attended = jnp.einsum('kgqp,pkd->qkgd', lowered_input(probs), value_low, precision=highest).reshape(sequence_length, QUERY_HEADS * HEAD_SIZE)
    attn_out = low_back(jnp.dot(lowered_input(low_back(attended)), out_full, precision=highest, preferred_element_type=jnp.float32))
    after = block_x + block_valid[:, None] * attn_out
    second = rms_scale(after, norm_gain_two)
    logits = jnp.dot(second, router_full, precision=highest, preferred_element_type=jnp.float32)
    chosen = jnp.take_along_axis(logits, block_routes, axis=1)
    gates = jax.nn.softmax(chosen, axis=-1)
    onehot = (block_routes[:, :, None] == jnp.arange(EXPERTS)[None, None, :]).astype(jnp.float32)
    mixing = jnp.einsum('tk,tke->te', gates, onehot, precision=highest) * block_valid[:, None]
    sent = lowered_input(second)
    copies = low_back(jnp.broadcast_to(sent[None], (EXPERTS, sequence_length, D)))
    gate_pre = low_back(jnp.einsum('etd,edf->etf', copies, gate_full, precision=highest))
    up_pre = low_back(jnp.einsum('etd,edf->etf', copies, up_full, precision=highest))
    hidden = lowered_input(jax.nn.silu(gate_pre) * up_pre)
    expert_out = lowered_input(low_back(jnp.einsum('etf,efd->etd', hidden, down_full, precision=highest)))
    mixed = jnp.einsum('te,etd->td', mixing, expert_out, precision=highest)
    return after + mixed

def forward(inputs, seg_blocks, valid_blocks, route_blocks, params):
    blocks = inputs.reshape(MICRO * DEVICES, TOK_MB, D)

    def one_block(items):
        return layer_block(params, items[0], items[1], items[2], items[3])
    outputs = lax.map(jax.checkpoint(one_block), (blocks, seg_blocks, valid_blocks, route_blocks))
    return outputs.reshape(MICRO, TOKENS, D)

def reference(hidden_in, segment_ids, token_counts, expert_ids, norm_one, qkv_weight, out_weight, norm_two, router_weight, gate_weight, up_weight, down_weight, cotangent):
    seg_blocks = segment_ids.reshape(MICRO * DEVICES, TOK_MB)
    valid_blocks = (jnp.arange(TOK_MB, dtype=jnp.int32)[None, :] < token_counts.reshape(MICRO * DEVICES)[:, None]).astype(jnp.float32)
    route_blocks = expert_ids.reshape(MICRO * DEVICES, TOK_MB, TOPK)
    floats = (hidden_in, norm_one, qkv_weight, out_weight, norm_two, router_weight, gate_weight, up_weight, down_weight)
    floats = tuple((entry.astype(jnp.float32) for entry in floats))

    def closed(inputs, gain_first, qkv_full, out_full, gain_second, router_full, gate_full, up_full, down_full):
        params = (gain_first, qkv_full, out_full, gain_second, router_full, gate_full, up_full, down_full)
        return forward(inputs, seg_blocks, valid_blocks, route_blocks, params)
    result, pullback = jax.vjp(closed, *floats)
    grads = pullback(cotangent.astype(jnp.float32))
    return (result.astype(jnp.bfloat16), grads[0], grads[1], grads[2], grads[3], grads[4], grads[5], grads[6], grads[7], grads[8])
```

```python
import functools

import jax
import jax.numpy as jnp
from jax import lax
from jax.experimental import pallas as pl
from jax.experimental.pallas import tpu as pltpu
from jax.sharding import Mesh
from jax.sharding import PartitionSpec as P

D = 1024
QUERY_HEADS = 16
KEY_VALUE_HEADS = 8
HEAD_SIZE = 64
FFE = 512
TOPK = 8
MICRO = 2
TOK_MB = 64
EXPERTS = 32
CAP = 24
ROWS = MICRO * TOK_MB
SLOTS = MICRO * CAP
EXTRA = 16
WIDE = ROWS + EXTRA
KV = KEY_VALUE_HEADS * HEAD_SIZE

epsilon = 1e-06
highest = lax.Precision.HIGHEST
f32 = jnp.float32
bf16 = jnp.bfloat16


def plane_pairs(first, second, swap):
    pairs = []
    for y in range(4):
        for z in range(4):
            for c in range(2):
                dy, dz = (first, second) if c == 0 else (second, first)
                target = (((y + dy) % 4) * 4 + (z + dz) % 4) * 2 + (c ^ swap)
                pairs.append(((y * 4 + z) * 2 + c, target))
    return pairs


def along_first(v, k):
    return lax.ppermute(v, ("y", "z", "core"), plane_pairs(k % 4, 0, 0))


def along_second(v, k):
    return lax.ppermute(v, ("y", "z", "core"), plane_pairs(0, k % 4, 0))


def swap_core(v):
    return lax.ppermute(v, "core", [(0, 1), (1, 0)])


def along_x(v, k):
    return lax.ppermute(v, "x", [(i, (i + k) % 4) for i in range(4)])


def gather_plane(v):
    stack = jnp.stack([v] + [along_first(v, k) for k in (1, 2, 3)])
    own = [stack] + [along_second(stack, j) for j in (1, 2, 3)]
    return own, [swap_core(group) for group in own]


def scatter_plane(own, sibling):
    merged = [
        (a.astype(f32) + swap_core(b).astype(f32)).astype(bf16) for a, b in zip(own, sibling)
    ]
    total = merged[0].astype(f32)
    for j in (1, 3, 2):
        total = total + along_second(merged[j], -j).astype(f32)
    total = total.astype(bf16)
    result = total[0].astype(f32)
    for i in (1, 3, 2):
        result = result + along_first(total[i], -i).astype(f32)
    return result


def nt(a, b):
    return lax.dot_general(a, b, (((1,), (1,)), ((), ())), preferred_element_type=f32)


def tn(a, b):
    return lax.dot_general(a, b, (((0,), (0,)), ((), ())), preferred_element_type=f32)


def nn(a, b):
    return jnp.dot(a, b, preferred_element_type=f32)


BLOCKS = 4
PACKED = BLOCKS * SLOTS


def expert_kernel(
    place_ref,
    own_rows, sib_rows, own_grad, sib_grad, gate_ref, up_ref, down_ref,
    own_back, sib_back, own_out, sib_out, x_ref, s_ref, h_ref, g_ref, u_ref,
    x_buf, c_buf,
):
    expert = place_ref[0]
    row_at = expert // 8
    lane_at = pl.multiple_of((expert % 8) * 128, 128)
    upper = (
        lax.broadcasted_iota(jnp.int32, (ROWS, ROWS), 0)
        < lax.broadcasted_iota(jnp.int32, (ROWS, ROWS), 1)
    ).astype(bf16)
    extra_row = lax.broadcasted_iota(jnp.int32, (EXTRA, 128), 0)
    slot_row = lax.broadcasted_iota(jnp.int32, (SLOTS, ROWS), 0).astype(f32)

    def side(rows_ref, grad_ref, back_ref, out_ref):
        picks = []
        weights = []
        for b in range(BLOCKS):
            info = rows_ref[b, ROWS:WIDE, pl.ds(lane_at, 128)].astype(f32)
            high = jnp.sum(jnp.where(extra_row == row_at, info, 0.0), axis=0, keepdims=True)
            low = jnp.sum(jnp.where(extra_row == row_at + 4, info, 0.0), axis=0, keepdims=True)
            chosen = high > 0.0
            flags = jnp.broadcast_to(chosen.astype(f32), (16, ROWS)).astype(bf16)
            rank = nn(flags, upper)[0:1]
            pick = jnp.where((slot_row == rank) & chosen, 1.0, 0.0)
            picks.append(pick)
            weights.append(jnp.sum(pick * (high + low), axis=1, keepdims=True))
            low_pick = pick.astype(bf16)
            x_buf[b * SLOTS:(b + 1) * SLOTS, :] = nn(low_pick, rows_ref[b, 0:ROWS, :]).astype(bf16)
            c_buf[b * SLOTS:(b + 1) * SLOTS, :] = nn(low_pick, grad_ref[b]).astype(bf16)
        mixing = jnp.concatenate(weights, axis=0)
        rows = x_buf[...]
        grads = c_buf[...].astype(f32)
        gate_pre = nn(rows, gate_ref[...])
        up_pre = nn(rows, up_ref[...])
        sigma = 1.0 / (1.0 + jnp.exp(-gate_pre))
        swish = gate_pre * sigma
        hidden = (swish * up_pre).astype(bf16)
        slot_grad = (mixing * grads).astype(bf16)
        hidden_grad = nt(slot_grad, down_ref[...])
        produced = nn(hidden, down_ref[...]).astype(bf16).astype(f32)
        gate_grad = jnp.sum(produced * grads, axis=1, keepdims=True)
        weighted = (mixing * produced).astype(bf16)
        slope = sigma * (1.0 + gate_pre * (1.0 - sigma))
        gate_pre_grad = (hidden_grad * up_pre * slope).astype(bf16)
        up_pre_grad = (hidden_grad * swish).astype(bf16)
        back = (nt(gate_pre_grad, gate_ref[...]) + nt(up_pre_grad, up_ref[...])).astype(bf16)
        for b in range(BLOCKS):
            span = slice(b * SLOTS, (b + 1) * SLOTS)
            low_pick = picks[b].astype(bf16)
            back_ref[b, 0:ROWS, :] = tn(low_pick, back[span]).astype(bf16)
            out_ref[b] = tn(low_pick, weighted[span]).astype(bf16)
            back_ref[b, ROWS:WIDE, :] = jnp.zeros((EXTRA, D), bf16)
            dots = jnp.sum(picks[b] * gate_grad[span], axis=0, keepdims=True)
            high = dots.astype(bf16).astype(f32)
            info = jnp.where(extra_row == row_at, high, 0.0)
            info = info + jnp.where(extra_row == row_at + 4, dots - high, 0.0)
            back_ref[b, ROWS:WIDE, pl.ds(lane_at, 128)] = info.astype(bf16)
        x_ref[...] = rows
        s_ref[...] = slot_grad
        h_ref[...] = hidden
        g_ref[...] = gate_pre_grad
        u_ref[...] = up_pre_grad

    @pl.when(pl.program_id(0) == 0)
    def _():
        side(own_rows, own_grad, own_back, own_out)

    @pl.when(pl.program_id(0) == 1)
    def _():
        side(sib_rows, sib_grad, sib_back, sib_out)


def run_experts(place, own_rows, sib_rows, own_grad, sib_grad, gate, up, down):
    def whole(*shape):
        return pl.BlockSpec(shape, lambda i, p: (0,) * len(shape))

    def part(width):
        return pl.BlockSpec((PACKED, width), lambda i, p: (i, 0))

    wide = jax.ShapeDtypeStruct((BLOCKS, WIDE, D), bf16)
    flat = jax.ShapeDtypeStruct((BLOCKS, ROWS, D), bf16)
    full = jax.ShapeDtypeStruct((2 * PACKED, D), bf16)
    half = jax.ShapeDtypeStruct((2 * PACKED, FFE), bf16)
    return pl.pallas_call(
        expert_kernel,
        grid_spec=pltpu.PrefetchScalarGridSpec(
            num_scalar_prefetch=1,
            grid=(2,),
            in_specs=[
                whole(BLOCKS, WIDE, D), whole(BLOCKS, WIDE, D),
                whole(BLOCKS, ROWS, D), whole(BLOCKS, ROWS, D),
                whole(D, FFE), whole(D, FFE), whole(FFE, D),
            ],
            out_specs=[
                whole(BLOCKS, WIDE, D), whole(BLOCKS, WIDE, D),
                whole(BLOCKS, ROWS, D), whole(BLOCKS, ROWS, D),
                part(D), part(D), part(FFE), part(FFE), part(FFE),
            ],
            scratch_shapes=[pltpu.VMEM((PACKED, D), bf16), pltpu.VMEM((PACKED, D), bf16)],
        ),
        out_shape=[wide, wide, flat, flat, full, full, half, half, half],
        compiler_params=pltpu.CompilerParams(vmem_limit_bytes=48 * 1024 * 1024),
        cost_estimate=pl.CostEstimate(
            flops=12 * 2 * PACKED * D * FFE, bytes_accessed=16_000_000, transcendentals=2 * PACKED * FFE
        ),
        name="experts",
    )(place, own_rows, sib_rows, own_grad, sib_grad, gate, up, down)


def weight_grad_kernel(place_ref, *refs):
    xs, ss, hs, gs, us = (refs[4 * i:4 * i + 4] for i in range(5))
    outs = refs[20:24]
    x_at = place_ref[1]
    for k in range(4):
        block = (x_at + 4 - k) % 4
        wide_at = pl.multiple_of(block * 256, 256)
        thin_at = pl.multiple_of(block * 128, 128)
        gate_sum = up_sum = down_sum = None
        for j in range(4):
            rows = xs[j][:, pl.ds(wide_at, 256)]
            one = tn(rows, gs[j][...])
            two = tn(rows, us[j][...])
            three = tn(hs[j][:, pl.ds(thin_at, 128)], ss[j][...])
            gate_sum = one if j == 0 else gate_sum + one
            up_sum = two if j == 0 else up_sum + two
            down_sum = three if j == 0 else down_sum + three
        outs[k][0:256, :] = gate_sum.astype(bf16)
        outs[k][256:512, :] = up_sum.astype(bf16)
        outs[k][512:640, :] = down_sum[:, 0:512].astype(bf16)
        outs[k][640:768, :] = down_sum[:, 512:1024].astype(bf16)


def run_weight_grads(place, saved):
    operands = [part[i] for i in range(5) for part in saved]
    out = jax.ShapeDtypeStruct((768, FFE), bf16)
    return pl.pallas_call(
        weight_grad_kernel,
        grid_spec=pltpu.PrefetchScalarGridSpec(
            num_scalar_prefetch=1,
            grid=(1,),
            in_specs=[pl.BlockSpec(v.shape, lambda i, p: (0, 0)) for v in operands],
            out_specs=[pl.BlockSpec((768, FFE), lambda i, p: (0, 0))] * 4,
        ),
        out_shape=[out] * 4,
        compiler_params=pltpu.CompilerParams(vmem_limit_bytes=48 * 1024 * 1024),
        cost_estimate=pl.CostEstimate(
            flops=3 * 2 * 8 * PACKED * D * FFE, bytes_accessed=14_000_000, transcendentals=0
        ),
        name="expert_weight_grads",
    )(place, *operands)


def block_at(v, index, size, axis):
    return lax.dynamic_slice_in_dim(v, index * size, size, axis)


def behind(v, at, size, axis):
    return [block_at(v, (at + 4 - k) % 4, size, axis) for k in range(4)]


def in_place(blocks, at, axis):
    stack = jnp.stack(blocks)
    return jnp.concatenate(
        [lax.dynamic_index_in_dim(stack, (at + 4 - a) % 4, 0, keepdims=False) for a in range(4)],
        axis=axis,
    )


def rms_backward(grad_out, values, inverse, gain):
    scaled = grad_out * gain
    gain_grad = jnp.sum(grad_out * values * inverse, axis=0)
    value_gradient = inverse * (
        scaled - values * inverse * inverse * jnp.mean(scaled * values, axis=-1, keepdims=True)
    )
    return (value_gradient, gain_grad)


def rotate(values, cosine, sine):
    a, b = values[..., :32], values[..., 32:]
    return jnp.concatenate([a * cosine - b * sine, b * cosine + a * sine], axis=-1)


def per_device(
    hidden_in,
    segment_ids,
    token_counts,
    expert_ids,
    norm_one,
    qkv_weight,
    out_weight,
    norm_two,
    router_weight,
    gate_weight,
    up_weight,
    down_weight,
    cotangent,
):
    x_at = lax.axis_index("x")
    y_at = lax.axis_index("y")
    z_at = lax.axis_index("z")
    core = lax.axis_index("core")
    first_at = jnp.where(core == 0, y_at, z_at)
    second_at = jnp.where(core == 0, z_at, y_at)
    place = jnp.stack([(y_at * 4 + z_at) * 2 + core, x_at]).astype(jnp.int32)
    scale = HEAD_SIZE ** (-0.5)
    groups = QUERY_HEADS // KEY_VALUE_HEADS

    def pick_half(v):
        n = v.shape[1] // 2
        own = block_at(v, core, n, 1)
        other = block_at(v, 1 - core, n, 1)
        return own, other

    def join_half(own, other):
        return jnp.where(
            core == 0,
            jnp.concatenate([own, other], axis=1),
            jnp.concatenate([other, own], axis=1),
        )

    small = jnp.concatenate(
        [
            router_weight.T,
            norm_one[None],
            norm_two[None],
            jnp.zeros((48 - 34, 256), bf16),
        ],
        axis=0,
    )
    small = [small] + [along_x(small, k) for k in (1, 2, 3)]
    small = in_place(small, x_at, 1).astype(f32)
    router_full = small[0:32]
    gain_first = small[32]
    gain_second = small[33]

    def gather_x(v):
        own, _ = pick_half(v)
        own = jnp.concatenate([own] + [along_x(own, k) for k in (1, 2, 3)], axis=0)
        return own, swap_core(own)

    qkv_own, qkv_sib = gather_x(qkv_weight)
    out_own, out_sib = gather_x(out_weight)

    grad_low = cotangent.reshape(ROWS, D)
    grad_own, grad_sib = gather_plane(grad_low)

    inputs = hidden_in.reshape(ROWS, D).astype(f32)
    valid = (
        (jnp.arange(TOK_MB, dtype=jnp.int32)[None, :] < token_counts).reshape(ROWS, 1).astype(f32)
    )
    segment_key = (
        segment_ids + (TOK_MB + 1) * jnp.arange(MICRO, dtype=jnp.int32)[:, None]
    ).reshape(ROWS)
    places = jnp.arange(ROWS)
    allowed = (segment_key[:, None] == segment_key[None, :]) & (places[:, None] >= places[None, :])
    position = jnp.sum(allowed.astype(f32), axis=1) - 1.0
    frequency = 10000.0 ** (-2.0 * jnp.arange(HEAD_SIZE // 2, dtype=f32) / HEAD_SIZE)
    angles = position[:, None] * frequency[None, :]
    cosine = jnp.cos(angles)[:, None, :]
    sine = jnp.sin(angles)[:, None, :]

    inverse_first = lax.rsqrt(jnp.mean(inputs * inputs, axis=-1, keepdims=True) + epsilon)
    normed_low = (inputs * inverse_first * gain_first).astype(bf16)
    normed_rel = jnp.concatenate(behind(normed_low, x_at, 256, 1), axis=1)
    projected = join_half(nn(normed_rel, qkv_own), nn(normed_rel, qkv_sib))
    query = projected[:, :D].reshape(ROWS, QUERY_HEADS, HEAD_SIZE)
    key = projected[:, D:D + KV].reshape(ROWS, KEY_VALUE_HEADS, HEAD_SIZE)
    value_low = projected[:, D + KV:].reshape(ROWS, KEY_VALUE_HEADS, HEAD_SIZE).astype(bf16)
    query_low = (
        rotate(query, cosine, sine).astype(bf16).reshape(ROWS, KEY_VALUE_HEADS, groups, HEAD_SIZE)
    )
    key_low = rotate(key, cosine, sine).astype(bf16)
    scores = jnp.einsum("qkgd,pkd->kgqp", query_low, key_low, preferred_element_type=f32) * scale
    scores = jnp.where(allowed, scores, -1e30)
    peak = jnp.max(scores, axis=-1, keepdims=True)
    expo = jnp.exp(scores - peak)
    probs = expo / jnp.sum(expo, axis=-1, keepdims=True)
    attended = jnp.einsum(
        "kgqp,pkd->qkgd", probs.astype(bf16), value_low, preferred_element_type=f32
    )
    attended_low = attended.reshape(ROWS, D).astype(bf16)
    attended_rel = jnp.concatenate(behind(attended_low, x_at, 256, 1), axis=1)
    attn_out = join_half(nn(attended_rel, out_own), nn(attended_rel, out_sib))
    after = inputs + valid * attn_out
    inverse_second = lax.rsqrt(jnp.mean(after * after, axis=-1, keepdims=True) + epsilon)
    second = after * inverse_second * gain_second
    logits = lax.dot_general(
        second, router_full, (((1,), (1,)), ((), ())), precision=highest, preferred_element_type=f32
    )
    routes = expert_ids.reshape(ROWS, TOPK)
    member = jnp.any(
        routes[:, :, None] == jnp.arange(EXPERTS, dtype=jnp.int32)[None, None, :], axis=1
    )
    masked = jnp.where(member, logits, -jnp.inf)
    top = jnp.max(masked, axis=-1, keepdims=True)
    gates = jnp.where(member, jnp.exp(masked - top), 0.0)
    gates = gates / jnp.sum(gates, axis=-1, keepdims=True)
    mixing = (gates * valid).T
    mixing_high = mixing.astype(bf16)
    mixing_low = (mixing - mixing_high.astype(f32)).astype(bf16)
    sent = jnp.concatenate(
        [
            second.astype(bf16),
            mixing_high.reshape(4, D),
            mixing_low.reshape(4, D),
            jnp.zeros((8, D), bf16),
        ],
        axis=0,
    )
    rows_own, rows_sib = gather_plane(sent)

    parts = {}
    for j in (0, 1, 3, 2):
        parts[j] = run_experts(
            place, rows_own[j], rows_sib[j], grad_own[j], grad_sib[j],
            gate_weight[0], up_weight[0], down_weight[0],
        )
    back = scatter_plane([parts[j][0] for j in range(4)], [parts[j][1] for j in range(4)])
    weight_chunks = run_weight_grads(place, [parts[j][4:9] for j in range(4)])
    mixed = scatter_plane([parts[j][2] for j in range(4)], [parts[j][3] for j in range(4)])

    output = (after + mixed).astype(bf16).reshape(MICRO, TOK_MB, D)

    weight_sum = weight_chunks[0].astype(f32)
    for k in (1, 3, 2):
        weight_sum = weight_sum + along_x(weight_chunks[k], -k).astype(f32)
    weight_sum = weight_sum.astype(bf16)
    weight_all = [weight_sum] + [along_x(weight_sum, k) for k in (1, 2, 3)]
    weight_all = jnp.stack(weight_all)
    ordered = [
        lax.dynamic_index_in_dim(weight_all, (x_at + 4 - a) % 4, 0, keepdims=False) for a in range(4)
    ]
    gate_total = jnp.concatenate([v[0:256] for v in ordered], axis=0).astype(f32)[None]
    up_total = jnp.concatenate([v[256:512] for v in ordered], axis=0).astype(f32)[None]
    down_total = jnp.concatenate(
        [jnp.concatenate([v[512:640], v[640:768]], axis=1) for v in ordered], axis=0
    ).astype(f32)[None]

    grad_out = grad_low.astype(f32)
    dots = back[ROWS:ROWS + 4] + back[ROWS + 4:ROWS + 8]
    gate_grad = dots.reshape(EXPERTS, ROWS).T * valid
    logit_grad = gates * (gate_grad - jnp.sum(gates * gate_grad, axis=-1, keepdims=True))
    router_local = lax.dot_general(
        logit_grad, second, (((0,), (0,)), ((), ())), precision=highest, preferred_element_type=f32
    )
    second_grad = back[0:ROWS] + jnp.dot(
        logit_grad, router_full, precision=highest, preferred_element_type=f32
    )
    after_norm_grad, gain_second_grad = rms_backward(
        second_grad, after, inverse_second, gain_second
    )
    after_grad = grad_out + after_norm_grad
    attn_grad = (valid * after_grad).astype(bf16)
    attn_grad_own, attn_grad_other = pick_half(attn_grad)
    attended_grad = nt(attn_grad_own, out_own) + nt(attn_grad_other, out_sib)
    attended_grad = in_place(
        [attended_grad[:, k * 256:(k + 1) * 256].astype(bf16) for k in range(4)], x_at, 1
    )
    attended_grad = attended_grad.reshape(ROWS, KEY_VALUE_HEADS, groups, HEAD_SIZE)
    value_grad = jnp.einsum(
        "kgqp,qkgd->pkd", probs.astype(bf16), attended_grad, preferred_element_type=f32
    )
    prob_grad = jnp.einsum("qkgd,pkd->kgqp", attended_grad, value_low, preferred_element_type=f32)
    score_grad = (
        probs * (prob_grad - jnp.sum(probs * prob_grad, axis=-1, keepdims=True))
    ).astype(bf16)
    query_grad = (
        jnp.einsum("kgqp,pkd->qkgd", score_grad, key_low, preferred_element_type=f32) * scale
    )
    key_grad = (
        jnp.einsum("kgqp,qkgd->pkd", score_grad, query_low, preferred_element_type=f32) * scale
    )
    query_grad = rotate(query_grad.reshape(ROWS, QUERY_HEADS, HEAD_SIZE), cosine, -sine)
    key_grad = rotate(key_grad, cosine, -sine)
    projected_grad = jnp.concatenate(
        [
            query_grad.reshape(ROWS, D),
            key_grad.reshape(ROWS, KV),
            value_grad.reshape(ROWS, KV),
        ],
        axis=1,
    ).astype(bf16)
    projected_own, projected_other = pick_half(projected_grad)
    normed_grad = nt(projected_own, qkv_own) + nt(projected_other, qkv_sib)
    normed_grad = in_place([normed_grad[:, k * 256:(k + 1) * 256] for k in range(4)], x_at, 1)
    input_norm_grad, gain_first_grad = rms_backward(normed_grad, inputs, inverse_first, gain_first)
    input_grad = (after_grad + input_norm_grad).reshape(MICRO, TOK_MB, D)

    normed_pair = jnp.concatenate([normed_rel, swap_core(normed_rel)], axis=0)
    attended_pair = jnp.concatenate([attended_rel, swap_core(attended_rel)], axis=0)
    attn_pair = jnp.concatenate([attn_grad_own, swap_core(attn_grad_other)], axis=0)
    projected_pair = jnp.concatenate([projected_own, swap_core(projected_other)], axis=0)

    def local_chunk(k):
        at = (first_at + k) % 4
        return jnp.concatenate(
            [
                tn(normed_pair, block_at(projected_pair, at, 256, 1)),
                tn(attended_pair, block_at(attn_pair, at, 128, 1)),
            ],
            axis=1,
        ).astype(bf16)

    total = local_chunk(0).astype(f32)
    for k in (1, 3, 2):
        total = total + along_first(local_chunk(k), k).astype(f32)
    total = total.astype(bf16).reshape(4, 4, 64, 384)
    chunk = [
        lax.dynamic_index_in_dim(total, (second_at + s) % 4, 1, keepdims=False) for s in range(4)
    ]
    total = chunk[0].astype(f32)
    for s in (1, 3, 2):
        total = total + along_second(chunk[s], s).astype(f32)
    total = total.astype(bf16)
    shard = total[0].astype(f32)
    for k in (1, 3, 2):
        shard = shard + along_x(total[k], -k).astype(f32)
    shard = shard.astype(bf16)
    shard = in_place([shard] + [along_second(shard, k) for k in (1, 2, 3)], second_at, 0)
    shard = [shard] + [along_first(shard, k) for k in (1, 2, 3)]
    qkv_mine = in_place([v[:, :256] for v in shard], first_at, 1)
    out_mine = in_place([v[:, 256:] for v in shard], first_at, 1)
    both = jnp.concatenate([qkv_mine, out_mine], axis=1)
    other = swap_core(both)
    qkv_grad = join_half(both[:, :D], other[:, :D]).astype(f32)
    out_proj_grad = join_half(both[:, D:], other[:, D:]).astype(f32)

    tiny = jnp.concatenate(
        [router_local, gain_first_grad[None], gain_second_grad[None], jnp.zeros((6, D), f32)], axis=0
    )
    tiny = behind(tiny, x_at, 256, 1)
    tiny = tiny[0] + along_x(tiny[1], -1) + along_x(tiny[3], -3) + along_x(tiny[2], -2)
    tiny = tiny + swap_core(tiny)
    tiny = tiny + along_first(tiny, 1) + along_first(tiny, 3) + along_first(tiny, 2)
    tiny = tiny + along_second(tiny, 1) + along_second(tiny, 3) + along_second(tiny, 2)

    return (
        output,
        input_grad,
        tiny[32],
        qkv_grad,
        out_proj_grad,
        tiny[33],
        tiny[0:32].T,
        gate_total,
        up_total,
        down_total,
    )


def solution(mesh):
    grid = Mesh(mesh.devices.reshape(4, 4, 4, 2), ("x", "y", "z", "core"))
    every = ("x", "y", "z", "core")
    plane = ("y", "z", "core")
    return jax.shard_map(
        per_device,
        mesh=grid,
        in_specs=(
            P(None, every, None),
            P(None, every),
            P(None, every),
            P(None, every, None),
            P("x"),
            P("x", None),
            P("x", None),
            P("x"),
            P("x", None),
            P(plane, None, None),
            P(plane, None, None),
            P(plane, None, None),
            P(None, every, None),
        ),
        out_specs=(
            P(None, every, None),
            P(None, every, None),
            P("x"),
            P("x", None),
            P("x", None),
            P("x"),
            P("x", None),
            P(plane, None, None),
            P(plane, None, None),
            P(plane, None, None),
        ),
        check_vma=False,
    )
```

```python
import functools

import jax
import jax.numpy as jnp
from jax import lax
from jax.experimental import pallas as pl
from jax.experimental.pallas import tpu as pltpu
from jax.sharding import Mesh
from jax.sharding import PartitionSpec as P

D = 1024
QUERY_HEADS = 16
KEY_VALUE_HEADS = 8
HEAD_SIZE = 64
FFE = 512
TOPK = 8
MICRO = 2
TOK_MB = 64
EXPERTS = 32
CAP = 24
ROWS = MICRO * TOK_MB
SLOTS = MICRO * CAP
EXTRA = 16
WIDE = ROWS + EXTRA
KV = KEY_VALUE_HEADS * HEAD_SIZE
SMALL_AT = D + D // 2
SHORT = pl.CostEstimate(flops=1_000_000, bytes_accessed=100_000, transcendentals=0)

epsilon = 1e-06
highest = lax.Precision.HIGHEST
f32 = jnp.float32
bf16 = jnp.bfloat16


def plane_pairs(first, second, swap):
    pairs = []
    for y in range(4):
        for z in range(4):
            for c in range(2):
                dy, dz = (first, second) if c == 0 else (second, first)
                target = (((y + dy) % 4) * 4 + (z + dz) % 4) * 2 + (c ^ swap)
                pairs.append(((y * 4 + z) * 2 + c, target))
    return pairs


def along_first(v, k):
    return lax.ppermute(v, ("y", "z", "core"), plane_pairs(k % 4, 0, 0))


def along_second(v, k):
    return lax.ppermute(v, ("y", "z", "core"), plane_pairs(0, k % 4, 0))


def swap_core(v):
    return lax.ppermute(v, "core", [(0, 1), (1, 0)])


def along_x(v, k):
    return lax.ppermute(v, "x", [(i, (i + k) % 4) for i in range(4)])


def stage(*values):
    return lax.optimization_barrier(values)


def spread_first(v):
    return [along_first(v, k) for k in (1, 2, 3)]


def add(first, *others):
    total = first.astype(f32)
    for v in others:
        total = total + v.astype(f32)
    return total


def nt(a, b):
    return lax.dot_general(a, b, (((1,), (1,)), ((), ())), preferred_element_type=f32)


def tn(a, b):
    return lax.dot_general(a, b, (((0,), (0,)), ((), ())), preferred_element_type=f32)


def nn(a, b):
    return jnp.dot(a, b, preferred_element_type=f32)


BLOCKS = 8
PACKED = BLOCKS * SLOTS


def expert_kernel(n_rows, n_grads, place_ref, *refs):
    row_refs, refs = refs[:n_rows], refs[n_rows:]
    grad_refs, refs = refs[:n_grads], refs[n_grads:]
    gate_ref, up_ref, down_ref = refs[:3]
    back_refs, out_refs, save_refs = refs[3:5], refs[5:7], refs[7:12]
    (row_buf, grad_buf, back_buf, out_buf, x_buf, c_buf, r_buf, s_buf, h_buf, g_buf, u_buf,
     mix_buf, pick_buf, dot_buf, gate_buf, up_buf, down_buf,
     row_sem, grad_sem, back_sem, out_sem, save_sem, weight_sem) = refs[12:]

    def pieces(sources, buf, sem):
        copies = []
        for ref in sources:
            for b in range(ref.shape[0]):
                at = len(copies)
                copies.append(pltpu.make_async_copy(ref.at[b], buf.at[at], sem.at[at]))
        return copies

    row_loads = pieces(row_refs, row_buf, row_sem)
    grad_loads = pieces(grad_refs, grad_buf, grad_sem)
    weight_loads = [
        pltpu.make_async_copy(ref, buf, weight_sem.at[i])
        for i, (ref, buf) in enumerate(
            zip((gate_ref, up_ref, down_ref), (gate_buf, up_buf, down_buf))
        )
    ]
    for one, two in zip(row_loads, grad_loads):
        one.start()
        two.start()
    for copy in weight_loads:
        copy.start()

    expert = place_ref[0]
    row_at = expert % 4
    lane_at = pl.multiple_of((expert // 4) * 128, 128)
    upper = (
        lax.broadcasted_iota(jnp.int32, (ROWS, ROWS), 0)
        < lax.broadcasted_iota(jnp.int32, (ROWS, ROWS), 1)
    ).astype(bf16)
    extra_row = lax.broadcasted_iota(jnp.int32, (EXTRA, 128), 0)
    slot_row = lax.broadcasted_iota(jnp.int32, (SLOTS, ROWS), 0).astype(f32)

    @pl.loop(0, BLOCKS)
    def _(b):
        pltpu.make_async_copy(row_refs[0].at[0], row_buf.at[b], row_sem.at[b]).wait()
        pltpu.make_async_copy(grad_refs[0].at[0], grad_buf.at[b], grad_sem.at[b]).wait()
        info = row_buf[b, ROWS:WIDE, pl.ds(lane_at, 128)].astype(f32)
        high = jnp.sum(jnp.where(extra_row == row_at, info, 0.0), axis=0, keepdims=True)
        low = jnp.sum(jnp.where(extra_row == row_at + 4, info, 0.0), axis=0, keepdims=True)
        chosen = high > 0.0
        flags = jnp.broadcast_to(chosen.astype(f32), (16, ROWS)).astype(bf16)
        rank = nn(flags, upper)[0:1]
        pick = jnp.where((slot_row == rank) & chosen, 1.0, 0.0)
        weight = jnp.sum(pick * (high + low), axis=1, keepdims=True)
        low_pick = pick.astype(bf16)
        pick_buf[b] = low_pick
        span = pl.ds(pl.multiple_of(b * SLOTS, SLOTS), SLOTS)
        mix_buf[span, :] = jnp.broadcast_to(weight, (SLOTS, 128))
        x_buf[span, :] = nn(low_pick, row_buf[b, 0:ROWS, :]).astype(bf16)
        c_buf[span, :] = nn(low_pick, grad_buf[b]).astype(bf16)

    saves = [
        pltpu.make_async_copy(buf, ref, save_sem.at[i])
        for i, (buf, ref) in enumerate(zip((x_buf, s_buf, h_buf, g_buf, u_buf), save_refs))
    ]
    saves[0].start()
    mixing = mix_buf[:, 0:1]
    grads = c_buf[...].astype(f32)
    s_buf[...] = (mixing * grads).astype(bf16)
    saves[1].start()
    for copy in weight_loads:
        copy.wait()
    gate_pre = nn(x_buf[...], gate_buf[...])
    up_pre = nn(x_buf[...], up_buf[...])
    sigma = 1.0 / (1.0 + jnp.exp(-gate_pre))
    swish = gate_pre * sigma
    h_buf[...] = (swish * up_pre).astype(bf16)
    saves[2].start()
    hidden_grad = nt(s_buf[...], down_buf[...])
    slope = sigma * (1.0 + gate_pre * (1.0 - sigma))
    g_buf[...] = (hidden_grad * up_pre * slope).astype(bf16)
    u_buf[...] = (hidden_grad * swish).astype(bf16)
    saves[3].start()
    saves[4].start()
    r_buf[...] = (nt(g_buf[...], gate_buf[...]) + nt(u_buf[...], up_buf[...])).astype(bf16)
    produced = nn(h_buf[...], down_buf[...]).astype(bf16).astype(f32)
    gate_grad = jnp.sum(produced * c_buf[...].astype(f32), axis=1, keepdims=True)
    dot_buf[...] = jnp.broadcast_to(gate_grad, (PACKED, 128))
    c_buf[...] = (mixing * produced).astype(bf16)

    @pl.loop(0, BLOCKS)
    def _(b):
        low_pick = pick_buf[b]
        span = pl.ds(pl.multiple_of(b * SLOTS, SLOTS), SLOTS)
        back_buf[b, 0:ROWS, :] = tn(low_pick, r_buf[span, :]).astype(bf16)
        out_buf[b] = tn(low_pick, c_buf[span, :]).astype(bf16)
        back_buf[b, ROWS:WIDE, :] = jnp.zeros((EXTRA, D), bf16)
        dots = jnp.sum(low_pick.astype(f32) * dot_buf[span, :], axis=0, keepdims=True)
        high = dots.astype(bf16).astype(f32)
        info = jnp.where(extra_row == row_at, high, 0.0)
        info = info + jnp.where(extra_row == row_at + 4, dots - high, 0.0)
        back_buf[b, ROWS:WIDE, pl.ds(lane_at, 128)] = info.astype(bf16)
        for side in range(2):
            @pl.when(b // 4 == side)
            def _():
                at = b - 4 * side
                pltpu.make_async_copy(back_buf.at[b], back_refs[side].at[at], back_sem.at[b]).start()
                pltpu.make_async_copy(out_buf.at[b], out_refs[side].at[at], out_sem.at[b]).start()

    for b in range(BLOCKS):
        side, at = b // 4, b % 4
        pltpu.make_async_copy(back_buf.at[b], back_refs[side].at[at], back_sem.at[b]).wait()
        pltpu.make_async_copy(out_buf.at[b], out_refs[side].at[at], out_sem.at[b]).wait()
    for copy in saves:
        copy.wait()


def run_experts(place, rows, grads, gate, up, down):
    any_space = pl.BlockSpec(memory_space=pl.ANY)
    wide = jax.ShapeDtypeStruct((4, WIDE, D), bf16)
    flat = jax.ShapeDtypeStruct((4, ROWS, D), bf16)
    full = jax.ShapeDtypeStruct((PACKED, D), bf16)
    half = jax.ShapeDtypeStruct((PACKED, FFE), bf16)
    return pl.pallas_call(
        functools.partial(expert_kernel, len(rows), len(grads)),
        in_specs=[pl.BlockSpec(memory_space=pltpu.SMEM)]
        + [any_space] * (len(rows) + len(grads) + 3),
        out_specs=[any_space] * 9,
        out_shape=[wide, wide, flat, flat, full, full, half, half, half],
        scratch_shapes=[
            pltpu.VMEM((BLOCKS, WIDE, D), bf16),
            pltpu.VMEM((BLOCKS, ROWS, D), bf16),
            pltpu.VMEM((BLOCKS, WIDE, D), bf16),
            pltpu.VMEM((BLOCKS, ROWS, D), bf16),
            pltpu.VMEM((PACKED, D), bf16),
            pltpu.VMEM((PACKED, D), bf16),
            pltpu.VMEM((PACKED, D), bf16),
            pltpu.VMEM((PACKED, D), bf16),
            pltpu.VMEM((PACKED, FFE), bf16),
            pltpu.VMEM((PACKED, FFE), bf16),
            pltpu.VMEM((PACKED, FFE), bf16),
            pltpu.VMEM((PACKED, 128), f32),
            pltpu.VMEM((BLOCKS, SLOTS, ROWS), bf16),
            pltpu.VMEM((PACKED, 128), f32),
            pltpu.VMEM((D, FFE), bf16),
            pltpu.VMEM((D, FFE), bf16),
            pltpu.VMEM((FFE, D), bf16),
            pltpu.SemaphoreType.DMA((BLOCKS,)),
            pltpu.SemaphoreType.DMA((BLOCKS,)),
            pltpu.SemaphoreType.DMA((BLOCKS,)),
            pltpu.SemaphoreType.DMA((BLOCKS,)),
            pltpu.SemaphoreType.DMA((5,)),
            pltpu.SemaphoreType.DMA((3,)),
        ],
        compiler_params=pltpu.CompilerParams(vmem_limit_bytes=60 * 1024 * 1024),
        cost_estimate=SHORT,
        name="experts",
    )(place, *rows, *grads, gate, up, down)


def weight_grad_kernel(*refs):
    xs, ss, hs, gs, us = (refs[4 * i:4 * i + 4] for i in range(5))
    outs = refs[20:23]
    x_buf, s_buf, h_buf, g_buf, u_buf, gate_buf, up_buf, down_buf, in_sem, out_sem = refs[23:]
    loads = []
    for j in range(4):
        for i, (sources, buf) in enumerate(
            zip((xs, gs, us, hs, ss), (x_buf, g_buf, u_buf, h_buf, s_buf))
        ):
            loads.append(pltpu.make_async_copy(sources[j], buf.at[j], in_sem.at[j, i]))
    for copy in loads:
        copy.start()
    for copy in loads:
        copy.wait()

    @pl.loop(0, 4)
    def _(k):
        wide_at = pl.multiple_of(k * 256, 256)
        thin_at = pl.multiple_of(k * 128, 128)
        rows = x_buf[:, :, pl.ds(wide_at, 256)].reshape(4 * PACKED, 256)
        thin = h_buf[:, :, pl.ds(thin_at, 128)].reshape(4 * PACKED, 128)
        gate_buf[k] = tn(rows, g_buf[...].reshape(4 * PACKED, FFE)).astype(bf16)
        up_buf[k] = tn(rows, u_buf[...].reshape(4 * PACKED, FFE)).astype(bf16)
        down_buf[k] = tn(thin, s_buf[...].reshape(4 * PACKED, D)).astype(bf16)
        for i, (buf, n) in enumerate(((gate_buf, 256), (up_buf, 256), (down_buf, 128))):
            span = pl.ds(pl.multiple_of(k * n, n), n)
            pltpu.make_async_copy(buf.at[k], outs[i].at[span, :], out_sem.at[i, k]).start()

    for k in range(4):
        for i, (buf, n) in enumerate(((gate_buf, 256), (up_buf, 256), (down_buf, 128))):
            span = pl.ds(k * n, n)
            pltpu.make_async_copy(buf.at[k], outs[i].at[span, :], out_sem.at[i, k]).wait()


def run_weight_grads(saved):
    operands = [part[i] for i in range(5) for part in saved]
    any_space = pl.BlockSpec(memory_space=pl.ANY)
    return pl.pallas_call(
        weight_grad_kernel,
        in_specs=[any_space] * 20,
        out_specs=[any_space] * 3,
        out_shape=[
            jax.ShapeDtypeStruct((D, FFE), bf16),
            jax.ShapeDtypeStruct((D, FFE), bf16),
            jax.ShapeDtypeStruct((FFE, D), bf16),
        ],
        scratch_shapes=[
            pltpu.VMEM((4, PACKED, D), bf16),
            pltpu.VMEM((4, PACKED, D), bf16),
            pltpu.VMEM((4, PACKED, FFE), bf16),
            pltpu.VMEM((4, PACKED, FFE), bf16),
            pltpu.VMEM((4, PACKED, FFE), bf16),
            pltpu.VMEM((4, 256, FFE), bf16),
            pltpu.VMEM((4, 256, FFE), bf16),
            pltpu.VMEM((4, 128, D), bf16),
            pltpu.SemaphoreType.DMA((4, 5)),
            pltpu.SemaphoreType.DMA((3, 4)),
        ],
        compiler_params=pltpu.CompilerParams(vmem_limit_bytes=60 * 1024 * 1024),
        cost_estimate=SHORT,
        name="expert_weight_grads",
    )(*operands)


def blocks_behind(x_at, n):
    return [pl.multiple_of(((x_at + 4 - k) % 4) * n, n) for k in range(4)]


def swapped_halves(v):
    lane = lax.broadcasted_iota(jnp.int32, v.shape, 1)
    return jnp.where(lane % HEAD_SIZE < HEAD_SIZE // 2, pltpu.roll(v, 96, 1), pltpu.roll(v, 32, 1))


def project_kernel(
    place_ref, x_ref, mine_ref, own_ref, sib_ref, tiny_ref, table_ref,
    normed_ref, q_ref, kv_ref, small_ref,
    norm_buf, all_buf, tiny_buf,
):
    x_at, core = place_ref[1], place_ref[4]
    lanes = blocks_behind(x_at, 256)
    for k in range(4):
        piece = tiny_ref[...] if k == 0 else own_ref[(k - 1) * 256:k * 256, SMALL_AT:SMALL_AT + 128]
        tiny_buf[:, pl.ds(lanes[k], 256)] = piece.astype(f32).T
    small_ref[...] = tiny_buf[0:40, :]
    x = x_ref[...].astype(f32)
    inverse = lax.rsqrt(jnp.mean(x * x, axis=1, keepdims=True) + epsilon)
    norm_buf[...] = (x * inverse * tiny_buf[32:33, :]).astype(bf16)
    rows = [norm_buf[:, pl.ds(at, 256)] for at in lanes]
    for k in range(4):
        normed_ref[:, k * 256:(k + 1) * 256] = rows[k]
    own_at = pl.multiple_of(core * D, D)
    sib_at = pl.multiple_of((1 - core) * D, D)
    for at, rest in ((own_at, own_ref), (sib_at, sib_ref)):
        total = nn(rows[0], mine_ref[:, pl.ds(at, D)])
        for k in (1, 2, 3):
            total = total + nn(rows[k], rest[(k - 1) * 256:k * 256, 0:D])
        all_buf[:, pl.ds(at, D)] = total
    cosine, sine = table_ref[:, 0:128], table_ref[:, 128:256]
    for c in range(12):
        v = all_buf[:, c * 128:(c + 1) * 128]
        turned = (v * cosine + swapped_halves(v) * sine).astype(bf16)
        if c < 8:
            q_ref[:, c * 128:(c + 1) * 128] = turned
        else:
            kv_ref[:, (c - 8) * 128:(c - 7) * 128] = turned
    kv_ref[:, KV:2 * KV] = all_buf[:, D + KV:D + 2 * KV].astype(bf16)


def head_scores(q_ref, kv_ref, allowed, h):
    chunk = q_ref[:, h * 128:(h + 1) * 128]
    query = jnp.concatenate([chunk[:, 0:64], chunk[:, 64:128]], axis=0)
    key = kv_ref[:, h * 64:(h + 1) * 64]
    value = kv_ref[:, KV + h * 64:KV + (h + 1) * 64]
    scores = jnp.where(allowed, nt(query, key) * HEAD_SIZE ** (-0.5), -1e30)
    expo = jnp.exp(scores - jnp.max(scores, axis=1, keepdims=True))
    probs = expo / jnp.sum(expo, axis=1, keepdims=True)
    return query, key, value, probs


def allowed_pairs(table_ref):
    shape = (2 * ROWS, ROWS)
    column = table_ref[:, 289:290]
    row = table_ref[:, 256:384].T[33:34]
    q = lax.broadcasted_iota(jnp.int32, shape, 0) % ROWS
    p = lax.broadcasted_iota(jnp.int32, shape, 1)
    return (jnp.concatenate([column, column], axis=0) == row) & (p <= q)


def attend_kernel(
    place_ref, x_ref, q_ref, kv_ref, small_ref, mine_ref, own_ref, sib_ref,
    table_ref,
    line_ref, after_ref, gates_ref, sent_ref,
    low_buf, out_buf,
):
    x_at, core = place_ref[1], place_ref[4]
    allowed = allowed_pairs(table_ref)
    for h in range(KEY_VALUE_HEADS):
        _, _, value, probs = head_scores(q_ref, kv_ref, allowed, h)
        got = nn(probs.astype(bf16), value)
        low_buf[:, h * 128:(h + 1) * 128] = jnp.concatenate(
            [got[0:ROWS], got[ROWS:2 * ROWS]], axis=1
        ).astype(bf16)
    rows = [low_buf[:, pl.ds(at, 256)] for at in blocks_behind(x_at, 256)]
    for k in range(4):
        line_ref[:, k * 256:(k + 1) * 256] = rows[k]
    own_at = pl.multiple_of(core * 512, 512)
    sib_at = pl.multiple_of((1 - core) * 512, 512)
    for at, rest in ((own_at, own_ref), (sib_at, sib_ref)):
        total = nn(rows[0], mine_ref[:, pl.ds(at, 512)])
        for k in (1, 2, 3):
            total = total + nn(rows[k], rest[(k - 1) * 256:k * 256, D:SMALL_AT])
        out_buf[:, pl.ds(at, 512)] = total
    valid = table_ref[:, 288:289]
    after = x_ref[...].astype(f32) + valid * out_buf[...]
    after_ref[...] = after
    inverse = lax.rsqrt(jnp.mean(after * after, axis=1, keepdims=True) + epsilon)
    second = after * inverse * small_ref[33:34, :]
    logits = lax.dot_general(
        second, small_ref[0:32, :], (((1,), (1,)), ((), ())),
        precision=highest, preferred_element_type=f32,
    )
    member = table_ref[:, 256:288] > 0.0
    masked = jnp.where(member, logits, -3e38)
    gates = jnp.where(member, jnp.exp(masked - jnp.max(masked, axis=1, keepdims=True)), 0.0)
    gates = gates / jnp.sum(gates, axis=1, keepdims=True)
    gates_ref[...] = gates
    mixing = jnp.concatenate([gates * valid, jnp.zeros((ROWS, 96), f32)], axis=1).T
    high = mixing[0:32].astype(bf16).astype(f32)
    low = mixing[0:32] - high
    info = [
        jnp.concatenate([high[4 * q:4 * q + 4], low[4 * q:4 * q + 4], jnp.zeros((8, 128), f32)], axis=0)
        for q in range(8)
    ]
    sent_ref[0:ROWS, :] = second.astype(bf16)
    sent_ref[ROWS:WIDE, :] = jnp.concatenate(info, axis=1).astype(bf16)


def norm_backward(grad, values, gain):
    inverse = lax.rsqrt(jnp.mean(values * values, axis=1, keepdims=True) + epsilon)
    scaled = grad * gain
    gain_grad = jnp.sum(grad * values * inverse, axis=0, keepdims=True)
    dot = jnp.mean(scaled * values, axis=1, keepdims=True)
    return inverse * (scaled - values * (inverse * inverse * dot)), gain_grad


def attend_back_kernel(
    place_ref, b0, b1, b2, b3, cot_ref, after_ref, gates_ref, small_ref,
    mine_ref, own_ref, sib_ref, q_ref, kv_ref, table_ref,
    mine_out, other_out, after_grad_ref, tiny_ref,
    low_buf, sum_buf, grad_buf, all_buf,
):
    x_at, first_at, second_at, core = (place_ref[i] for i in (1, 2, 3, 4))
    back = b0[...].astype(f32) + b1[...].astype(f32) + b2[...].astype(f32) + b3[...].astype(f32)
    extra = back[ROWS:WIDE]
    dots = extra[0:4] + extra[4:8]
    dots = jnp.concatenate([dots[:, q * 128:(q + 1) * 128] for q in range(8)], axis=0)
    dots = jnp.concatenate([dots, jnp.zeros((96, ROWS), f32)], axis=0).T[:, 0:32]
    valid, gates = table_ref[:, 288:289], gates_ref[...]
    gate_grad = dots * valid
    logit_grad = gates * (gate_grad - jnp.sum(gates * gate_grad, axis=1, keepdims=True))
    after = after_ref[...]
    gain = small_ref[33:34, :]
    inverse = lax.rsqrt(jnp.mean(after * after, axis=1, keepdims=True) + epsilon)
    second = after * inverse * gain
    wide_grad = jnp.concatenate([logit_grad, jnp.zeros((ROWS, 96), f32)], axis=1)
    tiny_ref[0:32, :] = jnp.dot(
        wide_grad.T, second, precision=highest, preferred_element_type=f32
    )[0:32]
    second_grad = back[0:ROWS] + jnp.dot(
        logit_grad, small_ref[0:32, :], precision=highest, preferred_element_type=f32
    )
    norm_grad, gain_grad = norm_backward(second_grad, after, gain)
    tiny_ref[32:40, :] = jnp.concatenate(
        [jnp.zeros((1, D), f32), gain_grad, jnp.zeros((6, D), f32)], axis=0
    )
    after_grad = cot_ref[...].astype(f32) + norm_grad
    after_grad_ref[...] = after_grad
    low_buf[...] = (valid * after_grad).astype(bf16)
    own_at = pl.multiple_of(core * 512, 512)
    sib_at = pl.multiple_of((1 - core) * 512, 512)
    own = low_buf[:, pl.ds(own_at, 512)]
    other = low_buf[:, pl.ds(sib_at, 512)]
    lanes = blocks_behind(x_at, 256)
    for k in range(4):
        if k == 0:
            got = nt(own, mine_ref[:, pl.ds(own_at, 512)]) + nt(other, mine_ref[:, pl.ds(sib_at, 512)])
        else:
            span = slice((k - 1) * 256, k * 256)
            got = nt(own, own_ref[span, D:SMALL_AT]) + nt(other, sib_ref[span, D:SMALL_AT])
        grad_buf[:, pl.ds(lanes[k], 256)] = got.astype(bf16)
    allowed = allowed_pairs(table_ref)
    cosine, sine = table_ref[:, 0:128], table_ref[:, 128:256]
    scale = HEAD_SIZE ** (-0.5)
    for h in range(KEY_VALUE_HEADS):
        query, key, value, probs = head_scores(q_ref, kv_ref, allowed, h)
        chunk = grad_buf[:, h * 128:(h + 1) * 128]
        grad = jnp.concatenate([chunk[:, 0:64], chunk[:, 64:128]], axis=0)
        prob_grad = nt(grad, value)
        score_grad = (
            probs * (prob_grad - jnp.sum(probs * prob_grad, axis=1, keepdims=True))
        ).astype(bf16)
        value_grad = tn(probs.astype(bf16), grad)
        query_grad = nn(score_grad, key) * scale
        key_grad = tn(score_grad, query) * scale
        sum_buf[:, h * 128:(h + 1) * 128] = jnp.concatenate(
            [query_grad[0:ROWS], query_grad[ROWS:2 * ROWS]], axis=1
        )
        sum_buf[:, D + h * 64:D + (h + 1) * 64] = key_grad
        all_buf[:, D + KV + h * 64:D + KV + (h + 1) * 64] = value_grad.astype(bf16)
    for c in range(12):
        v = sum_buf[:, c * 128:(c + 1) * 128]
        all_buf[:, c * 128:(c + 1) * 128] = (v * cosine - swapped_halves(v) * sine).astype(bf16)
    for f in range(4):
        at = (first_at + f) % 4
        mine_out[f, :, 0:256] = all_buf[:, pl.ds(pl.multiple_of(core * D + at * 256, 256), 256)]
        mine_out[f, :, 256:384] = low_buf[:, pl.ds(pl.multiple_of(core * 512 + at * 128, 128), 128)]
        at = (second_at + f) % 4
        other_out[f, :, 0:256] = all_buf[:, pl.ds(pl.multiple_of((1 - core) * D + at * 256, 256), 256)]
        other_out[f, :, 256:384] = low_buf[
            :, pl.ds(pl.multiple_of((1 - core) * 512 + at * 128, 128), 128)
        ]


def input_back_kernel(
    place_ref, mine_grad, other_grad, mine_ref, own_ref, sib_ref, x_ref, after_grad_ref, small_ref,
    tiny_in,
    input_grad_ref, tiny_ref,
    own_buf, other_buf, grad_buf,
):
    x_at, first_at, second_at, core = (place_ref[i] for i in (1, 2, 3, 4))
    for f in range(4):
        at = pl.multiple_of(((first_at + f) % 4) * 256, 256)
        own_buf[:, pl.ds(at, 256)] = mine_grad[f, :, 0:256]
        at = pl.multiple_of(((second_at + f) % 4) * 256, 256)
        other_buf[:, pl.ds(at, 256)] = other_grad[f, :, 0:256]
    own, other = own_buf[...], other_buf[...]
    own_at = pl.multiple_of(core * D, D)
    sib_at = pl.multiple_of((1 - core) * D, D)
    lanes = blocks_behind(x_at, 256)
    for k in range(4):
        if k == 0:
            got = nt(own, mine_ref[:, pl.ds(own_at, D)]) + nt(other, mine_ref[:, pl.ds(sib_at, D)])
        else:
            span = slice((k - 1) * 256, k * 256)
            got = nt(own, own_ref[span, 0:D]) + nt(other, sib_ref[span, 0:D])
        grad_buf[:, pl.ds(lanes[k], 256)] = got
    norm_grad, gain_grad = norm_backward(
        grad_buf[...], x_ref[...].astype(f32), small_ref[32:33, :]
    )
    input_grad_ref[...] = after_grad_ref[...] + norm_grad
    tiny_ref[0:32, :] = tiny_in[0:32, :]
    tiny_ref[32:40, :] = jnp.concatenate([gain_grad, tiny_in[33:40, :]], axis=0)


def attention_weights_kernel(
    place_ref, n0, n1, n2, n3, n4, a0, a1, a2, a3, a4, g0, g1, g2, g3, g4, t0, t1, t2, t3,
    o0, o1, o2, o3,
    sum_buf, tiny_buf,
):
    x_at, second_at = place_ref[1], place_ref[3]
    grads = [g0[0], g1[0], g2[...], g3[...], g4[...]]
    for lane, width, rows in ((0, 256, (n0, n1, n2, n3, n4)), (256, 128, (a0, a1, a2, a3, a4))):
        total = None
        for ref, grad in zip(rows, grads):
            one = tn(ref[...], grad[:, lane:lane + width])
            total = one if total is None else total + one
        sum_buf[:, lane:lane + width] = total
    tiny_buf[0:40, :] = t0[...] + t1[...] + t2[...] + t3[...]
    tiny_buf[40:128, :] = jnp.zeros((88, D), f32)
    for k, at in enumerate(blocks_behind(x_at, 256)):
        sum_buf[k * 256:(k + 1) * 256, 384:512] = tiny_buf[:, pl.ds(at, 256)].T
    for s, out in enumerate((o0, o1, o2, o3)):
        at = (second_at + s) % 4
        for k in range(4):
            out[k] = sum_buf[pl.ds(pl.multiple_of(k * 256 + at * 64, 64), 64), :].astype(bf16)


def run_local(kernel, name, place, operands, outs, scratch):
    vmem = pl.BlockSpec(memory_space=pltpu.VMEM)
    return pl.pallas_call(
        kernel,
        in_specs=[pl.BlockSpec(memory_space=pltpu.SMEM)] + [vmem] * len(operands),
        out_specs=[vmem] * len(outs),
        out_shape=[jax.ShapeDtypeStruct(shape, kind) for shape, kind in outs],
        scratch_shapes=[pltpu.VMEM(shape, kind) for shape, kind in scratch],
        compiler_params=pltpu.CompilerParams(vmem_limit_bytes=60 * 1024 * 1024),
        cost_estimate=SHORT,
        name=name,
    )(place, *operands)


def block_at(v, index, size, axis):
    return lax.dynamic_slice_in_dim(v, index * size, size, axis)


def behind(v, at, size, axis):
    return [block_at(v, (at + 4 - k) % 4, size, axis) for k in range(4)]


def in_place(blocks, at, axis):
    stack = jnp.stack(blocks)
    return jnp.concatenate(
        [lax.dynamic_index_in_dim(stack, (at + 4 - a) % 4, 0, keepdims=False) for a in range(4)],
        axis=axis,
    )


def per_device(
    hidden_in,
    segment_ids,
    token_counts,
    expert_ids,
    norm_one,
    qkv_weight,
    out_weight,
    norm_two,
    router_weight,
    gate_weight,
    up_weight,
    down_weight,
    cotangent,
):
    x_at = lax.axis_index("x")
    y_at = lax.axis_index("y")
    z_at = lax.axis_index("z")
    core = lax.axis_index("core")
    first_at = jnp.where(core == 0, y_at, z_at)
    second_at = jnp.where(core == 0, z_at, y_at)
    place = jnp.stack([(y_at * 4 + z_at) * 2 + core, x_at, first_at, second_at, core]).astype(jnp.int32)

    grad_low = cotangent.reshape(ROWS, D)
    inputs = hidden_in.reshape(ROWS, D)
    valid = (
        (jnp.arange(TOK_MB, dtype=jnp.int32)[None, :] < token_counts).reshape(ROWS, 1).astype(f32)
    )
    segment_key = (
        segment_ids + (TOK_MB + 1) * jnp.arange(MICRO, dtype=jnp.int32)[:, None]
    ).reshape(ROWS)
    column, row = segment_key[:, None], segment_key[None, :]
    places = jnp.arange(ROWS)
    allowed = (column == row) & (places[:, None] >= places[None, :])
    position = jnp.sum(allowed.astype(f32), axis=1) - 1.0
    frequency = 10000.0 ** (-2.0 * jnp.arange(HEAD_SIZE // 2, dtype=f32) / HEAD_SIZE)
    angles = position[:, None] * frequency[None, :]
    cosine, sine = jnp.cos(angles), jnp.sin(angles)
    routes = expert_ids.reshape(ROWS, TOPK)
    member = jnp.any(
        routes[:, :, None] == jnp.arange(EXPERTS, dtype=jnp.int32)[None, None, :], axis=1
    ).astype(f32)
    table = jnp.concatenate(
        [cosine] * 4 + [-sine, sine, -sine, sine]
        + [member, valid, column.astype(f32), jnp.zeros((ROWS, 94), f32)],
        axis=1,
    )

    small = jnp.concatenate(
        [router_weight, norm_one[:, None], norm_two[:, None], jnp.zeros((256, 94), bf16)], axis=1
    )
    packed = jnp.concatenate(
        [block_at(qkv_weight, core, D, 1), block_at(out_weight, core, FFE, 1), small], axis=1
    )
    back, ahead, got, table = stage(
        along_x(packed, 1), along_x(packed, -1), spread_first(grad_low), table
    )
    low, high = along_x(back[:128], 1), along_x(ahead[128:], -1)
    grad_rows = jnp.stack([grad_low] + got)
    low, high, grad_back, grad_ahead = stage(
        low, high, along_second(grad_rows, 1), along_second(grad_rows, -1)
    )
    full_own = jnp.concatenate([back, low, high, ahead], axis=0)
    full_sib = swap_core(full_own)
    half = (ROWS, D)
    projected = run_local(
        project_kernel, "project", place,
        [inputs, qkv_weight, full_own, full_sib, small, table],
        [(half, bf16), (half, bf16), (half, bf16), ((40, D), f32)],
        [(half, bf16), ((ROWS, 2 * D), f32), ((128, D), f32)],
    )
    projected, grad_two, grad_rows_sib = stage(
        projected, along_second(grad_rows, 2), swap_core(grad_rows)
    )
    grads = {0: [grad_rows, grad_rows_sib]}
    normed, query, kv, small_full = projected
    normed_other = swap_core(normed)
    attended = run_local(
        attend_kernel, "attend", place,
        [inputs, query, kv, small_full, out_weight, full_own, full_sib, table],
        [(half, bf16), (half, f32), ((ROWS, EXPERTS), f32), ((WIDE, D), bf16)],
        [(half, bf16), (half, f32)],
    )
    attended, normed_lines, back_sib, ahead_sib = stage(
        attended, spread_first(jnp.concatenate([normed, normed_other], axis=0)),
        swap_core(grad_back), swap_core(grad_ahead),
    )
    grads[1], grads[3] = [grad_back, back_sib], [grad_ahead, ahead_sib]
    line, after, gates, sent = attended

    def visit(j, *rows):
        return run_experts(
            place, list(rows), grads[j], gate_weight[0], up_weight[0], down_weight[0]
        )

    got, line_other, two_sib = stage(spread_first(sent), swap_core(line), swap_core(grad_two))
    grads[2] = [grad_two, two_sib]
    rows = jnp.stack([sent] + got)
    parts = {}
    parts[0], back, ahead = stage(
        visit(0, rows, swap_core(rows)), along_second(rows, 1), along_second(rows, -1)
    )
    parts[1], two, ahead_sib = stage(
        visit(1, back, swap_core(back)), along_second(rows, 2), swap_core(ahead)
    )
    pair = jnp.concatenate([line, line_other], axis=0)
    parts[3], two_sib, turn, lines = stage(
        visit(3, ahead, ahead_sib), swap_core(two), swap_core(parts[1][1]), spread_first(pair)
    )
    merged = add(parts[1][0], turn).astype(bf16)
    parts[2], got_back, turn = stage(
        visit(2, two, two_sib), along_second(merged, -1), swap_core(parts[3][1])
    )
    merged = add(parts[3][0], turn).astype(bf16)
    got_ahead = along_second(merged, -3)
    merged = add(parts[2][0], swap_core(parts[2][1])).astype(bf16)
    saved = [parts[j][4:9] for j in range(4)]
    merged, first_rows = stage(merged, saved[0][0])
    saved[0] = [first_rows] + list(saved[0][1:])
    chunks, got_ahead, got_two, turn = stage(
        run_weight_grads(saved), got_ahead, along_second(merged, -2), swap_core(parts[0][1])
    )
    expert_sums = [lax.psum(v, "x") for v in chunks]
    total = add(parts[0][0], turn, got_back, got_ahead, got_two).astype(bf16)
    arrived, turn_back, turn_ahead = stage(
        [along_first(total[i], -i) for i in (1, 2, 3)],
        swap_core(parts[1][3]), swap_core(parts[3][3]),
    )
    back = [total[0]] + arrived
    merged_back = add(parts[1][2], turn_back).astype(bf16)
    merged_ahead = add(parts[3][2], turn_ahead).astype(bf16)
    mine_grad, other_grad, after_grad, tiny = run_local(
        attend_back_kernel, "attend_back", place,
        back + [
            grad_low, after, gates, small_full, out_weight, full_own, full_sib,
            query, kv, table,
        ],
        [((4, ROWS, 384), bf16), ((4, ROWS, 384), bf16), (half, f32), ((40, D), f32)],
        [(half, bf16), ((ROWS, 3 * KV), f32), (half, bf16), ((ROWS, 2 * D), bf16)],
    )
    input_grad, tiny = run_local(
        input_back_kernel, "input_back", place,
        [mine_grad, other_grad, qkv_weight, full_own, full_sib, inputs, after_grad, small_full, tiny],
        [(half, f32), ((40, D), f32)],
        [(half, bf16), (half, bf16), (half, f32)],
    )
    input_grad, tiny, mine_grad, sib_grad, turn_two, turn_own, got_back, got_ahead = stage(
        input_grad, tiny, mine_grad, swap_core(other_grad),
        swap_core(parts[2][3]), swap_core(parts[0][3]),
        along_second(merged_back, -1), along_second(merged_ahead, -3),
    )
    merged = add(parts[2][2], turn_two).astype(bf16)

    line_grad = [
        along_first(jnp.concatenate([mine_grad[k], sib_grad[k]], axis=0), k) for k in (1, 2, 3)
    ]
    tiny, tinies, line_grad, got_two = stage(
        tiny, spread_first(tiny), line_grad, along_second(merged, -2)
    )
    chunk = run_local(
        attention_weights_kernel, "attention_weights", place,
        [normed, normed_other, *normed_lines, line, line_other, *lines, mine_grad, sib_grad, *line_grad, tiny, *tinies],
        [((4, 64, 512), bf16)] * 4,
        [((D, 512), f32), ((128, D), f32)],
    )
    total = add(parts[0][2], turn_own, got_back, got_ahead, got_two).astype(bf16)
    chunk, got, arrived, expert_sums = stage(
        chunk, [along_second(chunk[s], s) for s in (1, 2, 3)],
        [along_first(total[i], -i) for i in (1, 2, 3)], expert_sums,
    )
    output = (after + add(total[0], *arrived)).astype(bf16).reshape(MICRO, TOK_MB, D)
    total = add(chunk[0], *got).astype(bf16)
    shard = add(total[0], *[along_x(total[k], -k) for k in (1, 2, 3)]).astype(bf16)
    shard = in_place([shard] + [along_second(shard, k) for k in (1, 2, 3)], second_at, 0)
    tiny = shard[:, 384:]
    shard = shard[:, :384]
    shard = [shard] + spread_first(shard)
    both = jnp.concatenate(
        [
            in_place([v[:, :256] for v in shard], first_at, 1),
            in_place([v[:, 256:] for v in shard], first_at, 1),
            tiny,
        ],
        axis=1,
    )
    expert_sums = [v.astype(f32)[None] for v in expert_sums]
    both, *expert_sums = stage(both, *expert_sums)
    other = swap_core(both)
    tiny = both[:, SMALL_AT:].astype(f32) + other[:, SMALL_AT:].astype(f32)

    def join_half(own, other):
        return jnp.where(
            core == 0,
            jnp.concatenate([own, other], axis=1),
            jnp.concatenate([other, own], axis=1),
        ).astype(f32)

    return (
        output,
        input_grad.reshape(MICRO, TOK_MB, D),
        tiny[:, 32],
        join_half(both[:, :D], other[:, :D]),
        join_half(both[:, D:SMALL_AT], other[:, D:SMALL_AT]),
        tiny[:, 33],
        tiny[:, 0:32],
        expert_sums[0],
        expert_sums[1],
        expert_sums[2],
    )


def solution(mesh):
    grid = Mesh(mesh.devices.reshape(4, 4, 4, 2), ("x", "y", "z", "core"))
    every = ("x", "y", "z", "core")
    plane = ("y", "z", "core")
    return jax.shard_map(
        per_device,
        mesh=grid,
        in_specs=(
            P(None, every, None),
            P(None, every),
            P(None, every),
            P(None, every, None),
            P("x"),
            P("x", None),
            P("x", None),
            P("x"),
            P("x", None),
            P(plane, None, None),
            P(plane, None, None),
            P(plane, None, None),
            P(None, every, None),
        ),
        out_specs=(
            P(None, every, None),
            P(None, every, None),
            P("x"),
            P("x", None),
            P("x", None),
            P("x"),
            P("x", None),
            P(plane, None, None),
            P(plane, None, None),
            P(plane, None, None),
        ),
        check_vma=False,
    )
```

```python
import functools

import jax
import jax.numpy as jnp
from jax import lax
from jax.experimental import pallas as pl
from jax.experimental.pallas import tpu as pltpu
from jax.sharding import Mesh
from jax.sharding import PartitionSpec as P

D = 1024
QUERY_HEADS = 16
KEY_VALUE_HEADS = 8
HEAD_SIZE = 64
FFE = 512
TOPK = 8
MICRO = 2
TOK_MB = 64
EXPERTS = 32
CAP = 24
ROWS = MICRO * TOK_MB
SLOTS = MICRO * CAP
EXTRA = 16
WIDE = ROWS + EXTRA
KV = KEY_VALUE_HEADS * HEAD_SIZE
SMALL_AT = D + D // 2
SHORT = pl.CostEstimate(flops=1_000_000, bytes_accessed=100_000, transcendentals=0)

epsilon = 1e-06
highest = lax.Precision.HIGHEST
f32 = jnp.float32
bf16 = jnp.bfloat16


def plane_pairs(first, second, swap):
    pairs = []
    for y in range(4):
        for z in range(4):
            for c in range(2):
                dy, dz = (first, second) if c == 0 else (second, first)
                target = (((y + dy) % 4) * 4 + (z + dz) % 4) * 2 + (c ^ swap)
                pairs.append(((y * 4 + z) * 2 + c, target))
    return pairs


def along_first(v, k):
    return lax.ppermute(v, ("y", "z", "core"), plane_pairs(k % 4, 0, 0))


def along_second(v, k):
    return lax.ppermute(v, ("y", "z", "core"), plane_pairs(0, k % 4, 0))


def swap_core(v):
    return lax.ppermute(v, "core", [(0, 1), (1, 0)])


def along_x(v, k):
    return lax.ppermute(v, "x", [(i, (i + k) % 4) for i in range(4)])


def stage(*values):
    return lax.optimization_barrier(values)


def spread_first(v):
    return [along_first(v, k) for k in (1, 2, 3)]


def add(first, *others):
    total = first.astype(f32)
    for v in others:
        total = total + v.astype(f32)
    return total


def nt(a, b):
    return lax.dot_general(a, b, (((1,), (1,)), ((), ())), preferred_element_type=f32)


def tn(a, b):
    return lax.dot_general(a, b, (((0,), (0,)), ((), ())), preferred_element_type=f32)


def nn(a, b):
    return jnp.dot(a, b, preferred_element_type=f32)


BLOCKS = 8
PACKED = BLOCKS * SLOTS


def expert_kernel(n_rows, n_grads, place_ref, *refs):
    row_refs, refs = refs[:n_rows], refs[n_rows:]
    grad_refs, refs = refs[:n_grads], refs[n_grads:]
    gate_ref, up_ref, down_ref = refs[:3]
    back_refs, out_refs, save_refs = refs[3:5], refs[5:7], refs[7:12]
    (row_buf, grad_buf, back_buf, out_buf, x_buf, c_buf, r_buf, s_buf, h_buf, g_buf, u_buf,
     mix_buf, pick_buf, dot_buf, gate_buf, up_buf, down_buf,
     row_sem, grad_sem, back_sem, out_sem, save_sem, weight_sem) = refs[12:]

    def pieces(sources, buf, sem):
        copies = []
        for ref in sources:
            for b in range(ref.shape[0]):
                at = len(copies)
                copies.append(pltpu.make_async_copy(ref.at[b], buf.at[at], sem.at[at]))
        return copies

    row_loads = pieces(row_refs, row_buf, row_sem)
    grad_loads = pieces(grad_refs, grad_buf, grad_sem)
    weight_loads = [
        pltpu.make_async_copy(ref, buf, weight_sem.at[i])
        for i, (ref, buf) in enumerate(
            zip((gate_ref, up_ref, down_ref), (gate_buf, up_buf, down_buf))
        )
    ]
    for one, two in zip(row_loads, grad_loads):
        one.start()
        two.start()
    for copy in weight_loads:
        copy.start()

    expert = place_ref[0]
    row_at = expert % 4
    lane_at = pl.multiple_of((expert // 4) * 128, 128)
    upper = (
        lax.broadcasted_iota(jnp.int32, (ROWS, ROWS), 0)
        < lax.broadcasted_iota(jnp.int32, (ROWS, ROWS), 1)
    ).astype(bf16)
    extra_row = lax.broadcasted_iota(jnp.int32, (EXTRA, 128), 0)
    slot_row = lax.broadcasted_iota(jnp.int32, (SLOTS, ROWS), 0).astype(f32)

    @pl.loop(0, BLOCKS)
    def _(b):
        pltpu.make_async_copy(row_refs[0].at[0], row_buf.at[b], row_sem.at[b]).wait()
        pltpu.make_async_copy(grad_refs[0].at[0], grad_buf.at[b], grad_sem.at[b]).wait()
        info = row_buf[b, ROWS:WIDE, pl.ds(lane_at, 128)].astype(f32)
        high = jnp.sum(jnp.where(extra_row == row_at, info, 0.0), axis=0, keepdims=True)
        low = jnp.sum(jnp.where(extra_row == row_at + 4, info, 0.0), axis=0, keepdims=True)
        chosen = high > 0.0
        flags = jnp.broadcast_to(chosen.astype(f32), (16, ROWS)).astype(bf16)
        rank = nn(flags, upper)[0:1]
        pick = jnp.where((slot_row == rank) & chosen, 1.0, 0.0)
        weight = jnp.sum(pick * (high + low), axis=1, keepdims=True)
        low_pick = pick.astype(bf16)
        pick_buf[b] = low_pick
        span = pl.ds(pl.multiple_of(b * SLOTS, SLOTS), SLOTS)
        mix_buf[span, :] = jnp.broadcast_to(weight, (SLOTS, 128))
        x_buf[span, :] = nn(low_pick, row_buf[b, 0:ROWS, :]).astype(bf16)
        c_buf[span, :] = nn(low_pick, grad_buf[b]).astype(bf16)

    saves = [
        pltpu.make_async_copy(buf, ref, save_sem.at[i])
        for i, (buf, ref) in enumerate(zip((x_buf, s_buf, h_buf, g_buf, u_buf), save_refs))
    ]
    saves[0].start()
    mixing = mix_buf[:, 0:1]
    grads = c_buf[...].astype(f32)
    s_buf[...] = (mixing * grads).astype(bf16)
    saves[1].start()
    for copy in weight_loads:
        copy.wait()
    gate_pre = nn(x_buf[...], gate_buf[...])
    up_pre = nn(x_buf[...], up_buf[...])
    sigma = 1.0 / (1.0 + jnp.exp(-gate_pre))
    swish = gate_pre * sigma
    h_buf[...] = (swish * up_pre).astype(bf16)
    saves[2].start()
    hidden_grad = nt(s_buf[...], down_buf[...])
    slope = sigma * (1.0 + gate_pre * (1.0 - sigma))
    g_buf[...] = (hidden_grad * up_pre * slope).astype(bf16)
    u_buf[...] = (hidden_grad * swish).astype(bf16)
    saves[3].start()
    saves[4].start()
    r_buf[...] = (nt(g_buf[...], gate_buf[...]) + nt(u_buf[...], up_buf[...])).astype(bf16)
    produced = nn(h_buf[...], down_buf[...]).astype(bf16).astype(f32)
    gate_grad = jnp.sum(produced * c_buf[...].astype(f32), axis=1, keepdims=True)
    dot_buf[...] = jnp.broadcast_to(gate_grad, (PACKED, 128))
    c_buf[...] = (mixing * produced).astype(bf16)

    @pl.loop(0, BLOCKS)
    def _(b):
        low_pick = pick_buf[b]
        span = pl.ds(pl.multiple_of(b * SLOTS, SLOTS), SLOTS)
        back_buf[b, 0:ROWS, :] = tn(low_pick, r_buf[span, :]).astype(bf16)
        out_buf[b] = tn(low_pick, c_buf[span, :]).astype(bf16)
        back_buf[b, ROWS:WIDE, :] = jnp.zeros((EXTRA, D), bf16)
        dots = jnp.sum(low_pick.astype(f32) * dot_buf[span, :], axis=0, keepdims=True)
        high = dots.astype(bf16).astype(f32)
        info = jnp.where(extra_row == row_at, high, 0.0)
        info = info + jnp.where(extra_row == row_at + 4, dots - high, 0.0)
        back_buf[b, ROWS:WIDE, pl.ds(lane_at, 128)] = info.astype(bf16)
        for side in range(2):
            @pl.when(b // 4 == side)
            def _():
                at = b - 4 * side
                pltpu.make_async_copy(back_buf.at[b], back_refs[side].at[at], back_sem.at[b]).start()
                pltpu.make_async_copy(out_buf.at[b], out_refs[side].at[at], out_sem.at[b]).start()

    for b in range(BLOCKS):
        side, at = b // 4, b % 4
        pltpu.make_async_copy(back_buf.at[b], back_refs[side].at[at], back_sem.at[b]).wait()
        pltpu.make_async_copy(out_buf.at[b], out_refs[side].at[at], out_sem.at[b]).wait()
    for copy in saves:
        copy.wait()


def run_experts(place, rows, grads, gate, up, down):
    any_space = pl.BlockSpec(memory_space=pl.ANY)
    wide = jax.ShapeDtypeStruct((4, WIDE, D), bf16)
    flat = jax.ShapeDtypeStruct((4, ROWS, D), bf16)
    full = jax.ShapeDtypeStruct((PACKED, D), bf16)
    half = jax.ShapeDtypeStruct((PACKED, FFE), bf16)
    return pl.pallas_call(
        functools.partial(expert_kernel, len(rows), len(grads)),
        in_specs=[pl.BlockSpec(memory_space=pltpu.SMEM)]
        + [any_space] * (len(rows) + len(grads) + 3),
        out_specs=[any_space] * 9,
        out_shape=[wide, wide, flat, flat, full, full, half, half, half],
        scratch_shapes=[
            pltpu.VMEM((BLOCKS, WIDE, D), bf16),
            pltpu.VMEM((BLOCKS, ROWS, D), bf16),
            pltpu.VMEM((BLOCKS, WIDE, D), bf16),
            pltpu.VMEM((BLOCKS, ROWS, D), bf16),
            pltpu.VMEM((PACKED, D), bf16),
            pltpu.VMEM((PACKED, D), bf16),
            pltpu.VMEM((PACKED, D), bf16),
            pltpu.VMEM((PACKED, D), bf16),
            pltpu.VMEM((PACKED, FFE), bf16),
            pltpu.VMEM((PACKED, FFE), bf16),
            pltpu.VMEM((PACKED, FFE), bf16),
            pltpu.VMEM((PACKED, 128), f32),
            pltpu.VMEM((BLOCKS, SLOTS, ROWS), bf16),
            pltpu.VMEM((PACKED, 128), f32),
            pltpu.VMEM((D, FFE), bf16),
            pltpu.VMEM((D, FFE), bf16),
            pltpu.VMEM((FFE, D), bf16),
            pltpu.SemaphoreType.DMA((BLOCKS,)),
            pltpu.SemaphoreType.DMA((BLOCKS,)),
            pltpu.SemaphoreType.DMA((BLOCKS,)),
            pltpu.SemaphoreType.DMA((BLOCKS,)),
            pltpu.SemaphoreType.DMA((5,)),
            pltpu.SemaphoreType.DMA((3,)),
        ],
        compiler_params=pltpu.CompilerParams(vmem_limit_bytes=60 * 1024 * 1024),
        cost_estimate=SHORT,
        name="experts",
    )(place, *rows, *grads, gate, up, down)


def weight_grad_kernel(*refs):
    xs, ss, hs, gs, us = (refs[4 * i:4 * i + 4] for i in range(5))
    outs = refs[20:23]
    x_buf, s_buf, h_buf, g_buf, u_buf, gate_buf, up_buf, down_buf, in_sem, out_sem = refs[23:]
    loads = []
    for j in range(4):
        for i, (sources, buf) in enumerate(
            zip((xs, gs, us, hs, ss), (x_buf, g_buf, u_buf, h_buf, s_buf))
        ):
            loads.append(pltpu.make_async_copy(sources[j], buf.at[j], in_sem.at[j, i]))
    for copy in loads:
        copy.start()
    for copy in loads:
        copy.wait()

    @pl.loop(0, 4)
    def _(k):
        wide_at = pl.multiple_of(k * 256, 256)
        thin_at = pl.multiple_of(k * 128, 128)
        rows = x_buf[:, :, pl.ds(wide_at, 256)].reshape(4 * PACKED, 256)
        thin = h_buf[:, :, pl.ds(thin_at, 128)].reshape(4 * PACKED, 128)
        gate_buf[k] = tn(rows, g_buf[...].reshape(4 * PACKED, FFE)).astype(bf16)
        up_buf[k] = tn(rows, u_buf[...].reshape(4 * PACKED, FFE)).astype(bf16)
        down_buf[k] = tn(thin, s_buf[...].reshape(4 * PACKED, D)).astype(bf16)
        for i, (buf, n) in enumerate(((gate_buf, 256), (up_buf, 256), (down_buf, 128))):
            span = pl.ds(pl.multiple_of(k * n, n), n)
            pltpu.make_async_copy(buf.at[k], outs[i].at[span, :], out_sem.at[i, k]).start()

    for k in range(4):
        for i, (buf, n) in enumerate(((gate_buf, 256), (up_buf, 256), (down_buf, 128))):
            span = pl.ds(k * n, n)
            pltpu.make_async_copy(buf.at[k], outs[i].at[span, :], out_sem.at[i, k]).wait()


def run_weight_grads(saved):
    operands = [part[i] for i in range(5) for part in saved]
    any_space = pl.BlockSpec(memory_space=pl.ANY)
    return pl.pallas_call(
        weight_grad_kernel,
        in_specs=[any_space] * 20,
        out_specs=[any_space] * 3,
        out_shape=[
            jax.ShapeDtypeStruct((D, FFE), bf16),
            jax.ShapeDtypeStruct((D, FFE), bf16),
            jax.ShapeDtypeStruct((FFE, D), bf16),
        ],
        scratch_shapes=[
            pltpu.VMEM((4, PACKED, D), bf16),
            pltpu.VMEM((4, PACKED, D), bf16),
            pltpu.VMEM((4, PACKED, FFE), bf16),
            pltpu.VMEM((4, PACKED, FFE), bf16),
            pltpu.VMEM((4, PACKED, FFE), bf16),
            pltpu.VMEM((4, 256, FFE), bf16),
            pltpu.VMEM((4, 256, FFE), bf16),
            pltpu.VMEM((4, 128, D), bf16),
            pltpu.SemaphoreType.DMA((4, 5)),
            pltpu.SemaphoreType.DMA((3, 4)),
        ],
        compiler_params=pltpu.CompilerParams(vmem_limit_bytes=60 * 1024 * 1024),
        cost_estimate=SHORT,
        name="expert_weight_grads",
    )(*operands)


def blocks_behind(x_at, n):
    return [pl.multiple_of(((x_at + 4 - k) % 4) * n, n) for k in range(4)]


def swapped_halves(v):
    lane = lax.broadcasted_iota(jnp.int32, v.shape, 1)
    return jnp.where(lane % HEAD_SIZE < HEAD_SIZE // 2, pltpu.roll(v, 96, 1), pltpu.roll(v, 32, 1))


def project_kernel(
    place_ref, x_ref, mine_ref, own_ref, sib_ref, tiny_ref, table_ref,
    q_ref, kv_ref, small_ref,
    norm_buf, all_buf, tiny_buf, small_buf, own_buf, sib_buf, sem,
):
    x_at, core = place_ref[1], place_ref[4]
    lanes = blocks_behind(x_at, 256)
    loads = [
        pltpu.make_async_copy(own_ref.at[:, SMALL_AT:SMALL_AT + 128], small_buf, sem.at[0]),
        pltpu.make_async_copy(own_ref.at[:, 0:D], own_buf, sem.at[1]),
        pltpu.make_async_copy(sib_ref.at[:, 0:D], sib_buf, sem.at[2]),
    ]
    for copy in loads:
        copy.start()
    loads[0].wait()
    for k in range(4):
        piece = tiny_ref[...] if k == 0 else small_buf[(k - 1) * 256:k * 256, :]
        tiny_buf[:, pl.ds(lanes[k], 256)] = piece.astype(f32).T
    small_ref[...] = tiny_buf[0:40, :]
    x = x_ref[...].astype(f32)
    inverse = lax.rsqrt(jnp.mean(x * x, axis=1, keepdims=True) + epsilon)
    norm_buf[...] = (x * inverse * tiny_buf[32:33, :]).astype(bf16)
    rows = [norm_buf[:, pl.ds(at, 256)] for at in lanes]
    own_at = pl.multiple_of(core * D, D)
    sib_at = pl.multiple_of((1 - core) * D, D)
    for at, rest, copy in ((own_at, own_buf, loads[1]), (sib_at, sib_buf, loads[2])):
        total = nn(rows[0], mine_ref[:, pl.ds(at, D)])
        copy.wait()
        for k in (1, 2, 3):
            total = total + nn(rows[k], rest[(k - 1) * 256:k * 256, :])
        all_buf[:, pl.ds(at, D)] = total
    cosine, sine = table_ref[:, 0:128], table_ref[:, 128:256]
    for c in range(12):
        v = all_buf[:, c * 128:(c + 1) * 128]
        turned = (v * cosine + swapped_halves(v) * sine).astype(bf16)
        if c < 8:
            q_ref[:, c * 128:(c + 1) * 128] = turned
        else:
            kv_ref[:, (c - 8) * 128:(c - 7) * 128] = turned
    kv_ref[:, KV:2 * KV] = all_buf[:, D + KV:D + 2 * KV].astype(bf16)


def head_scores(q_ref, kv_ref, allowed, h):
    chunk = q_ref[:, h * 128:(h + 1) * 128]
    query = jnp.concatenate([chunk[:, 0:64], chunk[:, 64:128]], axis=0)
    key = kv_ref[:, h * 64:(h + 1) * 64]
    value = kv_ref[:, KV + h * 64:KV + (h + 1) * 64]
    scores = jnp.where(allowed, nt(query, key) * HEAD_SIZE ** (-0.5), -1e30)
    expo = jnp.exp(scores - jnp.max(scores, axis=1, keepdims=True))
    probs = expo / jnp.sum(expo, axis=1, keepdims=True)
    return query, key, value, probs


def allowed_pairs(table_ref):
    shape = (2 * ROWS, ROWS)
    column = table_ref[:, 289:290]
    row = table_ref[:, 256:384].T[33:34]
    q = lax.broadcasted_iota(jnp.int32, shape, 0) % ROWS
    p = lax.broadcasted_iota(jnp.int32, shape, 1)
    return (jnp.concatenate([column, column], axis=0) == row) & (p <= q)


def attend_kernel(
    place_ref, x_ref, q_ref, kv_ref, small_ref, mine_ref, own_ref, sib_ref,
    table_ref,
    line_ref, after_ref, gates_ref, sent_ref,
    low_buf, out_buf, own_buf, sib_buf, sem,
):
    x_at, core = place_ref[1], place_ref[4]
    loads = [
        pltpu.make_async_copy(own_ref.at[:, D:SMALL_AT], own_buf, sem.at[0]),
        pltpu.make_async_copy(sib_ref.at[:, D:SMALL_AT], sib_buf, sem.at[1]),
    ]
    for copy in loads:
        copy.start()
    allowed = allowed_pairs(table_ref)
    for h in range(KEY_VALUE_HEADS):
        _, _, value, probs = head_scores(q_ref, kv_ref, allowed, h)
        got = nn(probs.astype(bf16), value)
        low_buf[:, h * 128:(h + 1) * 128] = jnp.concatenate(
            [got[0:ROWS], got[ROWS:2 * ROWS]], axis=1
        ).astype(bf16)
    rows = [low_buf[:, pl.ds(at, 256)] for at in blocks_behind(x_at, 256)]
    for k in range(4):
        line_ref[:, k * 256:(k + 1) * 256] = rows[k]
    own_at = pl.multiple_of(core * 512, 512)
    sib_at = pl.multiple_of((1 - core) * 512, 512)
    for copy in loads:
        copy.wait()
    for at, rest in ((own_at, own_buf), (sib_at, sib_buf)):
        total = nn(rows[0], mine_ref[:, pl.ds(at, 512)])
        for k in (1, 2, 3):
            total = total + nn(rows[k], rest[(k - 1) * 256:k * 256, :])
        out_buf[:, pl.ds(at, 512)] = total
    valid = table_ref[:, 288:289]
    after = x_ref[...].astype(f32) + valid * out_buf[...]
    after_ref[...] = after
    inverse = lax.rsqrt(jnp.mean(after * after, axis=1, keepdims=True) + epsilon)
    second = after * inverse * small_ref[33:34, :]
    logits = lax.dot_general(
        second, small_ref[0:32, :], (((1,), (1,)), ((), ())),
        precision=highest, preferred_element_type=f32,
    )
    member = table_ref[:, 256:288] > 0.0
    masked = jnp.where(member, logits, -3e38)
    gates = jnp.where(member, jnp.exp(masked - jnp.max(masked, axis=1, keepdims=True)), 0.0)
    gates = gates / jnp.sum(gates, axis=1, keepdims=True)
    gates_ref[...] = gates
    mixing = jnp.concatenate([gates * valid, jnp.zeros((ROWS, 96), f32)], axis=1).T
    high = mixing[0:32].astype(bf16).astype(f32)
    low = mixing[0:32] - high
    info = [
        jnp.concatenate([high[4 * q:4 * q + 4], low[4 * q:4 * q + 4], jnp.zeros((8, 128), f32)], axis=0)
        for q in range(8)
    ]
    sent_ref[0:ROWS, :] = second.astype(bf16)
    sent_ref[ROWS:WIDE, :] = jnp.concatenate(info, axis=1).astype(bf16)


def norm_backward(grad, values, gain):
    inverse = lax.rsqrt(jnp.mean(values * values, axis=1, keepdims=True) + epsilon)
    scaled = grad * gain
    gain_grad = jnp.sum(grad * values * inverse, axis=0, keepdims=True)
    dot = jnp.mean(scaled * values, axis=1, keepdims=True)
    return inverse * (scaled - values * (inverse * inverse * dot)), gain_grad


def attend_back_kernel(
    place_ref, b0, b1, b2, b3, cot_ref, after_ref, gates_ref, small_ref,
    mine_ref, own_ref, sib_ref, q_ref, kv_ref, table_ref,
    mine_out, other_out, after_grad_ref, tiny_ref,
    low_buf, sum_buf, grad_buf, all_buf, own_buf, sib_buf, sem,
):
    x_at, first_at, second_at, core = (place_ref[i] for i in (1, 2, 3, 4))
    loads = [
        pltpu.make_async_copy(own_ref.at[:, D:SMALL_AT], own_buf, sem.at[0]),
        pltpu.make_async_copy(sib_ref.at[:, D:SMALL_AT], sib_buf, sem.at[1]),
    ]
    for copy in loads:
        copy.start()
    back = b0[...].astype(f32) + b1[...].astype(f32) + b2[...].astype(f32) + b3[...].astype(f32)
    extra = back[ROWS:WIDE]
    dots = extra[0:4] + extra[4:8]
    dots = jnp.concatenate([dots[:, q * 128:(q + 1) * 128] for q in range(8)], axis=0)
    dots = jnp.concatenate([dots, jnp.zeros((96, ROWS), f32)], axis=0).T[:, 0:32]
    valid, gates = table_ref[:, 288:289], gates_ref[...]
    gate_grad = dots * valid
    logit_grad = gates * (gate_grad - jnp.sum(gates * gate_grad, axis=1, keepdims=True))
    after = after_ref[...]
    gain = small_ref[33:34, :]
    inverse = lax.rsqrt(jnp.mean(after * after, axis=1, keepdims=True) + epsilon)
    second = after * inverse * gain
    wide_grad = jnp.concatenate([logit_grad, jnp.zeros((ROWS, 96), f32)], axis=1)
    tiny_ref[0:32, :] = jnp.dot(
        wide_grad.T, second, precision=highest, preferred_element_type=f32
    )[0:32]
    second_grad = back[0:ROWS] + jnp.dot(
        logit_grad, small_ref[0:32, :], precision=highest, preferred_element_type=f32
    )
    norm_grad, gain_grad = norm_backward(second_grad, after, gain)
    tiny_ref[32:40, :] = jnp.concatenate(
        [jnp.zeros((1, D), f32), gain_grad, jnp.zeros((6, D), f32)], axis=0
    )
    after_grad = cot_ref[...].astype(f32) + norm_grad
    after_grad_ref[...] = after_grad
    low_buf[...] = (valid * after_grad).astype(bf16)
    own_at = pl.multiple_of(core * 512, 512)
    sib_at = pl.multiple_of((1 - core) * 512, 512)
    own = low_buf[:, pl.ds(own_at, 512)]
    other = low_buf[:, pl.ds(sib_at, 512)]
    for copy in loads:
        copy.wait()
    lanes = blocks_behind(x_at, 256)
    for k in range(4):
        if k == 0:
            got = nt(own, mine_ref[:, pl.ds(own_at, 512)]) + nt(other, mine_ref[:, pl.ds(sib_at, 512)])
        else:
            span = slice((k - 1) * 256, k * 256)
            got = nt(own, own_buf[span, :]) + nt(other, sib_buf[span, :])
        grad_buf[:, pl.ds(lanes[k], 256)] = got.astype(bf16)
    allowed = allowed_pairs(table_ref)
    cosine, sine = table_ref[:, 0:128], table_ref[:, 128:256]
    scale = HEAD_SIZE ** (-0.5)
    for h in range(KEY_VALUE_HEADS):
        query, key, value, probs = head_scores(q_ref, kv_ref, allowed, h)
        chunk = grad_buf[:, h * 128:(h + 1) * 128]
        grad = jnp.concatenate([chunk[:, 0:64], chunk[:, 64:128]], axis=0)
        prob_grad = nt(grad, value)
        score_grad = (
            probs * (prob_grad - jnp.sum(probs * prob_grad, axis=1, keepdims=True))
        ).astype(bf16)
        value_grad = tn(probs.astype(bf16), grad)
        query_grad = nn(score_grad, key) * scale
        key_grad = tn(score_grad, query) * scale
        sum_buf[:, h * 128:(h + 1) * 128] = jnp.concatenate(
            [query_grad[0:ROWS], query_grad[ROWS:2 * ROWS]], axis=1
        )
        sum_buf[:, D + h * 64:D + (h + 1) * 64] = key_grad
        all_buf[:, D + KV + h * 64:D + KV + (h + 1) * 64] = value_grad.astype(bf16)
    for c in range(12):
        v = sum_buf[:, c * 128:(c + 1) * 128]
        all_buf[:, c * 128:(c + 1) * 128] = (v * cosine - swapped_halves(v) * sine).astype(bf16)
    for f in range(4):
        at = (first_at + f) % 4
        mine_out[f, :, 0:256] = all_buf[:, pl.ds(pl.multiple_of(core * D + at * 256, 256), 256)]
        mine_out[f, :, 256:384] = low_buf[:, pl.ds(pl.multiple_of(core * 512 + at * 128, 128), 128)]
        at = (second_at + f) % 4
        other_out[f, :, 0:256] = all_buf[:, pl.ds(pl.multiple_of((1 - core) * D + at * 256, 256), 256)]
        other_out[f, :, 256:384] = low_buf[
            :, pl.ds(pl.multiple_of((1 - core) * 512 + at * 128, 128), 128)
        ]


def input_back_kernel(
    place_ref, mine_grad, other_grad, mine_ref, own_ref, sib_ref, x_ref, after_grad_ref, small_ref,
    tiny_in,
    input_grad_ref, tiny_ref,
    own_buf, other_buf, grad_buf, own_rest, sib_rest, sem,
):
    x_at, first_at, second_at, core = (place_ref[i] for i in (1, 2, 3, 4))
    loads = [
        pltpu.make_async_copy(own_ref.at[:, 0:D], own_rest, sem.at[0]),
        pltpu.make_async_copy(sib_ref.at[:, 0:D], sib_rest, sem.at[1]),
    ]
    for copy in loads:
        copy.start()
    for f in range(4):
        at = pl.multiple_of(((first_at + f) % 4) * 256, 256)
        own_buf[:, pl.ds(at, 256)] = mine_grad[f, :, 0:256]
        at = pl.multiple_of(((second_at + f) % 4) * 256, 256)
        other_buf[:, pl.ds(at, 256)] = other_grad[f, :, 0:256]
    own, other = own_buf[...], other_buf[...]
    own_at = pl.multiple_of(core * D, D)
    sib_at = pl.multiple_of((1 - core) * D, D)
    lanes = blocks_behind(x_at, 256)
    for copy in loads:
        copy.wait()
    for k in range(4):
        if k == 0:
            got = nt(own, mine_ref[:, pl.ds(own_at, D)]) + nt(other, mine_ref[:, pl.ds(sib_at, D)])
        else:
            span = slice((k - 1) * 256, k * 256)
            got = nt(own, own_rest[span, :]) + nt(other, sib_rest[span, :])
        grad_buf[:, pl.ds(lanes[k], 256)] = got
    norm_grad, gain_grad = norm_backward(
        grad_buf[...], x_ref[...].astype(f32), small_ref[32:33, :]
    )
    input_grad_ref[...] = after_grad_ref[...] + norm_grad
    tiny_ref[0:32, :] = tiny_in[0:32, :]
    tiny_ref[32:40, :] = jnp.concatenate([gain_grad, tiny_in[33:40, :]], axis=0)


def norm_line_kernel(place_ref, own, sib, r1, r2, r3, small_ref, out_ref):
    gain = small_ref[32:33, :]
    lanes = blocks_behind(place_ref[1], 256)
    at = 0
    for ref, begin in ((own, 0), (sib, 0), (r1, ROWS), (r2, ROWS), (r3, ROWS)):
        for row in range(begin, ref.shape[0], ROWS):
            x = ref[row:row + ROWS, :].astype(f32)
            inverse = lax.rsqrt(jnp.mean(x * x, axis=1, keepdims=True) + epsilon)
            out_ref[at:at + ROWS, :] = (x * inverse * gain).astype(bf16)
            at += ROWS
    pieces = [out_ref[:, pl.ds(lane, 256)] for lane in lanes]
    for k in range(4):
        out_ref[:, k * 256:(k + 1) * 256] = pieces[k]


def attention_weights_kernel(
    place_ref, n_ref, a0, a1, a2, a3, a4, g0, g1, g2, g3, g4, tiny_ref,
    o0, o1, o2, o3,
    sum_buf, tiny_buf,
):
    x_at, second_at = place_ref[1], place_ref[3]
    grads = [g0[0], g1[0], g2[...], g3[...], g4[...]]
    out_sum = in_sum = None
    at = 0
    for ref, grad in zip((a0, a1, a2, a3, a4), grads):
        one = tn(ref[...], grad[:, 256:384])
        two = tn(n_ref[at:at + ref.shape[0], :], grad[:, 0:256])
        out_sum = one if out_sum is None else out_sum + one
        in_sum = two if in_sum is None else in_sum + two
        at += ref.shape[0]
    sum_buf[:, 0:256] = in_sum
    sum_buf[:, 256:384] = out_sum
    tiny_buf[0:40, :] = tiny_ref[...]
    tiny_buf[40:128, :] = jnp.zeros((88, D), f32)
    for k, lane in enumerate(blocks_behind(x_at, 256)):
        sum_buf[k * 256:(k + 1) * 256, 384:512] = tiny_buf[:, pl.ds(lane, 256)].T
    for s, out in enumerate((o0, o1, o2, o3)):
        at = (second_at + s) % 4
        for k in range(4):
            out[k] = sum_buf[pl.ds(pl.multiple_of(k * 256 + at * 64, 64), 64), :].astype(bf16)


def run_local(kernel, name, place, operands, outs, scratch, fetched=()):
    vmem = pl.BlockSpec(memory_space=pltpu.VMEM)
    apart = pl.BlockSpec(memory_space=pl.ANY)
    return pl.pallas_call(
        kernel,
        in_specs=[pl.BlockSpec(memory_space=pltpu.SMEM)]
        + [apart if i in fetched else vmem for i in range(len(operands))],
        out_specs=[vmem] * len(outs),
        out_shape=[jax.ShapeDtypeStruct(shape, kind) for shape, kind in outs],
        scratch_shapes=[pltpu.VMEM(shape, kind) for shape, kind in scratch]
        + ([pltpu.SemaphoreType.DMA((3,))] if fetched else []),
        compiler_params=pltpu.CompilerParams(vmem_limit_bytes=60 * 1024 * 1024),
        cost_estimate=SHORT,
        name=name,
    )(place, *operands)


def block_at(v, index, size, axis):
    return lax.dynamic_slice_in_dim(v, index * size, size, axis)


def behind(v, at, size, axis):
    return [block_at(v, (at + 4 - k) % 4, size, axis) for k in range(4)]


def in_place(blocks, at, axis):
    stack = jnp.stack(blocks)
    return jnp.concatenate(
        [lax.dynamic_index_in_dim(stack, (at + 4 - a) % 4, 0, keepdims=False) for a in range(4)],
        axis=axis,
    )


def per_device(
    hidden_in,
    segment_ids,
    token_counts,
    expert_ids,
    norm_one,
    qkv_weight,
    out_weight,
    norm_two,
    router_weight,
    gate_weight,
    up_weight,
    down_weight,
    cotangent,
):
    x_at = lax.axis_index("x")
    y_at = lax.axis_index("y")
    z_at = lax.axis_index("z")
    core = lax.axis_index("core")
    first_at = jnp.where(core == 0, y_at, z_at)
    second_at = jnp.where(core == 0, z_at, y_at)
    place = jnp.stack([(y_at * 4 + z_at) * 2 + core, x_at, first_at, second_at, core]).astype(jnp.int32)

    grad_low = cotangent.reshape(ROWS, D)
    inputs = hidden_in.reshape(ROWS, D)
    valid = (
        (jnp.arange(TOK_MB, dtype=jnp.int32)[None, :] < token_counts).reshape(ROWS, 1).astype(f32)
    )
    segment_key = (
        segment_ids + (TOK_MB + 1) * jnp.arange(MICRO, dtype=jnp.int32)[:, None]
    ).reshape(ROWS)
    column, row = segment_key[:, None], segment_key[None, :]
    places = jnp.arange(ROWS)
    allowed = (column == row) & (places[:, None] >= places[None, :])
    position = jnp.sum(allowed.astype(f32), axis=1) - 1.0
    frequency = 10000.0 ** (-2.0 * jnp.arange(HEAD_SIZE // 2, dtype=f32) / HEAD_SIZE)
    angles = position[:, None] * frequency[None, :]
    cosine, sine = jnp.cos(angles), jnp.sin(angles)
    routes = expert_ids.reshape(ROWS, TOPK)
    member = jnp.any(
        routes[:, :, None] == jnp.arange(EXPERTS, dtype=jnp.int32)[None, None, :], axis=1
    ).astype(f32)
    table = jnp.concatenate(
        [cosine] * 4 + [-sine, sine, -sine, sine]
        + [member, valid, column.astype(f32), jnp.zeros((ROWS, 94), f32)],
        axis=1,
    )

    small = jnp.concatenate(
        [router_weight, norm_one[:, None], norm_two[:, None], jnp.zeros((256, 94), bf16)], axis=1
    )
    packed = jnp.concatenate(
        [block_at(qkv_weight, core, D, 1), block_at(out_weight, core, FFE, 1), small], axis=1
    )
    inputs_sib = swap_core(inputs)
    rows_pack = jnp.concatenate([grad_low, inputs, inputs_sib], axis=0)
    hidden_lines = spread_first(rows_pack)
    grad_rows = jnp.stack([grad_low] + [v[:ROWS] for v in hidden_lines])
    back, ahead, hidden_lines, grad_rows, table = stage(
        along_x(packed, 1), along_x(packed, -1), hidden_lines, grad_rows, table
    )
    low, high = along_x(back[:128], 1), along_x(ahead[128:], -1)
    low, high, grad_back, grad_ahead = stage(
        low, high, along_second(grad_rows, 1), along_second(grad_rows, -1)
    )
    full_own = jnp.concatenate([back, low, high, ahead], axis=0)
    full_sib = swap_core(full_own)
    half = (ROWS, D)
    rest = ((768, 512), bf16)
    rest_wide = ((768, D), bf16)
    query, kv, small_full = run_local(
        project_kernel, "project", place,
        [inputs, qkv_weight, full_own, full_sib, small, table],
        [(half, bf16), (half, bf16), ((40, D), f32)],
        [(half, bf16), ((ROWS, 2 * D), f32), ((128, D), f32), ((768, 128), bf16), rest_wide, rest_wide],
        fetched=(2, 3),
    )
    attended = run_local(
        attend_kernel, "attend", place,
        [inputs, query, kv, small_full, out_weight, full_own, full_sib, table],
        [(half, bf16), (half, f32), ((ROWS, EXPERTS), f32), ((WIDE, D), bf16)],
        [(half, bf16), (half, f32), rest, rest],
        fetched=(5, 6),
    )
    attended, grad_two, rows_sib, back_sib, ahead_sib = stage(
        attended, along_second(grad_rows, 2),
        swap_core(grad_rows), swap_core(grad_back), swap_core(grad_ahead),
    )
    grads = {0: [grad_rows, rows_sib], 1: [grad_back, back_sib], 3: [grad_ahead, ahead_sib]}
    line, after, gates, sent = attended

    def visit(j, *rows):
        return run_experts(
            place, list(rows), grads[j], gate_weight[0], up_weight[0], down_weight[0]
        )

    got, line_other, two_sib = stage(spread_first(sent), swap_core(line), swap_core(grad_two))
    grads[2] = [grad_two, two_sib]
    rows = jnp.stack([sent] + got)
    parts = {}
    parts[0], back, ahead = stage(
        visit(0, rows, swap_core(rows)), along_second(rows, 1), along_second(rows, -1)
    )
    parts[1], two, ahead_sib = stage(
        visit(1, back, swap_core(back)), along_second(rows, 2), swap_core(ahead)
    )
    pair = jnp.concatenate([line, line_other], axis=0)
    parts[3], two_sib, turn_back, lines = stage(
        visit(3, ahead, ahead_sib), swap_core(two), swap_core(parts[1][1]), spread_first(pair)
    )
    merged_back = add(parts[1][0], turn_back).astype(bf16)
    normed_line, = run_local(
        norm_line_kernel, "norm_line", place,
        [inputs, inputs_sib, *hidden_lines, small_full], [((8 * ROWS, D), bf16)], [],
    )
    normed_line, merged_back, turn_ahead = stage(normed_line, merged_back, swap_core(parts[3][1]))
    merged_ahead = add(parts[3][0], turn_ahead).astype(bf16)
    parts[2], got_back, got_ahead, turn_own = stage(
        visit(2, two, two_sib), along_second(merged_back, -1), along_second(merged_ahead, -3),
        swap_core(parts[0][1]),
    )
    merged = add(parts[2][0], swap_core(parts[2][1])).astype(bf16)
    saved = [parts[j][4:9] for j in range(4)]
    merged, first_rows = stage(merged, saved[0][0])
    saved[0] = [first_rows] + list(saved[0][1:])
    chunks, got_two = stage(run_weight_grads(saved), along_second(merged, -2))
    expert_sums = [lax.psum(v, "x") for v in chunks]
    total = add(parts[0][0], turn_own, got_back, got_ahead, got_two).astype(bf16)
    arrived, turn_back, turn_ahead = stage(
        [along_first(total[i], -i) for i in (1, 2, 3)],
        swap_core(parts[1][3]), swap_core(parts[3][3]),
    )
    back = [total[0]] + arrived
    merged_back = add(parts[1][2], turn_back).astype(bf16)
    merged_ahead = add(parts[3][2], turn_ahead).astype(bf16)
    mine_grad, other_grad, after_grad, tiny = run_local(
        attend_back_kernel, "attend_back", place,
        back + [
            grad_low, after, gates, small_full, out_weight, full_own, full_sib, query, kv, table,
        ],
        [((4, ROWS, 384), bf16), ((4, ROWS, 384), bf16), (half, f32), ((40, D), f32)],
        [(half, bf16), ((ROWS, 3 * KV), f32), (half, bf16), ((ROWS, 2 * D), bf16), rest, rest],
        fetched=(9, 10),
    )
    input_grad, tiny = run_local(
        input_back_kernel, "input_back", place,
        [mine_grad, other_grad, qkv_weight, full_own, full_sib, inputs, after_grad, small_full, tiny],
        [(half, f32), ((40, D), f32)],
        [(half, bf16), (half, bf16), (half, f32), rest_wide, rest_wide],
        fetched=(3, 4),
    )
    input_grad, tiny, mine_grad, sib_grad, turn_two, turn_own, got_back, got_ahead = stage(
        input_grad, tiny, mine_grad, swap_core(other_grad),
        swap_core(parts[2][3]), swap_core(parts[0][3]),
        along_second(merged_back, -1), along_second(merged_ahead, -3),
    )

    line_grad = [
        along_first(jnp.concatenate([mine_grad[k], sib_grad[k]], axis=0), k) for k in (1, 2, 3)
    ]
    merged = add(parts[2][2], turn_two).astype(bf16)
    line_grad, merged = stage(line_grad, merged)
    chunk = run_local(
        attention_weights_kernel, "attention_weights", place,
        [normed_line, line, line_other, *lines, mine_grad, sib_grad, *line_grad, tiny],
        [((4, 64, 512), bf16)] * 4,
        [((D, 512), f32), ((128, D), f32)],
    )
    chunk, got = stage(chunk, [along_second(chunk[s], s) for s in (1, 2, 3)])
    total = add(chunk[0], *got).astype(bf16)
    total, got, got_two, expert_sums = stage(
        total, [along_x(total[k], -k) for k in (1, 2, 3)], along_second(merged, -2), expert_sums
    )
    shard = add(total[0], *got).astype(bf16)
    total = add(parts[0][2], turn_own, got_back, got_ahead, got_two).astype(bf16)
    shard, got, total, arrived = stage(
        shard, [along_second(shard, k) for k in (1, 2, 3)],
        total, [along_first(total[i], -i) for i in (1, 2, 3)],
    )
    output = (after + add(total[0], *arrived)).astype(bf16).reshape(MICRO, TOK_MB, D)
    shard = in_place([shard] + got, second_at, 0)
    expert_sums = [v.astype(f32)[None] for v in expert_sums]
    shard, got, expert_sums, output = stage(shard, spread_first(shard), expert_sums, output)
    shard = [shard] + got
    both = jnp.concatenate(
        [
            in_place([v[:, :256] for v in shard], first_at, 1),
            in_place([v[:, 256:384] for v in shard], first_at, 1),
            add(*[v[:, 384:] for v in shard]).astype(bf16),
        ],
        axis=1,
    )
    other = swap_core(both)
    tiny = both[:, SMALL_AT:].astype(f32) + other[:, SMALL_AT:].astype(f32)

    def join_half(own, other):
        return jnp.where(
            core == 0,
            jnp.concatenate([own, other], axis=1),
            jnp.concatenate([other, own], axis=1),
        ).astype(f32)

    return (
        output,
        input_grad.reshape(MICRO, TOK_MB, D),
        tiny[:, 32],
        join_half(both[:, :D], other[:, :D]),
        join_half(both[:, D:SMALL_AT], other[:, D:SMALL_AT]),
        tiny[:, 33],
        tiny[:, 0:32],
        expert_sums[0],
        expert_sums[1],
        expert_sums[2],
    )


def solution(mesh):
    grid = Mesh(mesh.devices.reshape(4, 4, 4, 2), ("x", "y", "z", "core"))
    every = ("x", "y", "z", "core")
    plane = ("y", "z", "core")
    return jax.shard_map(
        per_device,
        mesh=grid,
        in_specs=(
            P(None, every, None),
            P(None, every),
            P(None, every),
            P(None, every, None),
            P("x"),
            P("x", None),
            P("x", None),
            P("x"),
            P("x", None),
            P(plane, None, None),
            P(plane, None, None),
            P(plane, None, None),
            P(None, every, None),
        ),
        out_specs=(
            P(None, every, None),
            P(None, every, None),
            P("x"),
            P("x", None),
            P("x", None),
            P("x"),
            P("x", None),
            P(plane, None, None),
            P(plane, None, None),
            P(plane, None, None),
        ),
        check_vma=False,
    )
```

```python
import functools

import jax
import jax.numpy as jnp
from jax import lax
from jax.experimental import pallas as pl
from jax.experimental.pallas import tpu as pltpu
from jax.sharding import Mesh
from jax.sharding import PartitionSpec as P

D = 1024
QUERY_HEADS = 16
KEY_VALUE_HEADS = 8
HEAD_SIZE = 64
FFE = 512
TOPK = 8
MICRO = 2
TOK_MB = 64
EXPERTS = 32
CAP = 24
ROWS = MICRO * TOK_MB
SLOTS = MICRO * CAP
EXTRA = 16
WIDE = ROWS + EXTRA
KV = KEY_VALUE_HEADS * HEAD_SIZE
SMALL_AT = D + D // 2
SHORT = pl.CostEstimate(flops=1_000_000, bytes_accessed=100_000, transcendentals=0)

epsilon = 1e-06
highest = lax.Precision.HIGHEST
f32 = jnp.float32
bf16 = jnp.bfloat16


def plane_pairs(first, second, swap):
    pairs = []
    for y in range(4):
        for z in range(4):
            for c in range(2):
                dy, dz = (first, second) if c == 0 else (second, first)
                target = (((y + dy) % 4) * 4 + (z + dz) % 4) * 2 + (c ^ swap)
                pairs.append(((y * 4 + z) * 2 + c, target))
    return pairs


def along_first(v, k):
    return lax.ppermute(v, ("y", "z", "core"), plane_pairs(k % 4, 0, 0))


def along_second(v, k):
    return lax.ppermute(v, ("y", "z", "core"), plane_pairs(0, k % 4, 0))


def swap_core(v):
    return lax.ppermute(v, "core", [(0, 1), (1, 0)])


def along_x(v, k):
    return lax.ppermute(v, "x", [(i, (i + k) % 4) for i in range(4)])


def stage(*values):
    return lax.optimization_barrier(values)


def spread_first(v):
    return [along_first(v, k) for k in (1, 2, 3)]


def add(first, *others):
    total = first.astype(f32)
    for v in others:
        total = total + v.astype(f32)
    return total


def nt(a, b):
    return lax.dot_general(a, b, (((1,), (1,)), ((), ())), preferred_element_type=f32)


def tn(a, b):
    return lax.dot_general(a, b, (((0,), (0,)), ((), ())), preferred_element_type=f32)


def nn(a, b):
    return jnp.dot(a, b, preferred_element_type=f32)


BLOCKS = 8
PACKED = BLOCKS * SLOTS


def expert_kernel(n_rows, n_grads, place_ref, *refs):
    row_refs, refs = refs[:n_rows], refs[n_rows:]
    grad_refs, refs = refs[:n_grads], refs[n_grads:]
    gate_ref, up_ref, down_ref = refs[:3]
    back_refs, out_refs, save_refs = refs[3:5], refs[5:7], refs[7:12]
    (row_buf, grad_buf, back_buf, out_buf, x_buf, c_buf, r_buf, s_buf, h_buf, g_buf, u_buf,
     mix_buf, pick_buf, dot_buf, gate_buf, up_buf, down_buf,
     row_sem, grad_sem, back_sem, out_sem, save_sem, weight_sem) = refs[12:]

    def pieces(sources, buf, sem):
        copies = []
        for ref in sources:
            for b in range(ref.shape[0]):
                at = len(copies)
                copies.append(pltpu.make_async_copy(ref.at[b], buf.at[at], sem.at[at]))
        return copies

    row_loads = pieces(row_refs, row_buf, row_sem)
    grad_loads = pieces(grad_refs, grad_buf, grad_sem)
    weight_loads = [
        pltpu.make_async_copy(ref, buf, weight_sem.at[i])
        for i, (ref, buf) in enumerate(
            zip((gate_ref, up_ref, down_ref), (gate_buf, up_buf, down_buf))
        )
    ]
    for one, two in zip(row_loads, grad_loads):
        one.start()
        two.start()
    for copy in weight_loads:
        copy.start()

    expert = place_ref[0]
    row_at = expert % 4
    lane_at = pl.multiple_of((expert // 4) * 128, 128)
    upper = (
        lax.broadcasted_iota(jnp.int32, (ROWS, ROWS), 0)
        < lax.broadcasted_iota(jnp.int32, (ROWS, ROWS), 1)
    ).astype(bf16)
    extra_row = lax.broadcasted_iota(jnp.int32, (EXTRA, 128), 0)
    slot_row = lax.broadcasted_iota(jnp.int32, (SLOTS, ROWS), 0).astype(f32)

    @pl.loop(0, BLOCKS)
    def _(b):
        pltpu.make_async_copy(row_refs[0].at[0], row_buf.at[b], row_sem.at[b]).wait()
        pltpu.make_async_copy(grad_refs[0].at[0], grad_buf.at[b], grad_sem.at[b]).wait()
        info = row_buf[b, ROWS:WIDE, pl.ds(lane_at, 128)].astype(f32)
        high = jnp.sum(jnp.where(extra_row == row_at, info, 0.0), axis=0, keepdims=True)
        low = jnp.sum(jnp.where(extra_row == row_at + 4, info, 0.0), axis=0, keepdims=True)
        chosen = high > 0.0
        flags = jnp.broadcast_to(chosen.astype(f32), (16, ROWS)).astype(bf16)
        rank = nn(flags, upper)[0:1]
        pick = jnp.where((slot_row == rank) & chosen, 1.0, 0.0)
        weight = jnp.sum(pick * (high + low), axis=1, keepdims=True)
        low_pick = pick.astype(bf16)
        pick_buf[b] = low_pick
        span = pl.ds(pl.multiple_of(b * SLOTS, SLOTS), SLOTS)
        mix_buf[span, :] = jnp.broadcast_to(weight, (SLOTS, 128))
        x_buf[span, :] = nn(low_pick, row_buf[b, 0:ROWS, :]).astype(bf16)
        c_buf[span, :] = nn(low_pick, grad_buf[b]).astype(bf16)

    saves = [
        pltpu.make_async_copy(buf, ref, save_sem.at[i])
        for i, (buf, ref) in enumerate(zip((x_buf, s_buf, h_buf, g_buf, u_buf), save_refs))
    ]
    saves[0].start()
    mixing = mix_buf[:, 0:1]
    grads = c_buf[...].astype(f32)
    s_buf[...] = (mixing * grads).astype(bf16)
    saves[1].start()
    for copy in weight_loads:
        copy.wait()
    gate_pre = nn(x_buf[...], gate_buf[...])
    up_pre = nn(x_buf[...], up_buf[...])
    sigma = 1.0 / (1.0 + jnp.exp(-gate_pre))
    swish = gate_pre * sigma
    h_buf[...] = (swish * up_pre).astype(bf16)
    saves[2].start()
    hidden_grad = nt(s_buf[...], down_buf[...])
    slope = sigma * (1.0 + gate_pre * (1.0 - sigma))
    g_buf[...] = (hidden_grad * up_pre * slope).astype(bf16)
    u_buf[...] = (hidden_grad * swish).astype(bf16)
    saves[3].start()
    saves[4].start()
    r_buf[...] = (nt(g_buf[...], gate_buf[...]) + nt(u_buf[...], up_buf[...])).astype(bf16)
    produced = nn(h_buf[...], down_buf[...]).astype(bf16).astype(f32)
    gate_grad = jnp.sum(produced * c_buf[...].astype(f32), axis=1, keepdims=True)
    dot_buf[...] = jnp.broadcast_to(gate_grad, (PACKED, 128))
    c_buf[...] = (mixing * produced).astype(bf16)

    @pl.loop(0, BLOCKS)
    def _(b):
        low_pick = pick_buf[b]
        span = pl.ds(pl.multiple_of(b * SLOTS, SLOTS), SLOTS)
        back_buf[b, 0:ROWS, :] = tn(low_pick, r_buf[span, :]).astype(bf16)
        out_buf[b] = tn(low_pick, c_buf[span, :]).astype(bf16)
        back_buf[b, ROWS:WIDE, :] = jnp.zeros((EXTRA, D), bf16)
        dots = jnp.sum(low_pick.astype(f32) * dot_buf[span, :], axis=0, keepdims=True)
        high = dots.astype(bf16).astype(f32)
        info = jnp.where(extra_row == row_at, high, 0.0)
        info = info + jnp.where(extra_row == row_at + 4, dots - high, 0.0)
        back_buf[b, ROWS:WIDE, pl.ds(lane_at, 128)] = info.astype(bf16)
        for side in range(2):
            @pl.when(b // 4 == side)
            def _():
                at = b - 4 * side
                pltpu.make_async_copy(back_buf.at[b], back_refs[side].at[at], back_sem.at[b]).start()
                pltpu.make_async_copy(out_buf.at[b], out_refs[side].at[at], out_sem.at[b]).start()

    for b in range(BLOCKS):
        side, at = b // 4, b % 4
        pltpu.make_async_copy(back_buf.at[b], back_refs[side].at[at], back_sem.at[b]).wait()
        pltpu.make_async_copy(out_buf.at[b], out_refs[side].at[at], out_sem.at[b]).wait()
    for copy in saves:
        copy.wait()


def run_experts(place, rows, grads, gate, up, down):
    any_space = pl.BlockSpec(memory_space=pl.ANY)
    wide = jax.ShapeDtypeStruct((4, WIDE, D), bf16)
    flat = jax.ShapeDtypeStruct((4, ROWS, D), bf16)
    full = jax.ShapeDtypeStruct((PACKED, D), bf16)
    half = jax.ShapeDtypeStruct((PACKED, FFE), bf16)
    return pl.pallas_call(
        functools.partial(expert_kernel, len(rows), len(grads)),
        in_specs=[pl.BlockSpec(memory_space=pltpu.SMEM)]
        + [any_space] * (len(rows) + len(grads) + 3),
        out_specs=[any_space] * 9,
        out_shape=[wide, wide, flat, flat, full, full, half, half, half],
        scratch_shapes=[
            pltpu.VMEM((BLOCKS, WIDE, D), bf16),
            pltpu.VMEM((BLOCKS, ROWS, D), bf16),
            pltpu.VMEM((BLOCKS, WIDE, D), bf16),
            pltpu.VMEM((BLOCKS, ROWS, D), bf16),
            pltpu.VMEM((PACKED, D), bf16),
            pltpu.VMEM((PACKED, D), bf16),
            pltpu.VMEM((PACKED, D), bf16),
            pltpu.VMEM((PACKED, D), bf16),
            pltpu.VMEM((PACKED, FFE), bf16),
            pltpu.VMEM((PACKED, FFE), bf16),
            pltpu.VMEM((PACKED, FFE), bf16),
            pltpu.VMEM((PACKED, 128), f32),
            pltpu.VMEM((BLOCKS, SLOTS, ROWS), bf16),
            pltpu.VMEM((PACKED, 128), f32),
            pltpu.VMEM((D, FFE), bf16),
            pltpu.VMEM((D, FFE), bf16),
            pltpu.VMEM((FFE, D), bf16),
            pltpu.SemaphoreType.DMA((BLOCKS,)),
            pltpu.SemaphoreType.DMA((BLOCKS,)),
            pltpu.SemaphoreType.DMA((BLOCKS,)),
            pltpu.SemaphoreType.DMA((BLOCKS,)),
            pltpu.SemaphoreType.DMA((5,)),
            pltpu.SemaphoreType.DMA((3,)),
        ],
        compiler_params=pltpu.CompilerParams(vmem_limit_bytes=60 * 1024 * 1024),
        cost_estimate=SHORT,
        name="experts",
    )(place, *rows, *grads, gate, up, down)


def weight_grad_kernel(*refs):
    xs, ss, hs, gs, us = (refs[4 * i:4 * i + 4] for i in range(5))
    out_ref = refs[20]
    x_buf, s_buf, h_buf, g_buf, u_buf, out_buf, in_sem, out_sem = refs[21:]
    loads = []
    for j in range(4):
        for i, (sources, buf) in enumerate(
            zip((xs, gs, us, hs, ss), (x_buf, g_buf, u_buf, h_buf, s_buf))
        ):
            loads.append(pltpu.make_async_copy(sources[j], buf.at[j], in_sem.at[j, i]))
    for copy in loads:
        copy.start()
    for copy in loads:
        copy.wait()

    @pl.loop(0, 4)
    def _(k):
        wide_at = pl.multiple_of(k * 256, 256)
        thin_at = pl.multiple_of(k * 128, 128)
        rows = x_buf[:, :, pl.ds(wide_at, 256)].reshape(4 * PACKED, 256)
        thin = h_buf[:, :, pl.ds(thin_at, 128)].reshape(4 * PACKED, 128)
        out_buf[k, 0:256, :] = tn(rows, g_buf[...].reshape(4 * PACKED, FFE)).astype(bf16)
        out_buf[k, 256:512, :] = tn(rows, u_buf[...].reshape(4 * PACKED, FFE)).astype(bf16)
        down = tn(thin, s_buf[...].reshape(4 * PACKED, D)).astype(bf16)
        out_buf[k, 512:640, :] = down[:, 0:FFE]
        out_buf[k, 640:768, :] = down[:, FFE:D]
        pltpu.make_async_copy(out_buf.at[k], out_ref.at[k], out_sem.at[k]).start()

    for k in range(4):
        pltpu.make_async_copy(out_buf.at[k], out_ref.at[k], out_sem.at[k]).wait()


def run_weight_grads(saved):
    operands = [part[i] for i in range(5) for part in saved]
    any_space = pl.BlockSpec(memory_space=pl.ANY)
    return pl.pallas_call(
        weight_grad_kernel,
        in_specs=[any_space] * 20,
        out_specs=any_space,
        out_shape=jax.ShapeDtypeStruct((4, 768, FFE), bf16),
        scratch_shapes=[
            pltpu.VMEM((4, PACKED, D), bf16),
            pltpu.VMEM((4, PACKED, D), bf16),
            pltpu.VMEM((4, PACKED, FFE), bf16),
            pltpu.VMEM((4, PACKED, FFE), bf16),
            pltpu.VMEM((4, PACKED, FFE), bf16),
            pltpu.VMEM((4, 768, FFE), bf16),
            pltpu.SemaphoreType.DMA((4, 5)),
            pltpu.SemaphoreType.DMA((4,)),
        ],
        compiler_params=pltpu.CompilerParams(vmem_limit_bytes=60 * 1024 * 1024),
        cost_estimate=SHORT,
        name="expert_weight_grads",
    )(*operands)


def blocks_behind(x_at, n):
    return [pl.multiple_of(((x_at + 4 - k) % 4) * n, n) for k in range(4)]


def swapped_halves(v):
    lane = lax.broadcasted_iota(jnp.int32, v.shape, 1)
    return jnp.where(lane % HEAD_SIZE < HEAD_SIZE // 2, pltpu.roll(v, 96, 1), pltpu.roll(v, 32, 1))


def pack_kernel(place_ref, qkv_ref, out_ref, router_ref, one_ref, two_ref, packed_ref, small_ref):
    core = place_ref[4]
    packed_ref[:, 0:D] = qkv_ref[:, pl.ds(pl.multiple_of(core * D, D), D)]
    packed_ref[:, D:SMALL_AT] = out_ref[:, pl.ds(pl.multiple_of(core * 512, 512), 512)]
    gains = [jnp.zeros((32, 256), f32), one_ref[...].astype(f32), two_ref[...].astype(f32)]
    gains = jnp.concatenate(gains + [jnp.zeros((94, 256), f32)], axis=0).T
    router = jnp.concatenate([router_ref[...].astype(f32), jnp.zeros((256, 96), f32)], axis=1)
    small = (router + gains).astype(bf16)
    packed_ref[:, SMALL_AT:SMALL_AT + 128] = small
    small_ref[...] = small


def project_kernel(
    place_ref, x_ref, mine_ref, own_ref, sib_ref, tiny_ref, table_ref,
    q_ref, kv_ref, small_ref,
    norm_buf, all_buf, tiny_buf, small_buf, own_buf, sib_buf, sem,
):
    x_at, core = place_ref[1], place_ref[4]
    lanes = blocks_behind(x_at, 256)
    loads = [
        pltpu.make_async_copy(own_ref.at[:, SMALL_AT:SMALL_AT + 128], small_buf, sem.at[0]),
        pltpu.make_async_copy(own_ref.at[:, 0:D], own_buf, sem.at[1]),
        pltpu.make_async_copy(sib_ref.at[:, 0:D], sib_buf, sem.at[2]),
    ]
    for copy in loads:
        copy.start()
    loads[0].wait()
    for k in range(4):
        piece = tiny_ref[...] if k == 0 else small_buf[(k - 1) * 256:k * 256, :]
        tiny_buf[:, pl.ds(lanes[k], 256)] = piece.astype(f32).T
    small_ref[...] = tiny_buf[0:40, :]
    x = x_ref[...].astype(f32)
    inverse = lax.rsqrt(jnp.mean(x * x, axis=1, keepdims=True) + epsilon)
    norm_buf[...] = (x * inverse * tiny_buf[32:33, :]).astype(bf16)
    rows = [norm_buf[:, pl.ds(at, 256)] for at in lanes]
    own_at = pl.multiple_of(core * D, D)
    sib_at = pl.multiple_of((1 - core) * D, D)
    for at, rest, copy in ((own_at, own_buf, loads[1]), (sib_at, sib_buf, loads[2])):
        total = nn(rows[0], mine_ref[:, pl.ds(at, D)])
        copy.wait()
        for k in (1, 2, 3):
            total = total + nn(rows[k], rest[(k - 1) * 256:k * 256, :])
        all_buf[:, pl.ds(at, D)] = total
    cosine, sine = table_ref[:, 0:128], table_ref[:, 128:256]
    for c in range(12):
        v = all_buf[:, c * 128:(c + 1) * 128]
        turned = (v * cosine + swapped_halves(v) * sine).astype(bf16)
        if c < 8:
            q_ref[:, c * 128:(c + 1) * 128] = turned
        else:
            kv_ref[:, (c - 8) * 128:(c - 7) * 128] = turned
    kv_ref[:, KV:2 * KV] = all_buf[:, D + KV:D + 2 * KV].astype(bf16)


def head_scores(q_ref, kv_ref, allowed, h):
    chunk = q_ref[:, h * 128:(h + 1) * 128]
    query = jnp.concatenate([chunk[:, 0:64], chunk[:, 64:128]], axis=0)
    key = kv_ref[:, h * 64:(h + 1) * 64]
    value = kv_ref[:, KV + h * 64:KV + (h + 1) * 64]
    scores = jnp.where(allowed, nt(query, key) * HEAD_SIZE ** (-0.5), -1e30)
    expo = jnp.exp(scores - jnp.max(scores, axis=1, keepdims=True))
    probs = expo / jnp.sum(expo, axis=1, keepdims=True)
    return query, key, value, probs


def allowed_pairs(table_ref):
    shape = (2 * ROWS, ROWS)
    column = table_ref[:, 289:290]
    row = table_ref[:, 256:384].T[33:34]
    q = lax.broadcasted_iota(jnp.int32, shape, 0) % ROWS
    p = lax.broadcasted_iota(jnp.int32, shape, 1)
    return (jnp.concatenate([column, column], axis=0) == row) & (p <= q)


def attend_kernel(
    place_ref, x_ref, q_ref, kv_ref, small_ref, mine_ref, own_ref, sib_ref,
    table_ref,
    line_ref, after_ref, gates_ref, sent_ref,
    low_buf, out_buf, own_buf, sib_buf, sem,
):
    x_at, core = place_ref[1], place_ref[4]
    loads = [
        pltpu.make_async_copy(own_ref.at[:, D:SMALL_AT], own_buf, sem.at[0]),
        pltpu.make_async_copy(sib_ref.at[:, D:SMALL_AT], sib_buf, sem.at[1]),
    ]
    for copy in loads:
        copy.start()
    allowed = allowed_pairs(table_ref)
    for h in range(KEY_VALUE_HEADS):
        _, _, value, probs = head_scores(q_ref, kv_ref, allowed, h)
        got = nn(probs.astype(bf16), value)
        low_buf[:, h * 128:(h + 1) * 128] = jnp.concatenate(
            [got[0:ROWS], got[ROWS:2 * ROWS]], axis=1
        ).astype(bf16)
    rows = [low_buf[:, pl.ds(at, 256)] for at in blocks_behind(x_at, 256)]
    for k in range(4):
        line_ref[:, k * 256:(k + 1) * 256] = rows[k]
    own_at = pl.multiple_of(core * 512, 512)
    sib_at = pl.multiple_of((1 - core) * 512, 512)
    for copy in loads:
        copy.wait()
    for at, rest in ((own_at, own_buf), (sib_at, sib_buf)):
        total = nn(rows[0], mine_ref[:, pl.ds(at, 512)])
        for k in (1, 2, 3):
            total = total + nn(rows[k], rest[(k - 1) * 256:k * 256, :])
        out_buf[:, pl.ds(at, 512)] = total
    valid = table_ref[:, 288:289]
    after = x_ref[...].astype(f32) + valid * out_buf[...]
    after_ref[...] = after
    inverse = lax.rsqrt(jnp.mean(after * after, axis=1, keepdims=True) + epsilon)
    second = after * inverse * small_ref[33:34, :]
    logits = lax.dot_general(
        second, small_ref[0:32, :], (((1,), (1,)), ((), ())),
        precision=highest, preferred_element_type=f32,
    )
    member = table_ref[:, 256:288] > 0.0
    masked = jnp.where(member, logits, -3e38)
    gates = jnp.where(member, jnp.exp(masked - jnp.max(masked, axis=1, keepdims=True)), 0.0)
    gates = gates / jnp.sum(gates, axis=1, keepdims=True)
    gates_ref[...] = gates
    mixing = jnp.concatenate([gates * valid, jnp.zeros((ROWS, 96), f32)], axis=1).T
    high = mixing[0:32].astype(bf16).astype(f32)
    low = mixing[0:32] - high
    info = [
        jnp.concatenate([high[4 * q:4 * q + 4], low[4 * q:4 * q + 4], jnp.zeros((8, 128), f32)], axis=0)
        for q in range(8)
    ]
    sent_ref[0:ROWS, :] = second.astype(bf16)
    sent_ref[ROWS:WIDE, :] = jnp.concatenate(info, axis=1).astype(bf16)


def norm_backward(grad, values, gain):
    inverse = lax.rsqrt(jnp.mean(values * values, axis=1, keepdims=True) + epsilon)
    scaled = grad * gain
    gain_grad = jnp.sum(grad * values * inverse, axis=0, keepdims=True)
    dot = jnp.mean(scaled * values, axis=1, keepdims=True)
    return inverse * (scaled - values * (inverse * inverse * dot)), gain_grad


def attend_back_kernel(
    place_ref, b0, b1, b2, b3, cot_ref, after_ref, gates_ref, small_ref,
    mine_ref, own_ref, sib_ref, q_ref, kv_ref, table_ref,
    mine_out, other_out, after_grad_ref, tiny_ref,
    low_buf, sum_buf, grad_buf, all_buf, own_buf, sib_buf, sem,
):
    x_at, first_at, second_at, core = (place_ref[i] for i in (1, 2, 3, 4))
    loads = [
        pltpu.make_async_copy(own_ref.at[:, D:SMALL_AT], own_buf, sem.at[0]),
        pltpu.make_async_copy(sib_ref.at[:, D:SMALL_AT], sib_buf, sem.at[1]),
    ]
    for copy in loads:
        copy.start()
    back = b0[...].astype(f32) + b1[...].astype(f32) + b2[...].astype(f32) + b3[...].astype(f32)
    extra = back[ROWS:WIDE]
    dots = extra[0:4] + extra[4:8]
    dots = jnp.concatenate([dots[:, q * 128:(q + 1) * 128] for q in range(8)], axis=0)
    dots = jnp.concatenate([dots, jnp.zeros((96, ROWS), f32)], axis=0).T[:, 0:32]
    valid, gates = table_ref[:, 288:289], gates_ref[...]
    gate_grad = dots * valid
    logit_grad = gates * (gate_grad - jnp.sum(gates * gate_grad, axis=1, keepdims=True))
    after = after_ref[...]
    gain = small_ref[33:34, :]
    inverse = lax.rsqrt(jnp.mean(after * after, axis=1, keepdims=True) + epsilon)
    second = after * inverse * gain
    wide_grad = jnp.concatenate([logit_grad, jnp.zeros((ROWS, 96), f32)], axis=1)
    tiny_ref[0:32, :] = jnp.dot(
        wide_grad.T, second, precision=highest, preferred_element_type=f32
    )[0:32]
    second_grad = back[0:ROWS] + jnp.dot(
        logit_grad, small_ref[0:32, :], precision=highest, preferred_element_type=f32
    )
    norm_grad, gain_grad = norm_backward(second_grad, after, gain)
    tiny_ref[32:40, :] = jnp.concatenate(
        [jnp.zeros((1, D), f32), gain_grad, jnp.zeros((6, D), f32)], axis=0
    )
    after_grad = cot_ref[...].astype(f32) + norm_grad
    after_grad_ref[...] = after_grad
    low_buf[...] = (valid * after_grad).astype(bf16)
    own_at = pl.multiple_of(core * 512, 512)
    sib_at = pl.multiple_of((1 - core) * 512, 512)
    own = low_buf[:, pl.ds(own_at, 512)]
    other = low_buf[:, pl.ds(sib_at, 512)]
    for copy in loads:
        copy.wait()
    lanes = blocks_behind(x_at, 256)
    for k in range(4):
        if k == 0:
            got = nt(own, mine_ref[:, pl.ds(own_at, 512)]) + nt(other, mine_ref[:, pl.ds(sib_at, 512)])
        else:
            span = slice((k - 1) * 256, k * 256)
            got = nt(own, own_buf[span, :]) + nt(other, sib_buf[span, :])
        grad_buf[:, pl.ds(lanes[k], 256)] = got.astype(bf16)
    allowed = allowed_pairs(table_ref)
    cosine, sine = table_ref[:, 0:128], table_ref[:, 128:256]
    scale = HEAD_SIZE ** (-0.5)
    for h in range(KEY_VALUE_HEADS):
        query, key, value, probs = head_scores(q_ref, kv_ref, allowed, h)
        chunk = grad_buf[:, h * 128:(h + 1) * 128]
        grad = jnp.concatenate([chunk[:, 0:64], chunk[:, 64:128]], axis=0)
        prob_grad = nt(grad, value)
        score_grad = (
            probs * (prob_grad - jnp.sum(probs * prob_grad, axis=1, keepdims=True))
        ).astype(bf16)
        value_grad = tn(probs.astype(bf16), grad)
        query_grad = nn(score_grad, key) * scale
        key_grad = tn(score_grad, query) * scale
        sum_buf[:, h * 128:(h + 1) * 128] = jnp.concatenate(
            [query_grad[0:ROWS], query_grad[ROWS:2 * ROWS]], axis=1
        )
        sum_buf[:, D + h * 64:D + (h + 1) * 64] = key_grad
        all_buf[:, D + KV + h * 64:D + KV + (h + 1) * 64] = value_grad.astype(bf16)
    for c in range(12):
        v = sum_buf[:, c * 128:(c + 1) * 128]
        all_buf[:, c * 128:(c + 1) * 128] = (v * cosine - swapped_halves(v) * sine).astype(bf16)
    for f in range(4):
        at = (first_at + f) % 4
        mine_out[f, :, 0:256] = all_buf[:, pl.ds(pl.multiple_of(core * D + at * 256, 256), 256)]
        mine_out[f, :, 256:384] = low_buf[:, pl.ds(pl.multiple_of(core * 512 + at * 128, 128), 128)]
        at = (second_at + f) % 4
        other_out[f, :, 0:256] = all_buf[:, pl.ds(pl.multiple_of((1 - core) * D + at * 256, 256), 256)]
        other_out[f, :, 256:384] = low_buf[
            :, pl.ds(pl.multiple_of((1 - core) * 512 + at * 128, 128), 128)
        ]


def input_back_kernel(
    place_ref, mine_grad, other_grad, mine_ref, own_ref, sib_ref, x_ref, after_grad_ref, small_ref,
    tiny_in,
    input_grad_ref, tiny_ref,
    own_buf, other_buf, grad_buf, own_rest, sib_rest, sem,
):
    x_at, first_at, second_at, core = (place_ref[i] for i in (1, 2, 3, 4))
    loads = [
        pltpu.make_async_copy(own_ref.at[:, 0:D], own_rest, sem.at[0]),
        pltpu.make_async_copy(sib_ref.at[:, 0:D], sib_rest, sem.at[1]),
    ]
    for copy in loads:
        copy.start()
    for f in range(4):
        at = pl.multiple_of(((first_at + f) % 4) * 256, 256)
        own_buf[:, pl.ds(at, 256)] = mine_grad[f, :, 0:256]
        at = pl.multiple_of(((second_at + f) % 4) * 256, 256)
        other_buf[:, pl.ds(at, 256)] = other_grad[f, :, 0:256]
    own, other = own_buf[...], other_buf[...]
    own_at = pl.multiple_of(core * D, D)
    sib_at = pl.multiple_of((1 - core) * D, D)
    lanes = blocks_behind(x_at, 256)
    for copy in loads:
        copy.wait()
    for k in range(4):
        if k == 0:
            got = nt(own, mine_ref[:, pl.ds(own_at, D)]) + nt(other, mine_ref[:, pl.ds(sib_at, D)])
        else:
            span = slice((k - 1) * 256, k * 256)
            got = nt(own, own_rest[span, :]) + nt(other, sib_rest[span, :])
        grad_buf[:, pl.ds(lanes[k], 256)] = got
    norm_grad, gain_grad = norm_backward(
        grad_buf[...], x_ref[...].astype(f32), small_ref[32:33, :]
    )
    input_grad_ref[...] = after_grad_ref[...] + norm_grad
    tiny_ref[0:32, :] = tiny_in[0:32, :]
    tiny_ref[32:40, :] = jnp.concatenate([gain_grad, tiny_in[33:40, :]], axis=0)


def norm_line_kernel(place_ref, r0, r1, r2, r3, small_ref, out_ref):
    gain = small_ref[32:33, :]
    lanes = blocks_behind(place_ref[1], 256)
    at = 0
    for ref in (r0, r1, r2, r3):
        for row in range(0, ref.shape[0], ROWS):
            x = ref[row:row + ROWS, :].astype(f32)
            inverse = lax.rsqrt(jnp.mean(x * x, axis=1, keepdims=True) + epsilon)
            out_ref[at:at + ROWS, :] = (x * inverse * gain).astype(bf16)
            at += ROWS
    pieces = [out_ref[:, pl.ds(lane, 256)] for lane in lanes]
    for k in range(4):
        out_ref[:, k * 256:(k + 1) * 256] = pieces[k]


def attention_weights_kernel(
    place_ref, n_ref, a0, a1, a2, a3, g0, g1, g2, g3, g4, tiny_ref,
    o0, o1, o2, o3,
    sum_buf, tiny_buf,
):
    x_at = place_ref[1]
    grads = [jnp.concatenate([g0[0], g1[0]], axis=0), g2[...], g3[...], g4[...]]
    out_sum = in_sum = None
    at = 0
    for ref, grad in zip((a0, a1, a2, a3), grads):
        one = tn(ref[...], grad[:, 256:384])
        two = tn(n_ref[at:at + ref.shape[0], :], grad[:, 0:256])
        out_sum = one if out_sum is None else out_sum + one
        in_sum = two if in_sum is None else in_sum + two
        at += ref.shape[0]
    sum_buf[:, 0:256] = in_sum
    sum_buf[:, 256:384] = out_sum
    tiny_buf[0:40, :] = tiny_ref[...]
    tiny_buf[40:128, :] = jnp.zeros((88, D), f32)
    for k, lane in enumerate(blocks_behind(x_at, 256)):
        sum_buf[k * 256:(k + 1) * 256, 384:512] = tiny_buf[:, pl.ds(lane, 256)].T
    for k, out in enumerate((o0, o1, o2, o3)):
        out[...] = sum_buf[k * 256:(k + 1) * 256, :].astype(bf16)


def collect_kernel(place_ref, p0, p1, p2, p3, out_ref):
    tiny = None
    for ref, wide, thin in zip(
        (p0, p1, p2, p3), blocks_behind(place_ref[2], 256), blocks_behind(place_ref[2], 128)
    ):
        out_ref[:, pl.ds(wide, 256)] = ref[:, 0:256]
        out_ref[:, pl.ds(pl.multiple_of(D + thin, 128), 128)] = ref[:, 256:384]
        one = ref[:, 384:512].astype(f32)
        tiny = one if tiny is None else tiny + one
    out_ref[:, SMALL_AT:SMALL_AT + 128] = tiny.astype(bf16)


def finish_kernel(place_ref, own_ref, other_ref, qkv_ref, out_ref, router_ref, one_ref, two_ref):
    core = place_ref[4]
    for ref, side in ((own_ref, core), (other_ref, 1 - core)):
        qkv_ref[:, pl.ds(pl.multiple_of(side * D, D), D)] = ref[:, 0:D].astype(f32)
        out_ref[:, pl.ds(pl.multiple_of(side * 512, 512), 512)] = ref[:, D:SMALL_AT].astype(f32)
    tiny = own_ref[:, SMALL_AT:SMALL_AT + 128].astype(f32)
    tiny = tiny + other_ref[:, SMALL_AT:SMALL_AT + 128].astype(f32)
    router_ref[...] = tiny[:, 0:EXPERTS]
    turned = tiny.T
    one_ref[...] = turned[32:33]
    two_ref[...] = turned[33:34]


def widen_kernel(sum_ref, gate_ref, up_ref, down_ref):
    gate_ref[...] = sum_ref[0, 0:256, :].astype(f32)
    up_ref[...] = sum_ref[0, 256:512, :].astype(f32)
    down_ref[:, 0:FFE] = sum_ref[0, 512:640, :].astype(f32)
    down_ref[:, FFE:D] = sum_ref[0, 640:768, :].astype(f32)


def widen(sums):
    return pl.pallas_call(
        widen_kernel,
        grid=(4,),
        in_specs=[pl.BlockSpec((1, 768, FFE), lambda k: (k, 0, 0))],
        out_specs=[
            pl.BlockSpec((256, FFE), lambda k: (k, 0)),
            pl.BlockSpec((256, FFE), lambda k: (k, 0)),
            pl.BlockSpec((128, D), lambda k: (k, 0)),
        ],
        out_shape=[
            jax.ShapeDtypeStruct((D, FFE), f32),
            jax.ShapeDtypeStruct((D, FFE), f32),
            jax.ShapeDtypeStruct((FFE, D), f32),
        ],
        compiler_params=pltpu.CompilerParams(vmem_limit_bytes=60 * 1024 * 1024),
        cost_estimate=SHORT,
        name="widen",
    )(sums)


def run_local(kernel, name, place, operands, outs, scratch, fetched=(), room=60):
    vmem = pl.BlockSpec(memory_space=pltpu.VMEM)
    apart = pl.BlockSpec(memory_space=pl.ANY)
    return pl.pallas_call(
        kernel,
        in_specs=[pl.BlockSpec(memory_space=pltpu.SMEM)]
        + [apart if i in fetched else vmem for i in range(len(operands))],
        out_specs=[vmem] * len(outs),
        out_shape=[jax.ShapeDtypeStruct(shape, kind) for shape, kind in outs],
        scratch_shapes=[pltpu.VMEM(shape, kind) for shape, kind in scratch]
        + ([pltpu.SemaphoreType.DMA((3,))] if fetched else []),
        compiler_params=pltpu.CompilerParams(vmem_limit_bytes=room * 1024 * 1024),
        cost_estimate=SHORT,
        name=name,
    )(place, *operands)


def block_at(v, index, size, axis):
    return lax.dynamic_slice_in_dim(v, index * size, size, axis)


def per_device(
    hidden_in,
    segment_ids,
    token_counts,
    expert_ids,
    norm_one,
    qkv_weight,
    out_weight,
    norm_two,
    router_weight,
    gate_weight,
    up_weight,
    down_weight,
    cotangent,
):
    x_at = lax.axis_index("x")
    y_at = lax.axis_index("y")
    z_at = lax.axis_index("z")
    core = lax.axis_index("core")
    first_at = jnp.where(core == 0, y_at, z_at)
    second_at = jnp.where(core == 0, z_at, y_at)
    place = jnp.stack([(y_at * 4 + z_at) * 2 + core, x_at, first_at, second_at, core]).astype(jnp.int32)

    grad_low = cotangent.reshape(ROWS, D)
    inputs = hidden_in.reshape(ROWS, D)
    valid = (
        (jnp.arange(TOK_MB, dtype=jnp.int32)[None, :] < token_counts).reshape(ROWS, 1).astype(f32)
    )
    segment_key = (
        segment_ids + (TOK_MB + 1) * jnp.arange(MICRO, dtype=jnp.int32)[:, None]
    ).reshape(ROWS)
    column, row = segment_key[:, None], segment_key[None, :]
    places = jnp.arange(ROWS)
    allowed = (column == row) & (places[:, None] >= places[None, :])
    position = jnp.sum(allowed.astype(f32), axis=1) - 1.0
    frequency = 10000.0 ** (-2.0 * jnp.arange(HEAD_SIZE // 2, dtype=f32) / HEAD_SIZE)
    angles = position[:, None] * frequency[None, :]
    cosine, sine = jnp.cos(angles), jnp.sin(angles)
    routes = expert_ids.reshape(ROWS, TOPK)
    member = jnp.any(
        routes[:, :, None] == jnp.arange(EXPERTS, dtype=jnp.int32)[None, None, :], axis=1
    ).astype(f32)
    table = jnp.concatenate(
        [cosine] * 4 + [-sine, sine, -sine, sine]
        + [member, valid, column.astype(f32), jnp.zeros((ROWS, 94), f32)],
        axis=1,
    )

    packed, small = run_local(
        pack_kernel, "pack", place,
        [qkv_weight, out_weight, router_weight, norm_one[None], norm_two[None]],
        [((256, SMALL_AT + 128), bf16), ((256, 128), bf16)],
        [],
    )
    packed, grad_low = stage(packed, grad_low)
    grad_rows = jnp.stack([grad_low] + spread_first(grad_low))
    back, ahead, grad_rows, table = stage(
        along_x(packed, 1), along_x(packed, -1), grad_rows, table
    )
    low, high = along_x(back[:128], 1), along_x(ahead[128:], -1)
    inputs_pair = jnp.concatenate([inputs, swap_core(inputs)], axis=0)
    low, high, grad_back, grad_ahead, inputs_pair = stage(
        low, high, along_second(grad_rows, 1), along_second(grad_rows, -1), inputs_pair
    )
    full_own = jnp.concatenate([back, low, high, ahead], axis=0)
    full_sib = swap_core(full_own)
    half = (ROWS, D)
    rest = ((768, 512), bf16)
    rest_wide = ((768, D), bf16)
    query, kv, small_full = run_local(
        project_kernel, "project", place,
        [inputs, qkv_weight, full_own, full_sib, small, table],
        [(half, bf16), (half, bf16), ((40, D), f32)],
        [(half, bf16), ((ROWS, 2 * D), f32), ((128, D), f32), ((768, 128), bf16), rest_wide, rest_wide],
        fetched=(2, 3),
    )
    attended = run_local(
        attend_kernel, "attend", place,
        [inputs, query, kv, small_full, out_weight, full_own, full_sib, table],
        [(half, bf16), (half, f32), ((ROWS, EXPERTS), f32), ((WIDE, D), bf16)],
        [(half, bf16), (half, f32), rest, rest],
        fetched=(5, 6),
    )
    attended, hidden_lines, grad_two = stage(
        attended, spread_first(inputs_pair), along_second(grad_rows, 2)
    )
    line, after, gates, sent = attended

    def visit(j, *rows):
        return run_experts(
            place, list(rows), grads[j], gate_weight[0], up_weight[0], down_weight[0]
        )

    pair = jnp.concatenate([line, swap_core(line)], axis=0)
    got, pair, rows_sib = stage(spread_first(sent), pair, swap_core(grad_rows))
    grads = {0: [grad_rows, rows_sib]}
    rows = jnp.stack([sent] + got)
    parts = {}
    parts[0], back, ahead, back_sib, two_sib = stage(
        visit(0, rows, swap_core(rows)), along_second(rows, 1), along_second(rows, -1),
        swap_core(grad_back), swap_core(grad_two),
    )
    grads[1], grads[2] = [grad_back, back_sib], [grad_two, two_sib]
    parts[1], two, ahead_sib, turn = stage(
        visit(1, back, swap_core(back)), along_second(rows, 2), swap_core(ahead), swap_core(grad_ahead)
    )
    grads[3] = [grad_ahead, turn]
    parts[3], two_sib, turn_back, lines = stage(
        visit(3, ahead, ahead_sib), swap_core(two), swap_core(parts[1][1]), spread_first(pair)
    )
    merged_back = add(parts[1][0], turn_back).astype(bf16)
    normed_line, = run_local(
        norm_line_kernel, "norm_line", place,
        [inputs_pair, *hidden_lines, small_full], [((8 * ROWS, D), bf16)], [],
    )
    normed_line, merged_back, turn_ahead = stage(normed_line, merged_back, swap_core(parts[3][1]))
    merged_ahead = add(parts[3][0], turn_ahead).astype(bf16)
    parts[2], got_back, got_ahead, turn_own = stage(
        visit(2, two, two_sib), along_second(merged_back, -1), along_second(merged_ahead, -3),
        swap_core(parts[0][1]),
    )
    merged = add(parts[2][0], swap_core(parts[2][1])).astype(bf16)
    saved = [parts[j][4:9] for j in range(4)]
    merged, first_rows = stage(merged, saved[0][0])
    saved[0] = [first_rows] + list(saved[0][1:])
    partial = add(parts[0][0], turn_own, got_back, got_ahead).astype(bf16)
    chunks, partial, got_two, turn_back, turn_ahead, turn_two = stage(
        run_weight_grads(saved), partial, along_second(merged, -2),
        swap_core(parts[1][3]), swap_core(parts[3][3]), swap_core(parts[2][3]),
    )
    owned = lax.psum_scatter(chunks.reshape(4 * 768, FFE), "x", scatter_dimension=0, tiled=True)
    total = add(partial, got_two).astype(bf16)
    total, turn_back, turn_ahead, turn_two = stage(total, turn_back, turn_ahead, turn_two)
    merged_back = add(parts[1][2], turn_back).astype(bf16)
    merged_ahead = add(parts[3][2], turn_ahead).astype(bf16)
    merged = add(parts[2][2], turn_two).astype(bf16)
    arrived, merged_back, merged_ahead, merged, turn_own = stage(
        [along_first(total[i], -i) for i in (1, 2, 3)], merged_back, merged_ahead, merged,
        swap_core(parts[0][3]),
    )
    back = [total[0]] + arrived
    mine_grad, other_grad, after_grad, tiny = run_local(
        attend_back_kernel, "attend_back", place,
        back + [
            grad_low, after, gates, small_full, out_weight, full_own, full_sib, query, kv, table,
        ],
        [((4, ROWS, 384), bf16), ((4, ROWS, 384), bf16), (half, f32), ((40, D), f32)],
        [(half, bf16), ((ROWS, 3 * KV), f32), (half, bf16), ((ROWS, 2 * D), bf16), rest, rest],
        fetched=(9, 10),
    )
    mine_grad, other_grad, sib_grad, got_back, got_ahead = stage(
        mine_grad, other_grad, swap_core(other_grad),
        along_second(merged_back, -1), along_second(merged_ahead, -3),
    )
    input_grad, tiny = run_local(
        input_back_kernel, "input_back", place,
        [mine_grad, other_grad, qkv_weight, full_own, full_sib, inputs, after_grad, small_full, tiny],
        [(half, f32), ((40, D), f32)],
        [(half, bf16), (half, bf16), (half, f32), rest_wide, rest_wide],
        fetched=(3, 4),
    )
    line_grad = [
        along_first(jnp.concatenate([mine_grad[k], sib_grad[k]], axis=0), k) for k in (1, 2, 3)
    ]
    line_grad, input_grad, tiny, owned = stage(line_grad, input_grad, tiny, owned)
    expert_sums = lax.all_gather(owned, "x", axis=0, tiled=True)
    chunk = run_local(
        attention_weights_kernel, "attention_weights", place,
        [normed_line, pair, *lines, mine_grad, sib_grad, *line_grad, tiny],
        [((256, 512), bf16)] * 4,
        [((D, 512), f32), ((128, D), f32)],
    )
    chunk, got, got_two = stage(
        chunk, [along_x(chunk[k], -k) for k in (1, 2, 3)], along_second(merged, -2)
    )
    shard = add(chunk[0], *got).astype(bf16)
    total = add(parts[0][2], turn_own, got_back, got_ahead, got_two).astype(bf16)
    shard, got, total, arrived, expert_sums = stage(
        shard, [along_second(shard, k) for k in (1, 2, 3)],
        total, [along_first(total[i], -i) for i in (1, 3)], expert_sums,
    )
    shard = add(shard, *got).astype(bf16)
    gate_total, up_total, down_total = widen(expert_sums.reshape(4, 768, FFE))
    shard, got, gate_total, up_total, down_total, arrived_two = stage(
        shard, spread_first(shard), gate_total, up_total, down_total, along_first(total[2], -2)
    )
    output = (after + add(total[0], *arrived, arrived_two)).astype(bf16).reshape(MICRO, TOK_MB, D)
    both, = run_local(
        collect_kernel, "collect", place, [shard, *got], [((256, SMALL_AT + 128), bf16)], []
    )
    qkv_grad, out_grad, router_grad, gain_one, gain_two = run_local(
        finish_kernel, "finish", place, [both, swap_core(both)],
        [
            ((256, 2 * D), f32), ((256, D), f32), ((256, EXPERTS), f32),
            ((1, 256), f32), ((1, 256), f32),
        ],
        [],
    )

    return (
        output,
        input_grad.reshape(MICRO, TOK_MB, D),
        gain_one.reshape(256),
        qkv_grad,
        out_grad,
        gain_two.reshape(256),
        router_grad,
        gate_total[None],
        up_total[None],
        down_total[None],
    )


def solution(mesh):
    grid = Mesh(mesh.devices.reshape(4, 4, 4, 2), ("x", "y", "z", "core"))
    every = ("x", "y", "z", "core")
    plane = ("y", "z", "core")
    return jax.shard_map(
        per_device,
        mesh=grid,
        in_specs=(
            P(None, every, None),
            P(None, every),
            P(None, every),
            P(None, every, None),
            P("x"),
            P("x", None),
            P("x", None),
            P("x"),
            P("x", None),
            P(plane, None, None),
            P(plane, None, None),
            P(plane, None, None),
            P(None, every, None),
        ),
        out_specs=(
            P(None, every, None),
            P(None, every, None),
            P("x"),
            P("x", None),
            P("x", None),
            P("x"),
            P("x", None),
            P(plane, None, None),
            P(plane, None, None),
            P(plane, None, None),
        ),
        check_vma=False,
    )
```

```python
import functools

import jax
import jax.numpy as jnp
from jax import lax
from jax.experimental import pallas as pl
from jax.experimental.pallas import tpu as pltpu
from jax.sharding import Mesh
from jax.sharding import PartitionSpec as P

D = 1024
QUERY_HEADS = 16
KEY_VALUE_HEADS = 8
HEAD_SIZE = 64
FFE = 512
TOPK = 8
MICRO = 2
TOK_MB = 64
EXPERTS = 32
CAP = 24
ROWS = MICRO * TOK_MB
SLOTS = MICRO * CAP
EXTRA = 16
WIDE = ROWS + EXTRA
KV = KEY_VALUE_HEADS * HEAD_SIZE
SMALL_AT = D + D // 2
SHORT = pl.CostEstimate(flops=1_000_000, bytes_accessed=100_000, transcendentals=0)

epsilon = 1e-06
highest = lax.Precision.HIGHEST
f32 = jnp.float32
bf16 = jnp.bfloat16


def plane_pairs(first, second, swap):
    pairs = []
    for y in range(4):
        for z in range(4):
            for c in range(2):
                dy, dz = (first, second) if c == 0 else (second, first)
                target = (((y + dy) % 4) * 4 + (z + dz) % 4) * 2 + (c ^ swap)
                pairs.append(((y * 4 + z) * 2 + c, target))
    return pairs


def along_first(v, k):
    return lax.ppermute(v, ("y", "z", "core"), plane_pairs(k % 4, 0, 0))


def along_second(v, k):
    return lax.ppermute(v, ("y", "z", "core"), plane_pairs(0, k % 4, 0))


def swap_core(v):
    return lax.ppermute(v, "core", [(0, 1), (1, 0)])


def along_x(v, k):
    return lax.ppermute(v, "x", [(i, (i + k) % 4) for i in range(4)])


def stage(*values):
    return lax.optimization_barrier(values)


def spread_first(v):
    return [along_first(v, k) for k in (1, 2, 3)]


def add(first, *others):
    total = first.astype(f32)
    for v in others:
        total = total + v.astype(f32)
    return total


def nt(a, b):
    return lax.dot_general(a, b, (((1,), (1,)), ((), ())), preferred_element_type=f32)


def tn(a, b):
    return lax.dot_general(a, b, (((0,), (0,)), ((), ())), preferred_element_type=f32)


def nn(a, b):
    return jnp.dot(a, b, preferred_element_type=f32)


BLOCKS = 8
PACKED = BLOCKS * SLOTS


def expert_kernel(n_rows, n_grads, place_ref, *refs):
    row_refs, refs = refs[:n_rows], refs[n_rows:]
    grad_refs, refs = refs[:n_grads], refs[n_grads:]
    gate_ref, up_ref, down_ref = refs[:3]
    back_refs, out_refs, save_refs = refs[3:5], refs[5:7], refs[7:12]
    (row_buf, grad_buf, back_buf, out_buf, x_buf, c_buf, r_buf, s_buf, h_buf, g_buf, u_buf,
     mix_buf, pick_buf, dot_buf, gate_buf, up_buf, down_buf,
     row_sem, grad_sem, back_sem, out_sem, save_sem, weight_sem) = refs[12:]

    def pieces(sources, buf, sem):
        copies = []
        for ref in sources:
            for b in range(ref.shape[0]):
                at = len(copies)
                copies.append(pltpu.make_async_copy(ref.at[b], buf.at[at], sem.at[at]))
        return copies

    row_loads = pieces(row_refs, row_buf, row_sem)
    grad_loads = pieces(grad_refs, grad_buf, grad_sem)
    weight_loads = [
        pltpu.make_async_copy(ref, buf, weight_sem.at[i])
        for i, (ref, buf) in enumerate(
            zip((gate_ref, up_ref, down_ref), (gate_buf, up_buf, down_buf))
        )
    ]
    for one, two in zip(row_loads, grad_loads):
        one.start()
        two.start()
    for copy in weight_loads:
        copy.start()

    expert = place_ref[0]
    row_at = expert % 4
    lane_at = pl.multiple_of((expert // 4) * 128, 128)
    upper = (
        lax.broadcasted_iota(jnp.int32, (ROWS, ROWS), 0)
        < lax.broadcasted_iota(jnp.int32, (ROWS, ROWS), 1)
    ).astype(bf16)
    extra_row = lax.broadcasted_iota(jnp.int32, (EXTRA, 128), 0)
    slot_row = lax.broadcasted_iota(jnp.int32, (SLOTS, ROWS), 0).astype(f32)

    @pl.loop(0, BLOCKS)
    def _(b):
        pltpu.make_async_copy(row_refs[0].at[0], row_buf.at[b], row_sem.at[b]).wait()
        pltpu.make_async_copy(grad_refs[0].at[0], grad_buf.at[b], grad_sem.at[b]).wait()
        info = row_buf[b, ROWS:WIDE, pl.ds(lane_at, 128)].astype(f32)
        high = jnp.sum(jnp.where(extra_row == row_at, info, 0.0), axis=0, keepdims=True)
        low = jnp.sum(jnp.where(extra_row == row_at + 4, info, 0.0), axis=0, keepdims=True)
        chosen = high > 0.0
        flags = jnp.broadcast_to(chosen.astype(f32), (16, ROWS)).astype(bf16)
        rank = nn(flags, upper)[0:1]
        pick = jnp.where((slot_row == rank) & chosen, 1.0, 0.0)
        weight = jnp.sum(pick * (high + low), axis=1, keepdims=True)
        low_pick = pick.astype(bf16)
        pick_buf[b] = low_pick
        span = pl.ds(pl.multiple_of(b * SLOTS, SLOTS), SLOTS)
        mix_buf[span, :] = jnp.broadcast_to(weight, (SLOTS, 128))
        x_buf[span, :] = nn(low_pick, row_buf[b, 0:ROWS, :]).astype(bf16)
        c_buf[span, :] = nn(low_pick, grad_buf[b]).astype(bf16)

    saves = [
        pltpu.make_async_copy(buf, ref, save_sem.at[i])
        for i, (buf, ref) in enumerate(zip((x_buf, s_buf, h_buf, g_buf, u_buf), save_refs))
    ]
    saves[0].start()
    mixing = mix_buf[:, 0:1]
    grads = c_buf[...].astype(f32)
    s_buf[...] = (mixing * grads).astype(bf16)
    saves[1].start()
    for copy in weight_loads:
        copy.wait()
    gate_pre = nn(x_buf[...], gate_buf[...])
    up_pre = nn(x_buf[...], up_buf[...])
    sigma = 1.0 / (1.0 + jnp.exp(-gate_pre))
    swish = gate_pre * sigma
    h_buf[...] = (swish * up_pre).astype(bf16)
    saves[2].start()
    hidden_grad = nt(s_buf[...], down_buf[...])
    slope = sigma * (1.0 + gate_pre * (1.0 - sigma))
    g_buf[...] = (hidden_grad * up_pre * slope).astype(bf16)
    u_buf[...] = (hidden_grad * swish).astype(bf16)
    saves[3].start()
    saves[4].start()
    r_buf[...] = (nt(g_buf[...], gate_buf[...]) + nt(u_buf[...], up_buf[...])).astype(bf16)
    produced = nn(h_buf[...], down_buf[...]).astype(bf16).astype(f32)
    gate_grad = jnp.sum(produced * c_buf[...].astype(f32), axis=1, keepdims=True)
    dot_buf[...] = jnp.broadcast_to(gate_grad, (PACKED, 128))
    c_buf[...] = (mixing * produced).astype(bf16)

    @pl.loop(0, BLOCKS)
    def _(b):
        low_pick = pick_buf[b]
        span = pl.ds(pl.multiple_of(b * SLOTS, SLOTS), SLOTS)
        back_buf[b, 0:ROWS, :] = tn(low_pick, r_buf[span, :]).astype(bf16)
        out_buf[b] = tn(low_pick, c_buf[span, :]).astype(bf16)
        back_buf[b, ROWS:WIDE, :] = jnp.zeros((EXTRA, D), bf16)
        dots = jnp.sum(low_pick.astype(f32) * dot_buf[span, :], axis=0, keepdims=True)
        high = dots.astype(bf16).astype(f32)
        info = jnp.where(extra_row == row_at, high, 0.0)
        info = info + jnp.where(extra_row == row_at + 4, dots - high, 0.0)
        back_buf[b, ROWS:WIDE, pl.ds(lane_at, 128)] = info.astype(bf16)
        for side in range(2):
            @pl.when(b // 4 == side)
            def _():
                at = b - 4 * side
                pltpu.make_async_copy(back_buf.at[b], back_refs[side].at[at], back_sem.at[b]).start()
                pltpu.make_async_copy(out_buf.at[b], out_refs[side].at[at], out_sem.at[b]).start()

    for b in range(BLOCKS):
        side, at = b // 4, b % 4
        pltpu.make_async_copy(back_buf.at[b], back_refs[side].at[at], back_sem.at[b]).wait()
        pltpu.make_async_copy(out_buf.at[b], out_refs[side].at[at], out_sem.at[b]).wait()
    for copy in saves:
        copy.wait()


def run_experts(place, rows, grads, gate, up, down):
    any_space = pl.BlockSpec(memory_space=pl.ANY)
    wide = jax.ShapeDtypeStruct((4, WIDE, D), bf16)
    flat = jax.ShapeDtypeStruct((4, ROWS, D), bf16)
    full = jax.ShapeDtypeStruct((PACKED, D), bf16)
    half = jax.ShapeDtypeStruct((PACKED, FFE), bf16)
    return pl.pallas_call(
        functools.partial(expert_kernel, len(rows), len(grads)),
        in_specs=[pl.BlockSpec(memory_space=pltpu.SMEM)]
        + [any_space] * (len(rows) + len(grads) + 3),
        out_specs=[any_space] * 9,
        out_shape=[wide, wide, flat, flat, full, full, half, half, half],
        scratch_shapes=[
            pltpu.VMEM((BLOCKS, WIDE, D), bf16),
            pltpu.VMEM((BLOCKS, ROWS, D), bf16),
            pltpu.VMEM((BLOCKS, WIDE, D), bf16),
            pltpu.VMEM((BLOCKS, ROWS, D), bf16),
            pltpu.VMEM((PACKED, D), bf16),
            pltpu.VMEM((PACKED, D), bf16),
            pltpu.VMEM((PACKED, D), bf16),
            pltpu.VMEM((PACKED, D), bf16),
            pltpu.VMEM((PACKED, FFE), bf16),
            pltpu.VMEM((PACKED, FFE), bf16),
            pltpu.VMEM((PACKED, FFE), bf16),
            pltpu.VMEM((PACKED, 128), f32),
            pltpu.VMEM((BLOCKS, SLOTS, ROWS), bf16),
            pltpu.VMEM((PACKED, 128), f32),
            pltpu.VMEM((D, FFE), bf16),
            pltpu.VMEM((D, FFE), bf16),
            pltpu.VMEM((FFE, D), bf16),
            pltpu.SemaphoreType.DMA((BLOCKS,)),
            pltpu.SemaphoreType.DMA((BLOCKS,)),
            pltpu.SemaphoreType.DMA((BLOCKS,)),
            pltpu.SemaphoreType.DMA((BLOCKS,)),
            pltpu.SemaphoreType.DMA((5,)),
            pltpu.SemaphoreType.DMA((3,)),
        ],
        compiler_params=pltpu.CompilerParams(vmem_limit_bytes=60 * 1024 * 1024),
        cost_estimate=SHORT,
        name="experts",
    )(place, *rows, *grads, gate, up, down)


def weight_grad_kernel(*refs):
    xs, ss, hs, gs, us = (refs[4 * i:4 * i + 4] for i in range(5))
    out_ref = refs[20]
    x_buf, s_buf, h_buf, g_buf, u_buf, out_buf, in_sem, out_sem = refs[21:]
    loads = []
    for j in range(4):
        for i, (sources, buf) in enumerate(
            zip((xs, gs, us, hs, ss), (x_buf, g_buf, u_buf, h_buf, s_buf))
        ):
            loads.append(pltpu.make_async_copy(sources[j], buf.at[j], in_sem.at[j, i]))
    for copy in loads:
        copy.start()
    for copy in loads:
        copy.wait()

    @pl.loop(0, 4)
    def _(k):
        wide_at = pl.multiple_of(k * 256, 256)
        thin_at = pl.multiple_of(k * 128, 128)
        rows = x_buf[:, :, pl.ds(wide_at, 256)].reshape(4 * PACKED, 256)
        thin = h_buf[:, :, pl.ds(thin_at, 128)].reshape(4 * PACKED, 128)
        out_buf[k, 0:256, :] = tn(rows, g_buf[...].reshape(4 * PACKED, FFE)).astype(bf16)
        out_buf[k, 256:512, :] = tn(rows, u_buf[...].reshape(4 * PACKED, FFE)).astype(bf16)
        down = tn(thin, s_buf[...].reshape(4 * PACKED, D)).astype(bf16)
        out_buf[k, 512:640, :] = down[:, 0:FFE]
        out_buf[k, 640:768, :] = down[:, FFE:D]
        pltpu.make_async_copy(out_buf.at[k], out_ref.at[k], out_sem.at[k]).start()

    for k in range(4):
        pltpu.make_async_copy(out_buf.at[k], out_ref.at[k], out_sem.at[k]).wait()


def run_weight_grads(saved):
    operands = [part[i] for i in range(5) for part in saved]
    any_space = pl.BlockSpec(memory_space=pl.ANY)
    return pl.pallas_call(
        weight_grad_kernel,
        in_specs=[any_space] * 20,
        out_specs=any_space,
        out_shape=jax.ShapeDtypeStruct((4, 768, FFE), bf16),
        scratch_shapes=[
            pltpu.VMEM((4, PACKED, D), bf16),
            pltpu.VMEM((4, PACKED, D), bf16),
            pltpu.VMEM((4, PACKED, FFE), bf16),
            pltpu.VMEM((4, PACKED, FFE), bf16),
            pltpu.VMEM((4, PACKED, FFE), bf16),
            pltpu.VMEM((4, 768, FFE), bf16),
            pltpu.SemaphoreType.DMA((4, 5)),
            pltpu.SemaphoreType.DMA((4,)),
        ],
        compiler_params=pltpu.CompilerParams(vmem_limit_bytes=60 * 1024 * 1024),
        cost_estimate=SHORT,
        name="expert_weight_grads",
    )(*operands)


def blocks_behind(x_at, n):
    return [pl.multiple_of(((x_at + 4 - k) % 4) * n, n) for k in range(4)]


def swapped_halves(v):
    lane = lax.broadcasted_iota(jnp.int32, v.shape, 1)
    return jnp.where(lane % HEAD_SIZE < HEAD_SIZE // 2, pltpu.roll(v, 96, 1), pltpu.roll(v, 32, 1))


def pack_kernel(place_ref, qkv_ref, out_ref, router_ref, gains_ref, packed_ref, small_ref):
    core = place_ref[4]
    packed_ref[:, 0:D] = qkv_ref[:, pl.ds(pl.multiple_of(core * D, D), D)]
    packed_ref[:, D:SMALL_AT] = out_ref[:, pl.ds(pl.multiple_of(core * 512, 512), 512)]
    rows = [router_ref[...].astype(f32), gains_ref[...].astype(f32), jnp.zeros((94, 256), f32)]
    small = jnp.concatenate(rows, axis=0).T.astype(bf16)
    packed_ref[:, SMALL_AT:SMALL_AT + 128] = small
    small_ref[...] = small


def rest_copies(near_ref, far_ref, buf, sem, at, lane, width):
    columns = slice(lane, lane + width)
    return [
        pltpu.make_async_copy(near_ref.at[0:256, columns], buf.at[0:256], sem.at[at]),
        pltpu.make_async_copy(far_ref.at[:, columns], buf.at[256:512], sem.at[at + 1]),
        pltpu.make_async_copy(near_ref.at[256:512, columns], buf.at[512:768], sem.at[at + 2]),
    ]


def project_kernel(
    place_ref, x_ref, mine_ref, tiny_ref, table_ref, near_ref, far_ref, sib_near_ref, sib_far_ref,
    q_ref, kv_ref, small_ref,
    norm_buf, all_buf, tiny_buf, small_buf, own_buf, sib_buf, sem,
):
    x_at, core = place_ref[1], place_ref[4]
    lanes = blocks_behind(x_at, 256)
    small_loads = rest_copies(near_ref, far_ref, small_buf, sem, 0, SMALL_AT, 128)
    own_loads = rest_copies(near_ref, far_ref, own_buf, sem, 3, 0, D)
    sib_loads = rest_copies(sib_near_ref, sib_far_ref, sib_buf, sem, 6, 0, D)
    for copy in small_loads + own_loads + sib_loads:
        copy.start()
    for copy in small_loads:
        copy.wait()
    for k in range(4):
        piece = tiny_ref[...] if k == 0 else small_buf[(k - 1) * 256:k * 256, :]
        tiny_buf[:, pl.ds(lanes[k], 256)] = piece.astype(f32).T
    small_ref[...] = tiny_buf[0:40, :]
    x = x_ref[...].astype(f32)
    inverse = lax.rsqrt(jnp.mean(x * x, axis=1, keepdims=True) + epsilon)
    norm_buf[...] = (x * inverse * tiny_buf[32:33, :]).astype(bf16)
    rows = [norm_buf[:, pl.ds(at, 256)] for at in lanes]
    own_at = pl.multiple_of(core * D, D)
    sib_at = pl.multiple_of((1 - core) * D, D)
    for at, rest, loads in ((own_at, own_buf, own_loads), (sib_at, sib_buf, sib_loads)):
        total = nn(rows[0], mine_ref[:, pl.ds(at, D)])
        for copy in loads:
            copy.wait()
        for k in (1, 2, 3):
            total = total + nn(rows[k], rest[(k - 1) * 256:k * 256, :])
        all_buf[:, pl.ds(at, D)] = total
    cosine, sine = table_ref[:, 0:128], table_ref[:, 128:256]
    for c in range(12):
        v = all_buf[:, c * 128:(c + 1) * 128]
        turned = (v * cosine + swapped_halves(v) * sine).astype(bf16)
        if c < 8:
            q_ref[:, c * 128:(c + 1) * 128] = turned
        else:
            kv_ref[:, (c - 8) * 128:(c - 7) * 128] = turned
    kv_ref[:, KV:2 * KV] = all_buf[:, D + KV:D + 2 * KV].astype(bf16)


def head_scores(q_ref, kv_ref, allowed, h):
    chunk = q_ref[:, h * 128:(h + 1) * 128]
    query = jnp.concatenate([chunk[:, 0:64], chunk[:, 64:128]], axis=0)
    key = kv_ref[:, h * 64:(h + 1) * 64]
    value = kv_ref[:, KV + h * 64:KV + (h + 1) * 64]
    scores = jnp.where(allowed, nt(query, key) * HEAD_SIZE ** (-0.5), -1e30)
    expo = jnp.exp(scores - jnp.max(scores, axis=1, keepdims=True))
    probs = expo / jnp.sum(expo, axis=1, keepdims=True)
    return query, key, value, probs


def allowed_pairs(table_ref):
    shape = (2 * ROWS, ROWS)
    column = table_ref[:, 289:290]
    row = table_ref[:, 256:384].T[33:34]
    q = lax.broadcasted_iota(jnp.int32, shape, 0) % ROWS
    p = lax.broadcasted_iota(jnp.int32, shape, 1)
    return (jnp.concatenate([column, column], axis=0) == row) & (p <= q)


def attend_kernel(
    place_ref, x_ref, q_ref, kv_ref, small_ref, mine_ref, table_ref,
    near_ref, far_ref, sib_near_ref, sib_far_ref,
    line_ref, after_ref, gates_ref, sent_ref,
    low_buf, out_buf, own_buf, sib_buf, sem,
):
    x_at, core = place_ref[1], place_ref[4]
    loads = rest_copies(near_ref, far_ref, own_buf, sem, 0, D, 512)
    loads += rest_copies(sib_near_ref, sib_far_ref, sib_buf, sem, 3, D, 512)
    for copy in loads:
        copy.start()
    allowed = allowed_pairs(table_ref)
    for h in range(KEY_VALUE_HEADS):
        _, _, value, probs = head_scores(q_ref, kv_ref, allowed, h)
        got = nn(probs.astype(bf16), value)
        low_buf[:, h * 128:(h + 1) * 128] = jnp.concatenate(
            [got[0:ROWS], got[ROWS:2 * ROWS]], axis=1
        ).astype(bf16)
    rows = [low_buf[:, pl.ds(at, 256)] for at in blocks_behind(x_at, 256)]
    for k in range(4):
        line_ref[:, k * 256:(k + 1) * 256] = rows[k]
    own_at = pl.multiple_of(core * 512, 512)
    sib_at = pl.multiple_of((1 - core) * 512, 512)
    for copy in loads:
        copy.wait()
    for at, rest in ((own_at, own_buf), (sib_at, sib_buf)):
        total = nn(rows[0], mine_ref[:, pl.ds(at, 512)])
        for k in (1, 2, 3):
            total = total + nn(rows[k], rest[(k - 1) * 256:k * 256, :])
        out_buf[:, pl.ds(at, 512)] = total
    valid = table_ref[:, 288:289]
    after = x_ref[...].astype(f32) + valid * out_buf[...]
    after_ref[...] = after
    inverse = lax.rsqrt(jnp.mean(after * after, axis=1, keepdims=True) + epsilon)
    second = after * inverse * small_ref[33:34, :]
    logits = lax.dot_general(
        second, small_ref[0:32, :], (((1,), (1,)), ((), ())),
        precision=highest, preferred_element_type=f32,
    )
    member = table_ref[:, 256:288] > 0.0
    masked = jnp.where(member, logits, -3e38)
    gates = jnp.where(member, jnp.exp(masked - jnp.max(masked, axis=1, keepdims=True)), 0.0)
    gates = gates / jnp.sum(gates, axis=1, keepdims=True)
    gates_ref[...] = gates
    mixing = jnp.concatenate([gates * valid, jnp.zeros((ROWS, 96), f32)], axis=1).T
    high = mixing[0:32].astype(bf16).astype(f32)
    low = mixing[0:32] - high
    info = [
        jnp.concatenate([high[4 * q:4 * q + 4], low[4 * q:4 * q + 4], jnp.zeros((8, 128), f32)], axis=0)
        for q in range(8)
    ]
    sent_ref[0:ROWS, :] = second.astype(bf16)
    sent_ref[ROWS:WIDE, :] = jnp.concatenate(info, axis=1).astype(bf16)


def norm_backward(grad, values, gain):
    inverse = lax.rsqrt(jnp.mean(values * values, axis=1, keepdims=True) + epsilon)
    scaled = grad * gain
    gain_grad = jnp.sum(grad * values * inverse, axis=0, keepdims=True)
    dot = jnp.mean(scaled * values, axis=1, keepdims=True)
    return inverse * (scaled - values * (inverse * inverse * dot)), gain_grad


def attend_back_kernel(
    place_ref, b0, b1, b2, b3, cot_ref, after_ref, gates_ref, small_ref,
    mine_ref, q_ref, kv_ref, table_ref, near_ref, far_ref, sib_near_ref, sib_far_ref,
    mine_out, other_out, after_grad_ref, tiny_ref,
    low_buf, sum_buf, grad_buf, all_buf, own_buf, sib_buf, sem,
):
    x_at, first_at, second_at, core = (place_ref[i] for i in (1, 2, 3, 4))
    loads = rest_copies(near_ref, far_ref, own_buf, sem, 0, D, 512)
    loads += rest_copies(sib_near_ref, sib_far_ref, sib_buf, sem, 3, D, 512)
    for copy in loads:
        copy.start()
    back = b0[...].astype(f32) + b1[...].astype(f32) + b2[...].astype(f32) + b3[...].astype(f32)
    extra = back[ROWS:WIDE]
    dots = extra[0:4] + extra[4:8]
    dots = jnp.concatenate([dots[:, q * 128:(q + 1) * 128] for q in range(8)], axis=0)
    dots = jnp.concatenate([dots, jnp.zeros((96, ROWS), f32)], axis=0).T[:, 0:32]
    valid, gates = table_ref[:, 288:289], gates_ref[...]
    gate_grad = dots * valid
    logit_grad = gates * (gate_grad - jnp.sum(gates * gate_grad, axis=1, keepdims=True))
    after = after_ref[...]
    gain = small_ref[33:34, :]
    inverse = lax.rsqrt(jnp.mean(after * after, axis=1, keepdims=True) + epsilon)
    second = after * inverse * gain
    wide_grad = jnp.concatenate([logit_grad, jnp.zeros((ROWS, 96), f32)], axis=1)
    tiny_ref[0:32, :] = jnp.dot(
        wide_grad.T, second, precision=highest, preferred_element_type=f32
    )[0:32]
    second_grad = back[0:ROWS] + jnp.dot(
        logit_grad, small_ref[0:32, :], precision=highest, preferred_element_type=f32
    )
    norm_grad, gain_grad = norm_backward(second_grad, after, gain)
    tiny_ref[32:40, :] = jnp.concatenate(
        [jnp.zeros((1, D), f32), gain_grad, jnp.zeros((6, D), f32)], axis=0
    )
    after_grad = cot_ref[...].astype(f32) + norm_grad
    after_grad_ref[...] = after_grad
    low_buf[...] = (valid * after_grad).astype(bf16)
    own_at = pl.multiple_of(core * 512, 512)
    sib_at = pl.multiple_of((1 - core) * 512, 512)
    own = low_buf[:, pl.ds(own_at, 512)]
    other = low_buf[:, pl.ds(sib_at, 512)]
    for copy in loads:
        copy.wait()
    lanes = blocks_behind(x_at, 256)
    for k in range(4):
        if k == 0:
            got = nt(own, mine_ref[:, pl.ds(own_at, 512)]) + nt(other, mine_ref[:, pl.ds(sib_at, 512)])
        else:
            span = slice((k - 1) * 256, k * 256)
            got = nt(own, own_buf[span, :]) + nt(other, sib_buf[span, :])
        grad_buf[:, pl.ds(lanes[k], 256)] = got.astype(bf16)
    allowed = allowed_pairs(table_ref)
    cosine, sine = table_ref[:, 0:128], table_ref[:, 128:256]
    scale = HEAD_SIZE ** (-0.5)
    for h in range(KEY_VALUE_HEADS):
        query, key, value, probs = head_scores(q_ref, kv_ref, allowed, h)
        chunk = grad_buf[:, h * 128:(h + 1) * 128]
        grad = jnp.concatenate([chunk[:, 0:64], chunk[:, 64:128]], axis=0)
        prob_grad = nt(grad, value)
        score_grad = (
            probs * (prob_grad - jnp.sum(probs * prob_grad, axis=1, keepdims=True))
        ).astype(bf16)
        value_grad = tn(probs.astype(bf16), grad)
        query_grad = nn(score_grad, key) * scale
        key_grad = tn(score_grad, query) * scale
        sum_buf[:, h * 128:(h + 1) * 128] = jnp.concatenate(
            [query_grad[0:ROWS], query_grad[ROWS:2 * ROWS]], axis=1
        )
        sum_buf[:, D + h * 64:D + (h + 1) * 64] = key_grad
        all_buf[:, D + KV + h * 64:D + KV + (h + 1) * 64] = value_grad.astype(bf16)
    for c in range(12):
        v = sum_buf[:, c * 128:(c + 1) * 128]
        all_buf[:, c * 128:(c + 1) * 128] = (v * cosine - swapped_halves(v) * sine).astype(bf16)
    for f in range(4):
        at = (first_at + f) % 4
        mine_out[f, :, 0:256] = all_buf[:, pl.ds(pl.multiple_of(core * D + at * 256, 256), 256)]
        mine_out[f, :, 256:384] = low_buf[:, pl.ds(pl.multiple_of(core * 512 + at * 128, 128), 128)]
        at = (second_at + f) % 4
        other_out[f, :, 0:256] = all_buf[:, pl.ds(pl.multiple_of((1 - core) * D + at * 256, 256), 256)]
        other_out[f, :, 256:384] = low_buf[
            :, pl.ds(pl.multiple_of((1 - core) * 512 + at * 128, 128), 128)
        ]


def input_back_kernel(
    place_ref, mine_grad, other_grad, mine_ref, x_ref, after_grad_ref, small_ref, tiny_in,
    near_ref, far_ref, sib_near_ref, sib_far_ref,
    input_grad_ref, tiny_ref,
    own_buf, other_buf, grad_buf, own_rest, sib_rest, sem,
):
    x_at, first_at, second_at, core = (place_ref[i] for i in (1, 2, 3, 4))
    loads = rest_copies(near_ref, far_ref, own_rest, sem, 0, 0, D)
    loads += rest_copies(sib_near_ref, sib_far_ref, sib_rest, sem, 3, 0, D)
    for copy in loads:
        copy.start()
    for f in range(4):
        at = pl.multiple_of(((first_at + f) % 4) * 256, 256)
        own_buf[:, pl.ds(at, 256)] = mine_grad[f, :, 0:256]
        at = pl.multiple_of(((second_at + f) % 4) * 256, 256)
        other_buf[:, pl.ds(at, 256)] = other_grad[f, :, 0:256]
    own, other = own_buf[...], other_buf[...]
    own_at = pl.multiple_of(core * D, D)
    sib_at = pl.multiple_of((1 - core) * D, D)
    lanes = blocks_behind(x_at, 256)
    for copy in loads:
        copy.wait()
    for k in range(4):
        if k == 0:
            got = nt(own, mine_ref[:, pl.ds(own_at, D)]) + nt(other, mine_ref[:, pl.ds(sib_at, D)])
        else:
            span = slice((k - 1) * 256, k * 256)
            got = nt(own, own_rest[span, :]) + nt(other, sib_rest[span, :])
        grad_buf[:, pl.ds(lanes[k], 256)] = got
    norm_grad, gain_grad = norm_backward(
        grad_buf[...], x_ref[...].astype(f32), small_ref[32:33, :]
    )
    input_grad_ref[...] = after_grad_ref[...] + norm_grad
    tiny_ref[0:32, :] = tiny_in[0:32, :]
    tiny_ref[32:40, :] = jnp.concatenate([gain_grad, tiny_in[33:40, :]], axis=0)


def norm_line_kernel(place_ref, r0, r1, r2, r3, r4, r5, r6, r7, small_ref, out_ref):
    gain = small_ref[32:33, :]
    lanes = blocks_behind(place_ref[1], 256)
    for i, ref in enumerate((r0, r1, r2, r3, r4, r5, r6, r7)):
        x = ref[ref.shape[0] - ROWS:, :].astype(f32)
        inverse = lax.rsqrt(jnp.mean(x * x, axis=1, keepdims=True) + epsilon)
        out_ref[i * ROWS:(i + 1) * ROWS, :] = (x * inverse * gain).astype(bf16)
    pieces = [out_ref[:, pl.ds(lane, 256)] for lane in lanes]
    for k in range(4):
        out_ref[:, k * 256:(k + 1) * 256] = pieces[k]


def attention_weights_kernel(
    place_ref, n_ref, a0, a1, a2, a3, g0, g1, g2, g3, g4, tiny_ref,
    o0, o1, o2, o3,
    sum_buf, tiny_buf,
):
    x_at = place_ref[1]
    grads = [jnp.concatenate([g0[0], g1[0]], axis=0), g2[...], g3[...], g4[...]]
    out_sum = in_sum = None
    at = 0
    for ref, grad in zip((a0, a1, a2, a3), grads):
        one = tn(ref[...], grad[:, 256:384])
        two = tn(n_ref[at:at + ref.shape[0], :], grad[:, 0:256])
        out_sum = one if out_sum is None else out_sum + one
        in_sum = two if in_sum is None else in_sum + two
        at += ref.shape[0]
    sum_buf[:, 0:256] = in_sum
    sum_buf[:, 256:384] = out_sum
    tiny_buf[0:40, :] = tiny_ref[...]
    tiny_buf[40:128, :] = jnp.zeros((88, D), f32)
    for k, lane in enumerate(blocks_behind(x_at, 256)):
        sum_buf[k * 256:(k + 1) * 256, 384:512] = tiny_buf[:, pl.ds(lane, 256)].T
    for k, out in enumerate((o0, o1, o2, o3)):
        out[...] = sum_buf[k * 256:(k + 1) * 256, :].astype(bf16)


def collect_kernel(place_ref, p0, p1, p2, p3, out_ref):
    tiny = None
    for ref, wide, thin in zip(
        (p0, p1, p2, p3), blocks_behind(place_ref[2], 256), blocks_behind(place_ref[2], 128)
    ):
        out_ref[:, pl.ds(wide, 256)] = ref[:, 0:256]
        out_ref[:, pl.ds(pl.multiple_of(D + thin, 128), 128)] = ref[:, 256:384]
        one = ref[:, 384:512].astype(f32)
        tiny = one if tiny is None else tiny + one
    out_ref[:, SMALL_AT:SMALL_AT + 128] = tiny.astype(bf16)


def finish_kernel(place_ref, own_ref, other_ref, qkv_ref, out_ref, router_ref, one_ref, two_ref):
    core = place_ref[4]
    for ref, side in ((own_ref, core), (other_ref, 1 - core)):
        qkv_ref[:, pl.ds(pl.multiple_of(side * D, D), D)] = ref[:, 0:D].astype(f32)
        out_ref[:, pl.ds(pl.multiple_of(side * 512, 512), 512)] = ref[:, D:SMALL_AT].astype(f32)
    tiny = own_ref[:, SMALL_AT:SMALL_AT + 128].astype(f32)
    tiny = tiny + other_ref[:, SMALL_AT:SMALL_AT + 128].astype(f32)
    router_ref[...] = tiny[:, 0:EXPERTS]
    turned = tiny.T
    one_ref[...] = turned[32:33]
    two_ref[...] = turned[33:34]


def widen_kernel(sum_ref, gate_ref, up_ref, down_ref):
    gate_ref[...] = sum_ref[0, 0:256, :].astype(f32)
    up_ref[...] = sum_ref[0, 256:512, :].astype(f32)
    down_ref[:, 0:FFE] = sum_ref[0, 512:640, :].astype(f32)
    down_ref[:, FFE:D] = sum_ref[0, 640:768, :].astype(f32)


def widen(sums):
    return pl.pallas_call(
        widen_kernel,
        grid=(4,),
        in_specs=[pl.BlockSpec((1, 768, FFE), lambda k: (k, 0, 0))],
        out_specs=[
            pl.BlockSpec((256, FFE), lambda k: (k, 0)),
            pl.BlockSpec((256, FFE), lambda k: (k, 0)),
            pl.BlockSpec((128, D), lambda k: (k, 0)),
        ],
        out_shape=[
            jax.ShapeDtypeStruct((D, FFE), f32),
            jax.ShapeDtypeStruct((D, FFE), f32),
            jax.ShapeDtypeStruct((FFE, D), f32),
        ],
        compiler_params=pltpu.CompilerParams(vmem_limit_bytes=60 * 1024 * 1024),
        cost_estimate=SHORT,
        name="widen",
    )(sums)


def run_local(kernel, name, place, operands, outs, scratch, fetched=(), room=60):
    vmem = pl.BlockSpec(memory_space=pltpu.VMEM)
    apart = pl.BlockSpec(memory_space=pl.ANY)
    return pl.pallas_call(
        kernel,
        in_specs=[pl.BlockSpec(memory_space=pltpu.SMEM)]
        + [vmem] * len(operands)
        + [apart] * len(fetched),
        out_specs=[vmem] * len(outs),
        out_shape=[jax.ShapeDtypeStruct(shape, kind) for shape, kind in outs],
        scratch_shapes=[pltpu.VMEM(shape, kind) for shape, kind in scratch]
        + ([pltpu.SemaphoreType.DMA((9,))] if fetched else []),
        compiler_params=pltpu.CompilerParams(vmem_limit_bytes=room * 1024 * 1024),
        cost_estimate=SHORT,
        name=name,
    )(place, *operands, *fetched)


def block_at(v, index, size, axis):
    return lax.dynamic_slice_in_dim(v, index * size, size, axis)


def per_device(
    hidden_in,
    segment_ids,
    token_counts,
    expert_ids,
    norm_one,
    qkv_weight,
    out_weight,
    norm_two,
    router_weight,
    gate_weight,
    up_weight,
    down_weight,
    cotangent,
):
    x_at = lax.axis_index("x")
    y_at = lax.axis_index("y")
    z_at = lax.axis_index("z")
    core = lax.axis_index("core")
    first_at = jnp.where(core == 0, y_at, z_at)
    second_at = jnp.where(core == 0, z_at, y_at)
    place = jnp.stack([(y_at * 4 + z_at) * 2 + core, x_at, first_at, second_at, core]).astype(jnp.int32)

    grad_low = cotangent.reshape(ROWS, D)
    inputs = hidden_in.reshape(ROWS, D)
    valid = (
        (jnp.arange(TOK_MB, dtype=jnp.int32)[None, :] < token_counts).reshape(ROWS, 1).astype(f32)
    )
    segment_key = (
        segment_ids + (TOK_MB + 1) * jnp.arange(MICRO, dtype=jnp.int32)[:, None]
    ).reshape(ROWS)
    column, row = segment_key[:, None], segment_key[None, :]
    places = jnp.arange(ROWS)
    allowed = (column == row) & (places[:, None] >= places[None, :])
    position = jnp.sum(allowed.astype(f32), axis=1) - 1.0
    frequency = 10000.0 ** (-2.0 * jnp.arange(HEAD_SIZE // 2, dtype=f32) / HEAD_SIZE)
    angles = position[:, None] * frequency[None, :]
    cosine, sine = jnp.cos(angles), jnp.sin(angles)
    routes = expert_ids.reshape(ROWS, TOPK)
    member = jnp.any(
        routes[:, :, None] == jnp.arange(EXPERTS, dtype=jnp.int32)[None, None, :], axis=1
    ).astype(f32)
    table = jnp.concatenate(
        [cosine] * 4 + [-sine, sine, -sine, sine]
        + [member, valid, column.astype(f32), jnp.zeros((ROWS, 94), f32)],
        axis=1,
    )

    packed, small = run_local(
        pack_kernel, "pack", place,
        [qkv_weight, out_weight, router_weight.T, jnp.stack([norm_one, norm_two])],
        [((256, SMALL_AT + 128), bf16), ((256, 128), bf16)],
        [],
    )
    rows_pack = jnp.concatenate([grad_low, inputs], axis=0)
    from_back, from_ahead = along_x(packed, 1), along_x(packed, -1)
    rows_pack, _, inputs_sib = stage(rows_pack, packed, swap_core(inputs))
    lines_pack = spread_first(rows_pack)
    grad_rows = jnp.stack([grad_low] + [v[:ROWS] for v in lines_pack])
    first_values = swap_core(from_back[:16, SMALL_AT:])
    back, ahead, lines_pack, grad_rows, table, _ = stage(
        from_back, from_ahead, lines_pack, grad_rows, table, first_values
    )
    own_near = jnp.concatenate([back, ahead], axis=0)
    low, high, grad_back, grad_ahead, sib_near = stage(
        along_x(back[:128], 1), along_x(ahead[128:], -1),
        along_second(grad_rows, 1), along_second(grad_rows, -1), swap_core(own_near),
    )
    own_far = jnp.concatenate([low, high], axis=0)
    fetched = [own_near, own_far, sib_near, swap_core(own_far)]
    half = (ROWS, D)
    rest = ((768, 512), bf16)
    rest_wide = ((768, D), bf16)
    query, kv, small_full = run_local(
        project_kernel, "project", place,
        [inputs, qkv_weight, small, table],
        [(half, bf16), (half, bf16), ((40, D), f32)],
        [(half, bf16), ((ROWS, 2 * D), f32), ((128, D), f32), ((768, 128), bf16), rest_wide, rest_wide],
        fetched,
    )
    attended = run_local(
        attend_kernel, "attend", place,
        [inputs, query, kv, small_full, out_weight, table],
        [(half, bf16), (half, f32), ((ROWS, EXPERTS), f32), ((WIDE, D), bf16)],
        [(half, bf16), (half, f32), rest, rest],
        fetched,
    )
    attended, grad_two, sib_lines = stage(
        attended, along_second(grad_rows, 2), spread_first(inputs_sib)
    )
    line, after, gates, sent = attended

    def visit(rows, grads):
        return run_experts(place, rows, grads, gate_weight[0], up_weight[0], down_weight[0])

    pair = jnp.concatenate([line, swap_core(line)], axis=0)
    got, pair, rows_sib = stage(spread_first(sent), pair, swap_core(grad_rows))
    rows = jnp.stack([sent] + got)
    parts = {}
    parts[0], back, ahead, grad_two_sib, rows = stage(
        visit([rows, swap_core(rows)], [grad_rows, rows_sib]),
        along_second(rows, 1), along_second(rows, -1), swap_core(grad_two), rows,
    )
    parts[1], two, back_sib, ahead_sib, grad_back_sib, grad_ahead_sib = stage(
        visit([back, ahead], [grad_back, grad_ahead]), along_second(rows, 2),
        swap_core(back), swap_core(ahead), swap_core(grad_back), swap_core(grad_ahead),
    )
    parts[3], two_sib, lines = stage(
        visit([back_sib, ahead_sib], [grad_back_sib, grad_ahead_sib]),
        swap_core(two), spread_first(pair),
    )
    normed_line, = run_local(
        norm_line_kernel, "norm_line", place,
        [inputs, inputs_sib, lines_pack[0], sib_lines[0], lines_pack[1], sib_lines[1],
         lines_pack[2], sib_lines[2], small_full], [((8 * ROWS, D), bf16)], [],
    )
    normed_line, turn_back, turn_ahead = stage(
        normed_line, swap_core(parts[3][0]), swap_core(parts[3][1])
    )
    merged_back = add(parts[1][0], turn_back).astype(bf16)
    merged_ahead = add(parts[1][1], turn_ahead).astype(bf16)
    parts[2], got_back, got_ahead, turn_own = stage(
        visit([two, two_sib], [grad_two, grad_two_sib]), along_second(merged_back, -1), along_second(merged_ahead, -3),
        swap_core(parts[0][1]),
    )
    merged = add(parts[2][0], swap_core(parts[2][1])).astype(bf16)
    saved = [parts[j][4:9] for j in range(4)]
    merged, first_rows = stage(merged, saved[0][0])
    saved[0] = [first_rows] + list(saved[0][1:])
    partial = add(parts[0][0], turn_own, got_back, got_ahead).astype(bf16)
    chunks, partial, got_two, turn_back, turn_ahead, turn_two = stage(
        run_weight_grads(saved), partial, along_second(merged, -2),
        swap_core(parts[3][2]), swap_core(parts[3][3]), swap_core(parts[2][3]),
    )
    owned = lax.psum_scatter(chunks.reshape(4 * 768, FFE), "x", scatter_dimension=0, tiled=True)
    total = add(partial, got_two).astype(bf16)
    total, turn_back, turn_ahead, turn_two = stage(total, turn_back, turn_ahead, turn_two)
    merged_back = add(parts[1][2], turn_back).astype(bf16)
    merged_ahead = add(parts[1][3], turn_ahead).astype(bf16)
    merged = add(parts[2][2], turn_two).astype(bf16)
    arrived, merged_back, merged_ahead, merged, turn_own = stage(
        [along_first(total[i], -i) for i in (1, 2, 3)], merged_back, merged_ahead, merged,
        swap_core(parts[0][3]),
    )
    back = [total[0]] + arrived
    mine_grad, other_grad, after_grad, tiny = run_local(
        attend_back_kernel, "attend_back", place,
        back + [
            grad_low, after, gates, small_full, out_weight, query, kv, table,
        ],
        [((4, ROWS, 384), bf16), ((4, ROWS, 384), bf16), (half, f32), ((40, D), f32)],
        [(half, bf16), ((ROWS, 3 * KV), f32), (half, bf16), ((ROWS, 2 * D), bf16), rest, rest],
        fetched,
    )
    mine_grad, other_grad, sib_grad, got_back, got_ahead = stage(
        mine_grad, other_grad, swap_core(other_grad),
        along_second(merged_back, -1), along_second(merged_ahead, -3),
    )
    input_grad, tiny = run_local(
        input_back_kernel, "input_back", place,
        [mine_grad, other_grad, qkv_weight, inputs, after_grad, small_full, tiny],
        [(half, f32), ((40, D), f32)],
        [(half, bf16), (half, bf16), (half, f32), rest_wide, rest_wide],
        fetched,
    )
    line_grad = [
        along_first(jnp.concatenate([mine_grad[k], sib_grad[k]], axis=0), k) for k in (1, 2, 3)
    ]
    line_grad, input_grad, tiny, owned = stage(line_grad, input_grad, tiny, owned)
    expert_sums = lax.all_gather(owned, "x", axis=0, tiled=True)
    chunk = run_local(
        attention_weights_kernel, "attention_weights", place,
        [normed_line, pair, *lines, mine_grad, sib_grad, *line_grad, tiny],
        [((256, 512), bf16)] * 4,
        [((D, 512), f32), ((128, D), f32)],
    )
    chunk, got, got_two = stage(
        chunk, [along_x(chunk[k], -k) for k in (1, 2, 3)], along_second(merged, -2)
    )
    shard = add(chunk[0], *got).astype(bf16)
    total = add(parts[0][2], turn_own, got_back, got_ahead, got_two).astype(bf16)
    shard, got, total, arrived, expert_sums = stage(
        shard, [along_second(shard, k) for k in (1, 2, 3)],
        total, [along_first(total[i], -i) for i in (1, 3)], expert_sums,
    )
    shard = add(shard, *got).astype(bf16)
    gate_total, up_total, down_total = widen(expert_sums.reshape(4, 768, FFE))
    shard, got, gate_total, up_total, down_total, arrived_two = stage(
        shard, spread_first(shard), gate_total, up_total, down_total, along_first(total[2], -2)
    )
    output = (after + add(total[0], *arrived, arrived_two)).astype(bf16).reshape(MICRO, TOK_MB, D)
    both, = run_local(
        collect_kernel, "collect", place, [shard, *got], [((256, SMALL_AT + 128), bf16)], []
    )
    qkv_grad, out_grad, router_grad, gain_one, gain_two = run_local(
        finish_kernel, "finish", place, [both, swap_core(both)],
        [
            ((256, 2 * D), f32), ((256, D), f32), ((256, EXPERTS), f32),
            ((1, 256), f32), ((1, 256), f32),
        ],
        [],
    )

    return (
        output,
        input_grad.reshape(MICRO, TOK_MB, D),
        gain_one.reshape(256),
        qkv_grad,
        out_grad,
        gain_two.reshape(256),
        router_grad,
        gate_total[None],
        up_total[None],
        down_total[None],
    )


def solution(mesh):
    grid = Mesh(mesh.devices.reshape(4, 4, 4, 2), ("x", "y", "z", "core"))
    every = ("x", "y", "z", "core")
    plane = ("y", "z", "core")
    return jax.shard_map(
        per_device,
        mesh=grid,
        in_specs=(
            P(None, every, None),
            P(None, every),
            P(None, every),
            P(None, every, None),
            P("x"),
            P("x", None),
            P("x", None),
            P("x"),
            P("x", None),
            P(plane, None, None),
            P(plane, None, None),
            P(plane, None, None),
            P(None, every, None),
        ),
        out_specs=(
            P(None, every, None),
            P(None, every, None),
            P("x"),
            P("x", None),
            P("x", None),
            P("x"),
            P("x", None),
            P(plane, None, None),
            P(plane, None, None),
            P(plane, None, None),
        ),
        check_vma=False,
    )
```

```python
import functools

import jax
import jax.numpy as jnp
from jax import lax
from jax.experimental import pallas as pl
from jax.experimental.pallas import tpu as pltpu
from jax.sharding import Mesh
from jax.sharding import PartitionSpec as P

D = 1024
QUERY_HEADS = 16
KEY_VALUE_HEADS = 8
HEAD_SIZE = 64
FFE = 512
TOPK = 8
MICRO = 2
TOK_MB = 64
EXPERTS = 32
CAP = 24
ROWS = MICRO * TOK_MB
SLOTS = MICRO * CAP
EXTRA = 16
WIDE = ROWS + EXTRA
KV = KEY_VALUE_HEADS * HEAD_SIZE
SMALL_AT = D + D // 2
SHORT = pl.CostEstimate(flops=1_000_000, bytes_accessed=100_000, transcendentals=0)

epsilon = 1e-06
highest = lax.Precision.HIGHEST
f32 = jnp.float32
bf16 = jnp.bfloat16


def plane_pairs(first, second, swap):
    pairs = []
    for y in range(4):
        for z in range(4):
            for c in range(2):
                dy, dz = (first, second) if c == 0 else (second, first)
                target = (((y + dy) % 4) * 4 + (z + dz) % 4) * 2 + (c ^ swap)
                pairs.append(((y * 4 + z) * 2 + c, target))
    return pairs


def along_first(v, k):
    return lax.ppermute(v, ("y", "z", "core"), plane_pairs(k % 4, 0, 0))


def along_second(v, k):
    return lax.ppermute(v, ("y", "z", "core"), plane_pairs(0, k % 4, 0))


def swap_core(v):
    return lax.ppermute(v, "core", [(0, 1), (1, 0)])


def along_x(v, k):
    return lax.ppermute(v, "x", [(i, (i + k) % 4) for i in range(4)])


def stage(*values):
    return lax.optimization_barrier(values)


def spread_first(v):
    return [along_first(v, k) for k in (1, 2, 3)]


def add(first, *others):
    total = first.astype(f32)
    for v in others:
        total = total + v.astype(f32)
    return total


def nt(a, b):
    return lax.dot_general(a, b, (((1,), (1,)), ((), ())), preferred_element_type=f32)


def tn(a, b):
    return lax.dot_general(a, b, (((0,), (0,)), ((), ())), preferred_element_type=f32)


def nn(a, b):
    return jnp.dot(a, b, preferred_element_type=f32)


BLOCKS = 8
PACKED = BLOCKS * SLOTS


def expert_kernel(n_rows, n_grads, place_ref, *refs):
    row_refs, refs = refs[:n_rows], refs[n_rows:]
    grad_refs, refs = refs[:n_grads], refs[n_grads:]
    gate_ref, up_ref, down_ref = refs[:3]
    back_refs, out_refs, save_refs = refs[3:5], refs[5:7], refs[7:12]
    (row_buf, grad_buf, back_buf, out_buf, x_buf, c_buf, r_buf, s_buf, h_buf, g_buf, u_buf,
     mix_buf, pick_buf, dot_buf, gate_buf, up_buf, down_buf,
     row_sem, grad_sem, back_sem, out_sem, save_sem, weight_sem) = refs[12:]

    def pieces(sources, buf, sem):
        copies = []
        for ref in sources:
            for b in range(ref.shape[0]):
                at = len(copies)
                copies.append(pltpu.make_async_copy(ref.at[b], buf.at[at], sem.at[at]))
        return copies

    row_loads = pieces(row_refs, row_buf, row_sem)
    grad_loads = pieces(grad_refs, grad_buf, grad_sem)
    weight_loads = [
        pltpu.make_async_copy(ref, buf, weight_sem.at[i])
        for i, (ref, buf) in enumerate(
            zip((gate_ref, up_ref, down_ref), (gate_buf, up_buf, down_buf))
        )
    ]
    for one, two in zip(row_loads, grad_loads):
        one.start()
        two.start()
    for copy in weight_loads:
        copy.start()

    expert = place_ref[0]
    row_at = expert % 4
    lane_at = pl.multiple_of((expert // 4) * 128, 128)
    upper = (
        lax.broadcasted_iota(jnp.int32, (ROWS, ROWS), 0)
        < lax.broadcasted_iota(jnp.int32, (ROWS, ROWS), 1)
    ).astype(bf16)
    extra_row = lax.broadcasted_iota(jnp.int32, (EXTRA, 128), 0)
    slot_row = lax.broadcasted_iota(jnp.int32, (SLOTS, ROWS), 0).astype(f32)

    @pl.loop(0, BLOCKS)
    def _(b):
        pltpu.make_async_copy(row_refs[0].at[0], row_buf.at[b], row_sem.at[b]).wait()
        pltpu.make_async_copy(grad_refs[0].at[0], grad_buf.at[b], grad_sem.at[b]).wait()
        info = row_buf[b, ROWS:WIDE, pl.ds(lane_at, 128)].astype(f32)
        high = jnp.sum(jnp.where(extra_row == row_at, info, 0.0), axis=0, keepdims=True)
        low = jnp.sum(jnp.where(extra_row == row_at + 4, info, 0.0), axis=0, keepdims=True)
        chosen = high > 0.0
        flags = jnp.broadcast_to(chosen.astype(f32), (16, ROWS)).astype(bf16)
        rank = nn(flags, upper)[0:1]
        pick = jnp.where((slot_row == rank) & chosen, 1.0, 0.0)
        weight = jnp.sum(pick * (high + low), axis=1, keepdims=True)
        low_pick = pick.astype(bf16)
        pick_buf[b] = low_pick
        span = pl.ds(pl.multiple_of(b * SLOTS, SLOTS), SLOTS)
        mix_buf[span, :] = jnp.broadcast_to(weight, (SLOTS, 128))
        x_buf[span, :] = nn(low_pick, row_buf[b, 0:ROWS, :]).astype(bf16)
        c_buf[span, :] = nn(low_pick, grad_buf[b]).astype(bf16)

    saves = [
        pltpu.make_async_copy(buf, ref, save_sem.at[i])
        for i, (buf, ref) in enumerate(zip((x_buf, s_buf, h_buf, g_buf, u_buf), save_refs))
    ]
    saves[0].start()
    mixing = mix_buf[:, 0:1]
    grads = c_buf[...].astype(f32)
    s_buf[...] = (mixing * grads).astype(bf16)
    saves[1].start()
    for copy in weight_loads:
        copy.wait()
    gate_pre = nn(x_buf[...], gate_buf[...])
    up_pre = nn(x_buf[...], up_buf[...])
    sigma = 1.0 / (1.0 + jnp.exp(-gate_pre))
    swish = gate_pre * sigma
    h_buf[...] = (swish * up_pre).astype(bf16)
    saves[2].start()
    hidden_grad = nt(s_buf[...], down_buf[...])
    slope = sigma * (1.0 + gate_pre * (1.0 - sigma))
    g_buf[...] = (hidden_grad * up_pre * slope).astype(bf16)
    u_buf[...] = (hidden_grad * swish).astype(bf16)
    saves[3].start()
    saves[4].start()
    r_buf[...] = (nt(g_buf[...], gate_buf[...]) + nt(u_buf[...], up_buf[...])).astype(bf16)
    produced = nn(h_buf[...], down_buf[...]).astype(bf16).astype(f32)
    gate_grad = jnp.sum(produced * c_buf[...].astype(f32), axis=1, keepdims=True)
    dot_buf[...] = jnp.broadcast_to(gate_grad, (PACKED, 128))
    c_buf[...] = (mixing * produced).astype(bf16)

    @pl.loop(0, BLOCKS)
    def _(b):
        low_pick = pick_buf[b]
        span = pl.ds(pl.multiple_of(b * SLOTS, SLOTS), SLOTS)
        back_buf[b, 0:ROWS, :] = tn(low_pick, r_buf[span, :]).astype(bf16)
        out_buf[b] = tn(low_pick, c_buf[span, :]).astype(bf16)
        back_buf[b, ROWS:WIDE, :] = jnp.zeros((EXTRA, D), bf16)
        dots = jnp.sum(low_pick.astype(f32) * dot_buf[span, :], axis=0, keepdims=True)
        high = dots.astype(bf16).astype(f32)
        info = jnp.where(extra_row == row_at, high, 0.0)
        info = info + jnp.where(extra_row == row_at + 4, dots - high, 0.0)
        back_buf[b, ROWS:WIDE, pl.ds(lane_at, 128)] = info.astype(bf16)
        for side in range(2):
            @pl.when(b // 4 == side)
            def _():
                at = b - 4 * side
                pltpu.make_async_copy(back_buf.at[b], back_refs[side].at[at], back_sem.at[b]).start()
                pltpu.make_async_copy(out_buf.at[b], out_refs[side].at[at], out_sem.at[b]).start()

    for b in range(BLOCKS):
        side, at = b // 4, b % 4
        pltpu.make_async_copy(back_buf.at[b], back_refs[side].at[at], back_sem.at[b]).wait()
        pltpu.make_async_copy(out_buf.at[b], out_refs[side].at[at], out_sem.at[b]).wait()
    for copy in saves:
        copy.wait()


def run_experts(place, rows, grads, gate, up, down):
    any_space = pl.BlockSpec(memory_space=pl.ANY)
    wide = jax.ShapeDtypeStruct((4, WIDE, D), bf16)
    flat = jax.ShapeDtypeStruct((4, ROWS, D), bf16)
    full = jax.ShapeDtypeStruct((PACKED, D), bf16)
    half = jax.ShapeDtypeStruct((PACKED, FFE), bf16)
    return pl.pallas_call(
        functools.partial(expert_kernel, len(rows), len(grads)),
        in_specs=[pl.BlockSpec(memory_space=pltpu.SMEM)]
        + [any_space] * (len(rows) + len(grads) + 3),
        out_specs=[any_space] * 9,
        out_shape=[wide, wide, flat, flat, full, full, half, half, half],
        scratch_shapes=[
            pltpu.VMEM((BLOCKS, WIDE, D), bf16),
            pltpu.VMEM((BLOCKS, ROWS, D), bf16),
            pltpu.VMEM((BLOCKS, WIDE, D), bf16),
            pltpu.VMEM((BLOCKS, ROWS, D), bf16),
            pltpu.VMEM((PACKED, D), bf16),
            pltpu.VMEM((PACKED, D), bf16),
            pltpu.VMEM((PACKED, D), bf16),
            pltpu.VMEM((PACKED, D), bf16),
            pltpu.VMEM((PACKED, FFE), bf16),
            pltpu.VMEM((PACKED, FFE), bf16),
            pltpu.VMEM((PACKED, FFE), bf16),
            pltpu.VMEM((PACKED, 128), f32),
            pltpu.VMEM((BLOCKS, SLOTS, ROWS), bf16),
            pltpu.VMEM((PACKED, 128), f32),
            pltpu.VMEM((D, FFE), bf16),
            pltpu.VMEM((D, FFE), bf16),
            pltpu.VMEM((FFE, D), bf16),
            pltpu.SemaphoreType.DMA((BLOCKS,)),
            pltpu.SemaphoreType.DMA((BLOCKS,)),
            pltpu.SemaphoreType.DMA((BLOCKS,)),
            pltpu.SemaphoreType.DMA((BLOCKS,)),
            pltpu.SemaphoreType.DMA((5,)),
            pltpu.SemaphoreType.DMA((3,)),
        ],
        compiler_params=pltpu.CompilerParams(vmem_limit_bytes=56 * 1024 * 1024),
        cost_estimate=SHORT,
        name="experts",
    )(place, *rows, *grads, gate, up, down)


def weight_grad_kernel(*refs):
    xs, ss, hs, gs, us = (refs[4 * i:4 * i + 4] for i in range(5))
    out_ref = refs[20]
    x_buf, s_buf, h_buf, g_buf, u_buf, out_buf, in_sem, out_sem = refs[21:]
    loads = []
    for j in range(4):
        for i, (sources, buf) in enumerate(
            zip((xs, gs, us, hs, ss), (x_buf, g_buf, u_buf, h_buf, s_buf))
        ):
            loads.append(pltpu.make_async_copy(sources[j], buf.at[j], in_sem.at[j, i]))
    for copy in loads:
        copy.start()
    for copy in loads:
        copy.wait()

    @pl.loop(0, 4)
    def _(k):
        wide_at = pl.multiple_of(k * 256, 256)
        thin_at = pl.multiple_of(k * 128, 128)
        rows = x_buf[:, :, pl.ds(wide_at, 256)].reshape(4 * PACKED, 256)
        thin = h_buf[:, :, pl.ds(thin_at, 128)].reshape(4 * PACKED, 128)
        out_buf[k, 0:256, :] = tn(rows, g_buf[...].reshape(4 * PACKED, FFE)).astype(bf16)
        out_buf[k, 256:512, :] = tn(rows, u_buf[...].reshape(4 * PACKED, FFE)).astype(bf16)
        down = tn(thin, s_buf[...].reshape(4 * PACKED, D)).astype(bf16)
        out_buf[k, 512:640, :] = down[:, 0:FFE]
        out_buf[k, 640:768, :] = down[:, FFE:D]
        pltpu.make_async_copy(out_buf.at[k], out_ref.at[k], out_sem.at[k]).start()

    for k in range(4):
        pltpu.make_async_copy(out_buf.at[k], out_ref.at[k], out_sem.at[k]).wait()


def run_weight_grads(saved):
    operands = [part[i] for i in range(5) for part in saved]
    any_space = pl.BlockSpec(memory_space=pl.ANY)
    return pl.pallas_call(
        weight_grad_kernel,
        in_specs=[any_space] * 20,
        out_specs=any_space,
        out_shape=jax.ShapeDtypeStruct((4, 768, FFE), bf16),
        scratch_shapes=[
            pltpu.VMEM((4, PACKED, D), bf16),
            pltpu.VMEM((4, PACKED, D), bf16),
            pltpu.VMEM((4, PACKED, FFE), bf16),
            pltpu.VMEM((4, PACKED, FFE), bf16),
            pltpu.VMEM((4, PACKED, FFE), bf16),
            pltpu.VMEM((4, 768, FFE), bf16),
            pltpu.SemaphoreType.DMA((4, 5)),
            pltpu.SemaphoreType.DMA((4,)),
        ],
        compiler_params=pltpu.CompilerParams(vmem_limit_bytes=56 * 1024 * 1024),
        cost_estimate=SHORT,
        name="expert_weight_grads",
    )(*operands)


def blocks_behind(x_at, n):
    return [pl.multiple_of(((x_at + 4 - k) % 4) * n, n) for k in range(4)]


def swapped_halves(v):
    lane = lax.broadcasted_iota(jnp.int32, v.shape, 1)
    return jnp.where(lane % HEAD_SIZE < HEAD_SIZE // 2, pltpu.roll(v, 96, 1), pltpu.roll(v, 32, 1))


def pack_kernel(place_ref, qkv_ref, out_ref, router_ref, gains_ref, packed_ref, small_ref):
    core = place_ref[4]
    packed_ref[:, 0:D] = qkv_ref[:, pl.ds(pl.multiple_of(core * D, D), D)]
    packed_ref[:, D:SMALL_AT] = out_ref[:, pl.ds(pl.multiple_of(core * 512, 512), 512)]
    rows = [router_ref[...].astype(f32), gains_ref[...].astype(f32), jnp.zeros((94, 256), f32)]
    small = jnp.concatenate(rows, axis=0).T.astype(bf16)
    packed_ref[:, SMALL_AT:SMALL_AT + 128] = small
    small_ref[...] = small


def rest_copies(near_ref, far_ref, buf, sem, at, lane, width):
    columns = slice(lane, lane + width)
    return [
        pltpu.make_async_copy(near_ref.at[0:256, columns], buf.at[0:256], sem.at[at]),
        pltpu.make_async_copy(far_ref.at[:, columns], buf.at[256:512], sem.at[at + 1]),
        pltpu.make_async_copy(near_ref.at[256:512, columns], buf.at[512:768], sem.at[at + 2]),
    ]


def project_kernel(
    place_ref, x_ref, mine_ref, tiny_ref, table_ref, near_ref, far_ref, sib_near_ref, sib_far_ref,
    q_ref, kv_ref, small_ref,
    norm_buf, all_buf, tiny_buf, small_buf, own_buf, sib_buf, sem,
):
    x_at, core = place_ref[1], place_ref[4]
    lanes = blocks_behind(x_at, 256)
    small_loads = rest_copies(near_ref, far_ref, small_buf, sem, 0, SMALL_AT, 128)
    own_loads = rest_copies(near_ref, far_ref, own_buf, sem, 3, 0, D)
    sib_loads = rest_copies(sib_near_ref, sib_far_ref, sib_buf, sem, 6, 0, D)
    for copy in small_loads + own_loads + sib_loads:
        copy.start()
    for copy in small_loads:
        copy.wait()
    for k in range(4):
        piece = tiny_ref[...] if k == 0 else small_buf[(k - 1) * 256:k * 256, :]
        tiny_buf[:, pl.ds(lanes[k], 256)] = piece.astype(f32).T
    small_ref[...] = tiny_buf[0:40, :]
    x = x_ref[...].astype(f32)
    inverse = lax.rsqrt(jnp.mean(x * x, axis=1, keepdims=True) + epsilon)
    norm_buf[...] = (x * inverse * tiny_buf[32:33, :]).astype(bf16)
    rows = [norm_buf[:, pl.ds(at, 256)] for at in lanes]
    own_at = pl.multiple_of(core * D, D)
    sib_at = pl.multiple_of((1 - core) * D, D)
    for at, rest, loads in ((own_at, own_buf, own_loads), (sib_at, sib_buf, sib_loads)):
        total = nn(rows[0], mine_ref[:, pl.ds(at, D)])
        for copy in loads:
            copy.wait()
        for k in (1, 2, 3):
            total = total + nn(rows[k], rest[(k - 1) * 256:k * 256, :])
        all_buf[:, pl.ds(at, D)] = total
    cosine, sine = table_ref[:, 0:128], table_ref[:, 128:256]
    for c in range(12):
        v = all_buf[:, c * 128:(c + 1) * 128]
        turned = (v * cosine + swapped_halves(v) * sine).astype(bf16)
        if c < 8:
            q_ref[:, c * 128:(c + 1) * 128] = turned
        else:
            kv_ref[:, (c - 8) * 128:(c - 7) * 128] = turned
    kv_ref[:, KV:2 * KV] = all_buf[:, D + KV:D + 2 * KV].astype(bf16)


def head_scores(q_ref, kv_ref, allowed, h):
    chunk = q_ref[:, h * 128:(h + 1) * 128]
    query = jnp.concatenate([chunk[:, 0:64], chunk[:, 64:128]], axis=0)
    key = kv_ref[:, h * 64:(h + 1) * 64]
    value = kv_ref[:, KV + h * 64:KV + (h + 1) * 64]
    scores = jnp.where(allowed, nt(query, key) * HEAD_SIZE ** (-0.5), -1e30)
    expo = jnp.exp(scores - jnp.max(scores, axis=1, keepdims=True))
    probs = expo / jnp.sum(expo, axis=1, keepdims=True)
    return query, key, value, probs


def allowed_pairs(table_ref):
    shape = (2 * ROWS, ROWS)
    column = table_ref[:, 289:290]
    row = table_ref[:, 256:384].T[33:34]
    q = lax.broadcasted_iota(jnp.int32, shape, 0) % ROWS
    p = lax.broadcasted_iota(jnp.int32, shape, 1)
    return (jnp.concatenate([column, column], axis=0) == row) & (p <= q)


def attend_kernel(
    place_ref, x_ref, q_ref, kv_ref, small_ref, mine_ref, table_ref,
    near_ref, far_ref, sib_near_ref, sib_far_ref,
    line_ref, after_ref, gates_ref, sent_ref,
    low_buf, out_buf, own_buf, sib_buf, sem,
):
    x_at, core = place_ref[1], place_ref[4]
    loads = rest_copies(near_ref, far_ref, own_buf, sem, 0, D, 512)
    loads += rest_copies(sib_near_ref, sib_far_ref, sib_buf, sem, 3, D, 512)
    for copy in loads:
        copy.start()
    allowed = allowed_pairs(table_ref)
    for h in range(KEY_VALUE_HEADS):
        _, _, value, probs = head_scores(q_ref, kv_ref, allowed, h)
        got = nn(probs.astype(bf16), value)
        low_buf[:, h * 128:(h + 1) * 128] = jnp.concatenate(
            [got[0:ROWS], got[ROWS:2 * ROWS]], axis=1
        ).astype(bf16)
    rows = [low_buf[:, pl.ds(at, 256)] for at in blocks_behind(x_at, 256)]
    for k in range(4):
        line_ref[:, k * 256:(k + 1) * 256] = rows[k]
    own_at = pl.multiple_of(core * 512, 512)
    sib_at = pl.multiple_of((1 - core) * 512, 512)
    for copy in loads:
        copy.wait()
    for at, rest in ((own_at, own_buf), (sib_at, sib_buf)):
        total = nn(rows[0], mine_ref[:, pl.ds(at, 512)])
        for k in (1, 2, 3):
            total = total + nn(rows[k], rest[(k - 1) * 256:k * 256, :])
        out_buf[:, pl.ds(at, 512)] = total
    valid = table_ref[:, 288:289]
    after = x_ref[...].astype(f32) + valid * out_buf[...]
    after_ref[...] = after
    inverse = lax.rsqrt(jnp.mean(after * after, axis=1, keepdims=True) + epsilon)
    second = after * inverse * small_ref[33:34, :]
    logits = lax.dot_general(
        second, small_ref[0:32, :], (((1,), (1,)), ((), ())),
        precision=highest, preferred_element_type=f32,
    )
    member = table_ref[:, 256:288] > 0.0
    masked = jnp.where(member, logits, -3e38)
    gates = jnp.where(member, jnp.exp(masked - jnp.max(masked, axis=1, keepdims=True)), 0.0)
    gates = gates / jnp.sum(gates, axis=1, keepdims=True)
    gates_ref[...] = gates
    mixing = jnp.concatenate([gates * valid, jnp.zeros((ROWS, 96), f32)], axis=1).T
    high = mixing[0:32].astype(bf16).astype(f32)
    low = mixing[0:32] - high
    info = [
        jnp.concatenate([high[4 * q:4 * q + 4], low[4 * q:4 * q + 4], jnp.zeros((8, 128), f32)], axis=0)
        for q in range(8)
    ]
    sent_ref[0:ROWS, :] = second.astype(bf16)
    sent_ref[ROWS:WIDE, :] = jnp.concatenate(info, axis=1).astype(bf16)


def norm_backward(grad, values, gain):
    inverse = lax.rsqrt(jnp.mean(values * values, axis=1, keepdims=True) + epsilon)
    scaled = grad * gain
    gain_grad = jnp.sum(grad * values * inverse, axis=0, keepdims=True)
    dot = jnp.mean(scaled * values, axis=1, keepdims=True)
    return inverse * (scaled - values * (inverse * inverse * dot)), gain_grad


def attend_back_kernel(
    place_ref, b0, b1, b2, b3, cot_ref, after_ref, gates_ref, small_ref,
    mine_ref, q_ref, kv_ref, table_ref, near_ref, far_ref, sib_near_ref, sib_far_ref,
    mine_out, other_out, after_grad_ref, tiny_ref,
    low_buf, sum_buf, grad_buf, all_buf, own_buf, sib_buf, sem,
):
    x_at, first_at, second_at, core = (place_ref[i] for i in (1, 2, 3, 4))
    loads = rest_copies(near_ref, far_ref, own_buf, sem, 0, D, 512)
    loads += rest_copies(sib_near_ref, sib_far_ref, sib_buf, sem, 3, D, 512)
    for copy in loads:
        copy.start()
    back = b0[...].astype(f32) + b1[...].astype(f32) + b2[...].astype(f32) + b3[...].astype(f32)
    extra = back[ROWS:WIDE]
    dots = extra[0:4] + extra[4:8]
    dots = jnp.concatenate([dots[:, q * 128:(q + 1) * 128] for q in range(8)], axis=0)
    dots = jnp.concatenate([dots, jnp.zeros((96, ROWS), f32)], axis=0).T[:, 0:32]
    valid, gates = table_ref[:, 288:289], gates_ref[...]
    gate_grad = dots * valid
    logit_grad = gates * (gate_grad - jnp.sum(gates * gate_grad, axis=1, keepdims=True))
    after = after_ref[...]
    gain = small_ref[33:34, :]
    inverse = lax.rsqrt(jnp.mean(after * after, axis=1, keepdims=True) + epsilon)
    second = after * inverse * gain
    wide_grad = jnp.concatenate([logit_grad, jnp.zeros((ROWS, 96), f32)], axis=1)
    tiny_ref[0:32, :] = jnp.dot(
        wide_grad.T, second, precision=highest, preferred_element_type=f32
    )[0:32]
    second_grad = back[0:ROWS] + jnp.dot(
        logit_grad, small_ref[0:32, :], precision=highest, preferred_element_type=f32
    )
    norm_grad, gain_grad = norm_backward(second_grad, after, gain)
    tiny_ref[32:40, :] = jnp.concatenate(
        [jnp.zeros((1, D), f32), gain_grad, jnp.zeros((6, D), f32)], axis=0
    )
    after_grad = cot_ref[...].astype(f32) + norm_grad
    after_grad_ref[...] = after_grad
    low_buf[...] = (valid * after_grad).astype(bf16)
    own_at = pl.multiple_of(core * 512, 512)
    sib_at = pl.multiple_of((1 - core) * 512, 512)
    own = low_buf[:, pl.ds(own_at, 512)]
    other = low_buf[:, pl.ds(sib_at, 512)]
    for copy in loads:
        copy.wait()
    lanes = blocks_behind(x_at, 256)
    for k in range(4):
        if k == 0:
            got = nt(own, mine_ref[:, pl.ds(own_at, 512)]) + nt(other, mine_ref[:, pl.ds(sib_at, 512)])
        else:
            span = slice((k - 1) * 256, k * 256)
            got = nt(own, own_buf[span, :]) + nt(other, sib_buf[span, :])
        grad_buf[:, pl.ds(lanes[k], 256)] = got.astype(bf16)
    allowed = allowed_pairs(table_ref)
    cosine, sine = table_ref[:, 0:128], table_ref[:, 128:256]
    scale = HEAD_SIZE ** (-0.5)
    for h in range(KEY_VALUE_HEADS):
        query, key, value, probs = head_scores(q_ref, kv_ref, allowed, h)
        chunk = grad_buf[:, h * 128:(h + 1) * 128]
        grad = jnp.concatenate([chunk[:, 0:64], chunk[:, 64:128]], axis=0)
        prob_grad = nt(grad, value)
        score_grad = (
            probs * (prob_grad - jnp.sum(probs * prob_grad, axis=1, keepdims=True))
        ).astype(bf16)
        value_grad = tn(probs.astype(bf16), grad)
        query_grad = nn(score_grad, key) * scale
        key_grad = tn(score_grad, query) * scale
        sum_buf[:, h * 128:(h + 1) * 128] = jnp.concatenate(
            [query_grad[0:ROWS], query_grad[ROWS:2 * ROWS]], axis=1
        )
        sum_buf[:, D + h * 64:D + (h + 1) * 64] = key_grad
        all_buf[:, D + KV + h * 64:D + KV + (h + 1) * 64] = value_grad.astype(bf16)
    for c in range(12):
        v = sum_buf[:, c * 128:(c + 1) * 128]
        all_buf[:, c * 128:(c + 1) * 128] = (v * cosine - swapped_halves(v) * sine).astype(bf16)
    for f in range(4):
        at = (first_at + f) % 4
        mine_out[f, :, 0:256] = all_buf[:, pl.ds(pl.multiple_of(core * D + at * 256, 256), 256)]
        mine_out[f, :, 256:384] = low_buf[:, pl.ds(pl.multiple_of(core * 512 + at * 128, 128), 128)]
        at = (second_at + f) % 4
        other_out[f, :, 0:256] = all_buf[:, pl.ds(pl.multiple_of((1 - core) * D + at * 256, 256), 256)]
        other_out[f, :, 256:384] = low_buf[
            :, pl.ds(pl.multiple_of((1 - core) * 512 + at * 128, 128), 128)
        ]


def input_back_kernel(
    place_ref, mine_grad, other_grad, mine_ref, x_ref, after_grad_ref, small_ref, tiny_in,
    near_ref, far_ref, sib_near_ref, sib_far_ref,
    input_grad_ref, tiny_ref,
    own_buf, other_buf, grad_buf, own_rest, sib_rest, sem,
):
    x_at, first_at, second_at, core = (place_ref[i] for i in (1, 2, 3, 4))
    loads = rest_copies(near_ref, far_ref, own_rest, sem, 0, 0, D)
    loads += rest_copies(sib_near_ref, sib_far_ref, sib_rest, sem, 3, 0, D)
    for copy in loads:
        copy.start()
    for f in range(4):
        at = pl.multiple_of(((first_at + f) % 4) * 256, 256)
        own_buf[:, pl.ds(at, 256)] = mine_grad[f, :, 0:256]
        at = pl.multiple_of(((second_at + f) % 4) * 256, 256)
        other_buf[:, pl.ds(at, 256)] = other_grad[f, :, 0:256]
    own, other = own_buf[...], other_buf[...]
    own_at = pl.multiple_of(core * D, D)
    sib_at = pl.multiple_of((1 - core) * D, D)
    lanes = blocks_behind(x_at, 256)
    for copy in loads:
        copy.wait()
    for k in range(4):
        if k == 0:
            got = nt(own, mine_ref[:, pl.ds(own_at, D)]) + nt(other, mine_ref[:, pl.ds(sib_at, D)])
        else:
            span = slice((k - 1) * 256, k * 256)
            got = nt(own, own_rest[span, :]) + nt(other, sib_rest[span, :])
        grad_buf[:, pl.ds(lanes[k], 256)] = got
    norm_grad, gain_grad = norm_backward(
        grad_buf[...], x_ref[...].astype(f32), small_ref[32:33, :]
    )
    input_grad_ref[...] = after_grad_ref[...] + norm_grad
    tiny_ref[0:32, :] = tiny_in[0:32, :]
    tiny_ref[32:40, :] = jnp.concatenate([gain_grad, tiny_in[33:40, :]], axis=0)


def norm_line_kernel(place_ref, r0, r1, r2, r3, r4, r5, r6, r7, small_ref, out_ref):
    gain = small_ref[32:33, :]
    lanes = blocks_behind(place_ref[1], 256)
    for i, ref in enumerate((r0, r1, r2, r3, r4, r5, r6, r7)):
        x = ref[ref.shape[0] - ROWS:, :].astype(f32)
        inverse = lax.rsqrt(jnp.mean(x * x, axis=1, keepdims=True) + epsilon)
        out_ref[i * ROWS:(i + 1) * ROWS, :] = (x * inverse * gain).astype(bf16)
    pieces = [out_ref[:, pl.ds(lane, 256)] for lane in lanes]
    for k in range(4):
        out_ref[:, k * 256:(k + 1) * 256] = pieces[k]


def attention_weights_kernel(
    place_ref, n_ref, a0, a1, a2, a3, g0, g1, g2, g3, g4, tiny_ref,
    o0, o1, o2, o3,
    sum_buf, tiny_buf,
):
    x_at = place_ref[1]
    grads = [jnp.concatenate([g0[0], g1[0]], axis=0), g2[...], g3[...], g4[...]]
    out_sum = in_sum = None
    at = 0
    for ref, grad in zip((a0, a1, a2, a3), grads):
        one = tn(ref[...], grad[:, 256:384])
        two = tn(n_ref[at:at + ref.shape[0], :], grad[:, 0:256])
        out_sum = one if out_sum is None else out_sum + one
        in_sum = two if in_sum is None else in_sum + two
        at += ref.shape[0]
    sum_buf[:, 0:256] = in_sum
    sum_buf[:, 256:384] = out_sum
    tiny_buf[0:40, :] = tiny_ref[...]
    tiny_buf[40:128, :] = jnp.zeros((88, D), f32)
    for k, lane in enumerate(blocks_behind(x_at, 256)):
        sum_buf[k * 256:(k + 1) * 256, 384:512] = tiny_buf[:, pl.ds(lane, 256)].T
    for k, out in enumerate((o0, o1, o2, o3)):
        out[...] = sum_buf[k * 256:(k + 1) * 256, :].astype(bf16)


def collect_kernel(place_ref, p0, p1, p2, p3, out_ref):
    tiny = None
    for ref, wide, thin in zip(
        (p0, p1, p2, p3), blocks_behind(place_ref[2], 256), blocks_behind(place_ref[2], 128)
    ):
        out_ref[:, pl.ds(wide, 256)] = ref[:, 0:256]
        out_ref[:, pl.ds(pl.multiple_of(D + thin, 128), 128)] = ref[:, 256:384]
        one = ref[:, 384:512].astype(f32)
        tiny = one if tiny is None else tiny + one
    out_ref[:, SMALL_AT:SMALL_AT + 128] = tiny.astype(bf16)


def finish_kernel(place_ref, own_ref, other_ref, qkv_ref, out_ref, router_ref, one_ref, two_ref):
    core = place_ref[4]
    for ref, side in ((own_ref, core), (other_ref, 1 - core)):
        qkv_ref[:, pl.ds(pl.multiple_of(side * D, D), D)] = ref[:, 0:D].astype(f32)
        out_ref[:, pl.ds(pl.multiple_of(side * 512, 512), 512)] = ref[:, D:SMALL_AT].astype(f32)
    tiny = own_ref[:, SMALL_AT:SMALL_AT + 128].astype(f32)
    tiny = tiny + other_ref[:, SMALL_AT:SMALL_AT + 128].astype(f32)
    turned = tiny.T
    router_ref[...] = turned[0:EXPERTS]
    one_ref[...] = turned[32:33]
    two_ref[...] = turned[33:34]


def widen_kernel(sum_ref, gate_ref, up_ref, down_ref):
    gate_ref[...] = sum_ref[0, 0:256, :].astype(f32)
    up_ref[...] = sum_ref[0, 256:512, :].astype(f32)
    down_ref[:, 0:FFE] = sum_ref[0, 512:640, :].astype(f32)
    down_ref[:, FFE:D] = sum_ref[0, 640:768, :].astype(f32)


def widen(sums):
    return pl.pallas_call(
        widen_kernel,
        grid=(4,),
        in_specs=[pl.BlockSpec((1, 768, FFE), lambda k: (k, 0, 0))],
        out_specs=[
            pl.BlockSpec((256, FFE), lambda k: (k, 0)),
            pl.BlockSpec((256, FFE), lambda k: (k, 0)),
            pl.BlockSpec((128, D), lambda k: (k, 0)),
        ],
        out_shape=[
            jax.ShapeDtypeStruct((D, FFE), f32),
            jax.ShapeDtypeStruct((D, FFE), f32),
            jax.ShapeDtypeStruct((FFE, D), f32),
        ],
        compiler_params=pltpu.CompilerParams(vmem_limit_bytes=56 * 1024 * 1024),
        cost_estimate=SHORT,
        name="widen",
    )(sums)


def run_local(kernel, name, place, operands, outs, scratch, fetched=(), room=60):
    vmem = pl.BlockSpec(memory_space=pltpu.VMEM)
    apart = pl.BlockSpec(memory_space=pl.ANY)
    return pl.pallas_call(
        kernel,
        in_specs=[pl.BlockSpec(memory_space=pltpu.SMEM)]
        + [vmem] * len(operands)
        + [apart] * len(fetched),
        out_specs=[vmem] * len(outs),
        out_shape=[jax.ShapeDtypeStruct(shape, kind) for shape, kind in outs],
        scratch_shapes=[pltpu.VMEM(shape, kind) for shape, kind in scratch]
        + ([pltpu.SemaphoreType.DMA((9,))] if fetched else []),
        compiler_params=pltpu.CompilerParams(vmem_limit_bytes=room * 1024 * 1024),
        cost_estimate=SHORT,
        name=name,
    )(place, *operands, *fetched)


def block_at(v, index, size, axis):
    return lax.dynamic_slice_in_dim(v, index * size, size, axis)


def per_device(
    hidden_in,
    segment_ids,
    token_counts,
    expert_ids,
    norm_one,
    qkv_weight,
    out_weight,
    norm_two,
    router_weight,
    gate_weight,
    up_weight,
    down_weight,
    cotangent,
):
    x_at = lax.axis_index("x")
    y_at = lax.axis_index("y")
    z_at = lax.axis_index("z")
    core = lax.axis_index("core")
    first_at = jnp.where(core == 0, y_at, z_at)
    second_at = jnp.where(core == 0, z_at, y_at)
    place = jnp.stack([(y_at * 4 + z_at) * 2 + core, x_at, first_at, second_at, core]).astype(jnp.int32)

    grad_low = cotangent.reshape(ROWS, D)
    inputs = hidden_in.reshape(ROWS, D)
    valid = (
        (jnp.arange(TOK_MB, dtype=jnp.int32)[None, :] < token_counts).reshape(ROWS, 1).astype(f32)
    )
    segment_key = (
        segment_ids + (TOK_MB + 1) * jnp.arange(MICRO, dtype=jnp.int32)[:, None]
    ).reshape(ROWS)
    column, row = segment_key[:, None], segment_key[None, :]
    places = jnp.arange(ROWS)
    allowed = (column == row) & (places[:, None] >= places[None, :])
    position = jnp.sum(allowed.astype(f32), axis=1) - 1.0
    frequency = 10000.0 ** (-2.0 * jnp.arange(HEAD_SIZE // 2, dtype=f32) / HEAD_SIZE)
    angles = position[:, None] * frequency[None, :]
    cosine, sine = jnp.cos(angles), jnp.sin(angles)
    routes = expert_ids.reshape(ROWS, TOPK)
    member = jnp.any(
        routes[:, :, None] == jnp.arange(EXPERTS, dtype=jnp.int32)[None, None, :], axis=1
    ).astype(f32)
    table = jnp.concatenate(
        [cosine] * 4 + [-sine, sine, -sine, sine]
        + [member, valid, column.astype(f32), jnp.zeros((ROWS, 94), f32)],
        axis=1,
    )

    packed, small = run_local(
        pack_kernel, "pack", place,
        [qkv_weight, out_weight, router_weight.T, jnp.stack([norm_one, norm_two])],
        [((256, SMALL_AT + 128), bf16), ((256, 128), bf16)],
        [],
    )
    rows_pack = jnp.concatenate([grad_low, inputs], axis=0)
    from_back, from_ahead = along_x(packed, 1), along_x(packed, -1)
    rows_pack, _, inputs_sib = stage(rows_pack, packed, swap_core(inputs))
    lines_pack = spread_first(rows_pack)
    grad_rows = jnp.stack([grad_low] + [v[:ROWS] for v in lines_pack])
    first_values = swap_core(from_back[:16, SMALL_AT:])
    back, ahead, lines_pack, grad_rows, table, _ = stage(
        from_back, from_ahead, lines_pack, grad_rows, table, first_values
    )
    own_near = jnp.concatenate([back, ahead], axis=0)
    low, high, grad_back, grad_ahead, sib_near = stage(
        along_x(back[:128], 1), along_x(ahead[128:], -1),
        along_second(grad_rows, 1), along_second(grad_rows, -1), swap_core(own_near),
    )
    own_far = jnp.concatenate([low, high], axis=0)
    fetched = [own_near, own_far, sib_near, swap_core(own_far)]
    half = (ROWS, D)
    rest = ((768, 512), bf16)
    rest_wide = ((768, D), bf16)
    query, kv, small_full = run_local(
        project_kernel, "project", place,
        [inputs, qkv_weight, small, table],
        [(half, bf16), (half, bf16), ((40, D), f32)],
        [(half, bf16), ((ROWS, 2 * D), f32), ((128, D), f32), ((768, 128), bf16), rest_wide, rest_wide],
        fetched,
    )
    attended = run_local(
        attend_kernel, "attend", place,
        [inputs, query, kv, small_full, out_weight, table],
        [(half, bf16), (half, f32), ((ROWS, EXPERTS), f32), ((WIDE, D), bf16)],
        [(half, bf16), (half, f32), rest, rest],
        fetched,
    )
    attended, grad_two, sib_lines = stage(
        attended, along_second(grad_rows, 2), spread_first(inputs_sib)
    )
    line, after, gates, sent = attended

    def visit(rows, grads):
        return run_experts(place, rows, grads, gate_weight[0], up_weight[0], down_weight[0])

    pair = jnp.concatenate([line, swap_core(line)], axis=0)
    got, pair, rows_sib = stage(spread_first(sent), pair, swap_core(grad_rows))
    rows = jnp.stack([sent] + got)
    parts = {}
    parts[0], back, ahead, grad_two_sib, rows = stage(
        visit([rows, swap_core(rows)], [grad_rows, rows_sib]),
        along_second(rows, 1), along_second(rows, -1), swap_core(grad_two), rows,
    )
    parts[1], two, back_sib, ahead_sib, grad_back_sib, grad_ahead_sib = stage(
        visit([back, ahead], [grad_back, grad_ahead]), along_second(rows, 2),
        swap_core(back), swap_core(ahead), swap_core(grad_back), swap_core(grad_ahead),
    )
    parts[3], two_sib, lines = stage(
        visit([back_sib, ahead_sib], [grad_back_sib, grad_ahead_sib]),
        swap_core(two), spread_first(pair),
    )
    normed_line, = run_local(
        norm_line_kernel, "norm_line", place,
        [inputs, inputs_sib, lines_pack[0], sib_lines[0], lines_pack[1], sib_lines[1],
         lines_pack[2], sib_lines[2], small_full], [((8 * ROWS, D), bf16)], [],
    )
    normed_line, turn_back, turn_ahead = stage(
        normed_line, swap_core(parts[3][0]), swap_core(parts[3][1])
    )
    merged_back = add(parts[1][0], turn_back).astype(bf16)
    merged_ahead = add(parts[1][1], turn_ahead).astype(bf16)
    parts[2], got_back, got_ahead, turn_own = stage(
        visit([two, two_sib], [grad_two, grad_two_sib]), along_second(merged_back, -1), along_second(merged_ahead, -3),
        swap_core(parts[0][1]),
    )
    merged = add(parts[2][0], swap_core(parts[2][1])).astype(bf16)
    saved = [parts[j][4:9] for j in range(4)]
    merged, first_rows = stage(merged, saved[0][0])
    saved[0] = [first_rows] + list(saved[0][1:])
    partial = add(parts[0][0], turn_own, got_back, got_ahead).astype(bf16)
    chunks, partial, got_two, turn_back, turn_ahead, turn_two = stage(
        run_weight_grads(saved), partial, along_second(merged, -2),
        swap_core(parts[3][2]), swap_core(parts[3][3]), swap_core(parts[2][3]),
    )
    owned = lax.psum_scatter(chunks.reshape(4 * 768, FFE), "x", scatter_dimension=0, tiled=True)
    total = add(partial, got_two).astype(bf16)
    total, turn_back, turn_ahead, turn_two = stage(total, turn_back, turn_ahead, turn_two)
    merged_back = add(parts[1][2], turn_back).astype(bf16)
    merged_ahead = add(parts[1][3], turn_ahead).astype(bf16)
    merged = add(parts[2][2], turn_two).astype(bf16)
    arrived, merged_back, merged_ahead, merged, turn_own = stage(
        [along_first(total[i], -i) for i in (1, 2, 3)], merged_back, merged_ahead, merged,
        swap_core(parts[0][3]),
    )
    back = [total[0]] + arrived
    mine_grad, other_grad, after_grad, tiny = run_local(
        attend_back_kernel, "attend_back", place,
        back + [
            grad_low, after, gates, small_full, out_weight, query, kv, table,
        ],
        [((4, ROWS, 384), bf16), ((4, ROWS, 384), bf16), (half, f32), ((40, D), f32)],
        [(half, bf16), ((ROWS, 3 * KV), f32), (half, bf16), ((ROWS, 2 * D), bf16), rest, rest],
        fetched,
    )
    mine_grad, other_grad, sib_grad, got_back, got_ahead = stage(
        mine_grad, other_grad, swap_core(other_grad),
        along_second(merged_back, -1), along_second(merged_ahead, -3),
    )
    input_grad, tiny = run_local(
        input_back_kernel, "input_back", place,
        [mine_grad, other_grad, qkv_weight, inputs, after_grad, small_full, tiny],
        [(half, f32), ((40, D), f32)],
        [(half, bf16), (half, bf16), (half, f32), rest_wide, rest_wide],
        fetched,
    )
    line_grad = [
        along_first(jnp.concatenate([mine_grad[k], sib_grad[k]], axis=0), k) for k in (1, 2, 3)
    ]
    line_grad, input_grad, tiny, owned = stage(line_grad, input_grad, tiny, owned)
    expert_sums = lax.all_gather(owned, "x", axis=0, tiled=True)
    chunk = run_local(
        attention_weights_kernel, "attention_weights", place,
        [normed_line, pair, *lines, mine_grad, sib_grad, *line_grad, tiny],
        [((256, 512), bf16)] * 4,
        [((D, 512), f32), ((128, D), f32)],
    )
    chunk, got, got_two = stage(
        chunk, [along_x(chunk[k], -k) for k in (1, 2, 3)], along_second(merged, -2)
    )
    shard = add(chunk[0], *got).astype(bf16)
    total = add(parts[0][2], turn_own, got_back, got_ahead, got_two).astype(bf16)
    shard, got, total, arrived, expert_sums = stage(
        shard, [along_second(shard, k) for k in (1, 2, 3)],
        total, [along_first(total[i], -i) for i in (1, 3)], expert_sums,
    )
    shard = add(shard, *got).astype(bf16)
    gate_total, up_total, down_total = widen(expert_sums.reshape(4, 768, FFE))
    shard, got, gate_total, up_total, down_total, arrived_two = stage(
        shard, spread_first(shard), gate_total, up_total, down_total, along_first(total[2], -2)
    )
    output = (after + add(total[0], *arrived, arrived_two)).astype(bf16).reshape(MICRO, TOK_MB, D)
    both, = run_local(
        collect_kernel, "collect", place, [shard, *got], [((256, SMALL_AT + 128), bf16)], []
    )
    qkv_grad, out_grad, router_grad, gain_one, gain_two = run_local(
        finish_kernel, "finish", place, [both, swap_core(both)],
        [
            ((256, 2 * D), f32), ((256, D), f32), ((EXPERTS, 256), f32),
            ((1, 256), f32), ((1, 256), f32),
        ],
        [],
    )

    return (
        output,
        input_grad.reshape(MICRO, TOK_MB, D),
        gain_one.reshape(256),
        qkv_grad,
        out_grad,
        gain_two.reshape(256),
        router_grad.T,
        gate_total[None],
        up_total[None],
        down_total[None],
    )


def solution(mesh):
    grid = Mesh(mesh.devices.reshape(4, 4, 4, 2), ("x", "y", "z", "core"))
    every = ("x", "y", "z", "core")
    plane = ("y", "z", "core")
    return jax.shard_map(
        per_device,
        mesh=grid,
        in_specs=(
            P(None, every, None),
            P(None, every),
            P(None, every),
            P(None, every, None),
            P("x"),
            P("x", None),
            P("x", None),
            P("x"),
            P("x", None),
            P(plane, None, None),
            P(plane, None, None),
            P(plane, None, None),
            P(None, every, None),
        ),
        out_specs=(
            P(None, every, None),
            P(None, every, None),
            P("x"),
            P("x", None),
            P("x", None),
            P("x"),
            P("x", None),
            P(plane, None, None),
            P(plane, None, None),
            P(plane, None, None),
        ),
        check_vma=False,
    )
```
